32 devices in a mesh: blk: 2 (over x), dp: 4 (over z), tensor: 4 (over y, core).
Axes of the slice: x: 2, y: 2, z: 4, core: 2. Of those that a mesh axis runs over, the one named last changes fastest.
Arguments:
- stream_in: bfloat16 [8192, 767], P(('dp', 'tensor'))
- lengths: int32 [16], P('dp'), may hold values from 0 to 2048, as said below
- norm_gains: float32 [2, 768], P('blk'), may hold values from 0.5 to 1.5
- w_qkv: bfloat16 [768, 2304], P(None, 'tensor'), may hold values from -0.21875 to 0.21875
- w_attn_out: bfloat16 [768, 767], P('tensor'), may hold values from -1.25 to 1.25
- w_up: bfloat16 [768, 3072], P(None, 'tensor'), may hold values from -0.21875 to 0.21875
- w_down: bfloat16 [3072, 767], P('tensor'), may hold values from -0.109375 to 0.109375
- cotangent: bfloat16 [8192, 767], P(('dp', 'tensor')), may hold values from -6 to 6
Outputs:
- block_io: bfloat16 [2, 8192, 767], P('blk', ('dp', 'tensor'))
- gain_grads: float32 [2, 768], P('blk')
- grad_qkv: float32 [768, 2304], P(None, 'tensor')
- grad_attn_out: float32 [768, 767], P('tensor')
- grad_up: float32 [768, 3072], P(None, 'tensor')
- grad_down: float32 [3072, 767], P('tensor')
- stream_rms: float32 [], replicated
The draws below stay inside these ranges and needn't reach their ends.
Inputs may be any that keep to these rules, and one draw needn't show every extreme that they name: Each data shard's 4 entries hold its sequences' lengths, each 512 or 2048, followed by zeros, and sum to 2048; over all shards exactly half the tokens lie in sequences of 2048; how many long sequences a shard holds varies from shard to shard.
All inputs are finite; a program needn't handle non-finite values.
Results may differ from the reference program's by a relative error of at most 0.014.
Values may be sent and summed in bfloat16 or wider, within the bound.
A program may use at most 192 MiB of HBM per device.

```python
import jax
import jax.numpy as jnp
from jax import lax

D = 768
HEADS = 12
HS = 64
FF = 3072
DC = 767
SHORT = 512
LONG = 2048
TOK_DEV = 2048
TOKENS = 8192
N_DP = 4


def draw_stream_in(key, part):
    key = jax.random.fold_in(key, 5)
    positions = jnp.arange(TOKENS, dtype=jnp.float32) / (TOKENS - 1)
    base_rows = jax.random.normal(key, (TOKENS, DC), jnp.float32)
    row_scale = 1.0 + 2.0 * positions
    return (base_rows * row_scale[:, None]).astype(jnp.bfloat16)


def shard_order(shard_key):
    return jax.random.permutation(shard_key, TOK_DEV // SHORT)


def draw_lengths(key, part):
    key = jax.random.fold_in(key, 7)
    most_long = TOK_DEV // LONG
    slot_count = TOK_DEV // SHORT
    half_count = N_DP // 2
    picked = jax.random.randint(jax.random.fold_in(key, 1), (half_count,), 0, most_long + 1)
    long_counts = jax.random.permutation(jax.random.fold_in(key, 2), jnp.concatenate([picked, most_long - picked]))
    short_counts = (TOK_DEV - long_counts * LONG) // SHORT
    places = jnp.arange(slot_count, dtype=jnp.int32)
    is_used = places[None, :] < (long_counts + short_counts)[:, None]
    slot_sizes = jnp.where(places[None, :] < long_counts[:, None], LONG, SHORT)
    slot_sizes = jnp.where(is_used, slot_sizes, 0)
    shard_keys = jax.random.split(jax.random.fold_in(key, 3), N_DP)
    orders = jax.vmap(shard_order)(shard_keys)
    priority = jnp.where(is_used, orders, slot_count + places[None, :])
    arrange = jnp.argsort(priority, axis=1, stable=True)
    return jnp.take_along_axis(slot_sizes, arrange, axis=1).reshape(-1).astype(jnp.int32)


def levels(rng, dims, cuts, low, top_value):
    def one(axis_at, blocks):
        steps = jax.random.uniform(jax.random.fold_in(jax.random.fold_in(rng, 6), axis_at), (blocks,), jnp.float32, low / len(cuts), top_value / len(cuts))
        return jnp.repeat(jnp.exp(steps), dims[axis_at] // blocks).reshape((-1,) + (1,) * (len(dims) - axis_at - 1))

    factor_of = one(*cuts[0])
    for cut in cuts[1:]:
        factor_of = factor_of * one(*cut)
    return factor_of


def centred(own_key, dims, width, most, cuts=(), held_as=jnp.bfloat16):
    entries = jax.random.normal(own_key, dims, jnp.float32) * width
    if len(cuts) > 0:
        entries = levels(own_key, dims, cuts, -0.22, 0.18) * entries
    return jnp.clip(entries, min=-most, max=most).astype(held_as)


def setup_inputs(seed: int = 0) -> dict:
    seeds = jax.random.split(jax.random.key(seed), 9)
    return {
        "stream_in": draw_stream_in(jax.random.fold_in(seeds[8], 71), 0),
        "lengths": draw_lengths(jax.random.fold_in(seeds[8], 71), 0),
        "norm_gains": jnp.clip(1.0 + 0.1 * jax.random.normal(seeds[2], (2, D), jnp.float32), 0.5, 1.5),
        "w_qkv": centred(seeds[3], (D, 3 * D), D ** -0.5, 0.21875, ((1, 4),)),
        "w_attn_out": centred(seeds[4], (D, DC), (D // 32) ** -0.5, 1.25, ((0, 4),)),
        "w_up": centred(seeds[5], (D, FF), D ** -0.5, 0.21875, ((1, 4),)),
        "w_down": centred(seeds[6], (FF, DC), FF ** -0.5, 0.109375, ((0, 4),)),
        "cotangent": centred(seeds[7], (TOKENS, DC), 1.0, 6.0, ((0, 16),)),
    }


@jax.custom_vjp
def low(v):
    return lax.optimization_barrier(v.astype(jnp.bfloat16)).astype(jnp.float32)

@jax.custom_vjp
def low_back(v):
    return v

def low_keep(v):
    return (low(v), None)

def low_pass(kept, grad):
    return (grad,)

def back_keep(v):
    return (v, None)

def back_low(kept, grad):
    return (low(grad),)
low.defvjp(low_keep, low_pass)
low_back.defvjp(back_keep, back_low)
EPSILON = 1e-05
HIGHEST_PRECISION = lax.Precision.HIGHEST
MASKED = -1e+30

def crms_norm(stream, gain_row):
    row_total = lax.optimization_barrier(jnp.sum(stream, axis=-1, keepdims=True))
    full_rows = jnp.concatenate([stream, -row_total], axis=-1)
    mean_square = lax.optimization_barrier(jnp.mean(full_rows * full_rows, axis=-1, keepdims=True))
    return full_rows * lax.rsqrt(mean_square + EPSILON) * gain_row

def segment_ids(length_row):
    ends_all = jnp.cumsum(length_row).astype(jnp.int32)
    places = jnp.arange(TOK_DEV, dtype=jnp.int32)
    return lax.optimization_barrier(jnp.sum((places[:, None] >= ends_all[None, :]).astype(jnp.int32), axis=1)).astype(jnp.int32)

def attention(queries, key_all, value_all, segment):
    window_pad = LONG - SHORT
    key_padded = jnp.concatenate([jnp.zeros((window_pad, HEADS, HS), jnp.float32), key_all], axis=0)
    value_padded = jnp.concatenate([jnp.zeros((window_pad, HEADS, HS), jnp.float32), value_all], axis=0)
    segment_padded = jnp.concatenate([jnp.full((window_pad,), -1, jnp.int32), segment], axis=0)
    score_scale = HS ** (-0.5)

    def attend_block(block_index):
        row_start = (block_index * SHORT).astype(jnp.int32)
        query_rows = lax.dynamic_slice_in_dim(queries, row_start, SHORT, 0)
        key_rows = lax.dynamic_slice_in_dim(key_padded, row_start, LONG, 0)
        value_rows = lax.dynamic_slice_in_dim(value_padded, row_start, LONG, 0)
        query_seg = lax.dynamic_slice_in_dim(segment, row_start, SHORT, 0)
        key_seg = lax.dynamic_slice_in_dim(segment_padded, row_start, LONG, 0)
        causal = jnp.arange(LONG)[None, :] <= jnp.arange(SHORT)[:, None] + window_pad
        allowed = causal & (query_seg[:, None] == key_seg[None, :])
        scores = low_back(jnp.einsum('qhe,khe->hqk', query_rows, key_rows, precision=HIGHEST_PRECISION) * score_scale)
        scores = jnp.where(allowed[None], scores, MASKED)
        row_max = lax.optimization_barrier(jnp.max(scores, axis=-1, keepdims=True))
        weights = jnp.exp(scores - row_max)
        weights_low = low(weights / lax.optimization_barrier(jnp.sum(weights, axis=-1, keepdims=True)))
        return jnp.einsum('hqk,khe->qhe', weights_low, value_rows, precision=HIGHEST_PRECISION)
    blocks = lax.map(jax.checkpoint(attend_block), jnp.arange(TOK_DEV // SHORT, dtype=jnp.int32))
    return blocks.reshape(TOK_DEV, HEADS * HS)

def layer(stream, norm_gains, w_qkv, w_attn_out, w_up, w_down, segment):
    normed_one = low(crms_norm(stream, norm_gains[0]))
    mixed_qkv = low_back(low(jnp.dot(normed_one, w_qkv, precision=HIGHEST_PRECISION)))
    mixed_qkv = mixed_qkv.reshape(TOK_DEV, HEADS, 3, HS)
    attended = attention(mixed_qkv[:, :, 0], mixed_qkv[:, :, 1], mixed_qkv[:, :, 2], segment)
    attended = low_back(low(attended))
    middle = low_back(low(stream + jnp.dot(attended, w_attn_out, precision=HIGHEST_PRECISION)))
    normed_two = low(crms_norm(middle, norm_gains[1]))
    hidden = low_back(jnp.dot(normed_two, w_up, precision=HIGHEST_PRECISION))
    active = low(jax.nn.gelu(hidden, approximate=True))
    block_out = middle + jnp.dot(active, w_down, precision=HIGHEST_PRECISION)
    return (block_out, middle)

def reference(stream_in, lengths, norm_gains, w_qkv, w_attn_out, w_up, w_down, cotangent):
    weights_all = (norm_gains.astype(jnp.float32), w_qkv.astype(jnp.float32), w_attn_out.astype(jnp.float32), w_up.astype(jnp.float32), w_down.astype(jnp.float32))
    streams = stream_in.astype(jnp.float32).reshape(N_DP, TOK_DEV, DC)
    cot_rows = cotangent.astype(jnp.float32).reshape(N_DP, TOK_DEV, DC)
    length_rows = lengths.reshape(N_DP, TOK_DEV // SHORT)

    def shard_step(partials, shard_data):
        stream, length_row, cot_shard = shard_data
        segment = segment_ids(length_row)

        def layer_fn(s_arg, g_arg, a_arg, b_arg, c_arg, d_arg):
            return layer(s_arg, g_arg, a_arg, b_arg, c_arg, d_arg, segment)
        block_out, pullback, middle = jax.vjp(layer_fn, stream, *weights_all, has_aux=True)
        gradients = pullback(cot_shard)
        row_total = lax.optimization_barrier(jnp.sum(middle, axis=1))
        squares = jnp.sum(middle * middle) + jnp.sum(row_total * row_total)
        updated = tuple((p + g for p, g in zip(partials[:-1], gradients[1:]))) + (partials[-1] + squares,)
        return (updated, (gradients[0].astype(jnp.bfloat16), block_out.astype(jnp.bfloat16)))
    initial = tuple((jnp.zeros_like(w) for w in weights_all)) + (jnp.zeros((), jnp.float32),)
    totals_all, (grad_in, block_out) = lax.scan(shard_step, initial, (streams, length_rows, cot_rows))
    block_io = jnp.stack([grad_in.reshape(TOKENS, DC), block_out.reshape(TOKENS, DC)], axis=0)
    stream_rms = jnp.sqrt(totals_all[5] / (TOKENS * D))
    return (block_io, totals_all[0], totals_all[1], totals_all[2], totals_all[3], totals_all[4], stream_rms)
```

```python
from types import SimpleNamespace

import jax
import jax.numpy as jnp
from jax import lax
from jax.experimental import pallas as pl
from jax.experimental.pallas import tpu as pltpu
from jax.sharding import PartitionSpec as P

HS = 64
EPSILON = 1e-05
MASKED = -1e30
BF = jnp.bfloat16
F32 = jnp.float32
MESH = pl.DeviceIdType.MESH
PIECE = 96
ROOT = 0.7978845608028654


def dot_nn(a, b):
    return jnp.dot(a, b, preferred_element_type=F32)


def dot_nt(a, b):
    return lax.dot_general(a, b, (((1,), (1,)), ((), ())), preferred_element_type=F32)


def dot_tn(a, b):
    return lax.dot_general(a, b, (((0,), (0,)), ((), ())), preferred_element_type=F32)


def rows(start, count, multiple):
    return pl.ds(pl.multiple_of(start, multiple), count)


def lane_groups(value):
    return [value[:, i : i + 128] for i in range(0, value.shape[1], 128)]


def kernel_for(sizes):
    R, H, D, C, FF, NH, N = (sizes[k] for k in ("R", "H", "D", "C", "FF", "NH", "N"))
    QW = NH * 3 * HS
    AW = NH * HS
    PIECES = (2 * D + AW + QW) // PIECE
    DOWN, UP, OUT, QKV = 0, FF, FF + D, FF + D + AW
    half_n = N // 2

    names = {}

    def scratch(name, shape, dtype):
        names[name] = pltpu.VMEM(shape, dtype)

    scratch("gbuf", (2, 8, D), F32)
    scratch("sp", (R, D), BF)
    scratch("wao", (AW, D), BF)
    scratch("wdn", (FF, D), BF)
    scratch("n1", (4 * R, D), BF)
    scratch("q", (NH, 4 * R, HS), BF)
    scratch("k", (NH, 4 * R, HS), BF)
    scratch("v", (NH, 4 * R, HS), BF)
    scratch("e", (10 * NH, H, R), BF)
    scratch("il", (NH, 4 * H, 1), F32)
    scratch("att", (4 * H, AW), BF)
    scratch("proj", (4, H, D), BF)
    scratch("rsc", (2, H, D), BF)
    scratch("ysnd", (H, D), BF)
    scratch("rsy", (H, D), BF)
    scratch("mid", (H, D), BF)
    scratch("n2", (4 * H, D), BF)
    scratch("cot", (4 * H, D), BF)
    scratch("act", (4 * H, FF), BF)
    scratch("gh", (4 * H, FF), BF)
    scratch("gp", (4, H, D), BF)
    scratch("rsc2", (2, H, D), BF)
    scratch("ysnd2", (H, D), BF)
    scratch("rsy2", (H, D), BF)
    scratch("gm", (4 * H, D), BF)
    scratch("gother", (H, D), BF)
    scratch("dmt", (QW, R), BF)
    scratch("dkt", (4, NH, HS, R), F32)
    scratch("dvt", (4, NH, HS, R), F32)
    scratch("gq", (QW, D), F32)
    scratch("rscf", (2, R, D), BF)
    scratch("rsyf", (R, D), BF)
    scratch("rsxf", (R, D), BF)
    scratch("gsrc", (PIECES * PIECE, D), BF)
    scratch("gb", (PIECES * PIECE // 2, D), BF)
    scratch("gc", (PIECES * PIECE // 2, D), BF)
    scratch("sm", (5, 8, D), F32)
    scratch("smr", (3, 8, D), F32)
    scratch("smz", (N, 8, D), F32)
    n_vmem = len(names)
    S_SRC, S_PART, S_OUT = 0, PIECES, 2 * PIECES
    R_A, R_B, R_C, R_RES = 0, PIECES, 2 * PIECES, 3 * PIECES
    FIRST = 4 * PIECES
    N_SEM = FIRST + 64 + N
    scratch_shapes = list(names.values()) + [
        pltpu.SemaphoreType.DMA((N_SEM,)),
        pltpu.SemaphoreType.DMA((N_SEM,)),
    ]

    def body(
        lens, gains, stream, cot_in, w_qkv, w_ao, w_up, w_dn, o_io, o_gr, o_sm, *refs
    ):
        m = SimpleNamespace(**dict(zip(names, refs[:n_vmem], strict=True)))
        ssem, rsem = refs[n_vmem:]
        res = o_gr
        x = lax.axis_index("blk")
        d = lax.axis_index("dp")
        t = lax.axis_index("tensor")
        y = lax.div(t, 2)
        c = lax.rem(t, 2)
        t1 = 2 * y + 1 - c
        t2 = 2 * (1 - y) + c
        t3 = 2 * (1 - y) + 1 - c
        core, ydev, xdev = (x, d, t1), (x, d, t2), (1 - x, d, t)
        xh, oh = x * H, (1 - x) * H

        counter = [FIRST]
        pending = []

        def link(src, dst, dev, s_idx=None, r_idx=None):
            if s_idx is None:
                s_idx = r_idx = counter[0]
                counter[0] += 1
            return pltpu.make_async_remote_copy(
                src_ref=src,
                dst_ref=dst,
                send_sem=ssem.at[s_idx],
                recv_sem=rsem.at[r_idx],
                device_id=dev,
                device_id_type=MESH,
            )

        def send(src, dst, dev):
            copy = link(src, dst, dev)
            copy.start()
            pending.append(copy)
            return copy

        barrier = pltpu.get_barrier_semaphore()
        for peer in (core, ydev, xdev):
            pl.semaphore_signal(barrier, inc=1, device_id=peer, device_id_type=MESH)
        for j in range(1, N):
            pl.semaphore_signal(
                barrier,
                inc=1,
                device_id=(x, lax.rem(d + j, N), t),
                device_id_type=MESH,
            )
        pl.semaphore_wait(barrier, 3 + N - 1)

        lane = lax.broadcasted_iota(jnp.int32, (1, D), 1)
        last = lane == D - 1

        def total(value):
            return jnp.sum(value, axis=1, keepdims=True)

        def full_of(stream_rows):
            full = jnp.where(last, -total(stream_rows), stream_rows)
            return full, lax.rsqrt(total(full * full) * (1.0 / D) + EPSILON)

        def crms_back(grad, full, r, gain):
            a = grad * gain
            mean = total(a * full) * (1.0 / D)
            df = r * (a - full * (r * r * mean))
            tail = total(jnp.where(last, df, 0.0))
            return jnp.where(last, 0.0, df - tail)

        m.gbuf[x] = jnp.broadcast_to(gains[...], (8, D))
        gain_copy = send(m.gbuf.at[x], m.gbuf.at[x], xdev)
        m.sp[:, D - 128 :] = jnp.zeros((R, 128), BF)
        m.sp[:, :C] = stream[...]
        m.wao[:, D - 128 :] = jnp.zeros((AW, 128), BF)
        m.wao[:, :C] = w_ao[...]
        m.wdn[:, D - 128 :] = jnp.zeros((FF, 128), BF)
        m.wdn[:, :C] = w_dn[...]
        here = rows(t * H, H, H)
        m.cot[here, D - 128 :] = jnp.zeros((H, 128), BF)
        m.cot[here, :C] = cot_in[rows(xh, H, H), :]
        gain_copy.wait_recv()

        def norm_one(start, count):
            def step(i, _):
                r0 = start + i * 64
                full, r = full_of(m.sp[rows(r0, 64, 64), :].astype(F32))
                m.n1[rows(t * R + r0, 64, 64), :] = (full * r * m.gbuf[0, :1, :]).astype(BF)
                return 0

            lax.fori_loop(0, count // 64, step, 0)

        half = H // 2
        norm_one(xh, H)
        y_copies = []
        for k in range(2):
            part = m.n1.at[rows(t * R + xh + k * half, half, half)]
            y_copies.append(send(part, part, ydev))
        norm_one(oh, H)
        part = m.n1.at[rows(t * R, R, R)]
        own_copy = send(part, part, core)
        part = m.cot.at[here]
        cot_core = send(part, part, core)

        def qkv_rows(start):
            mixed = dot_nn(m.n1[rows(start, H, H), :], w_qkv[...])
            at = rows(start, H, H)
            for h in range(NH):
                for p, ref in enumerate((m.q, m.k, m.v)):
                    part = mixed[:, (3 * h + p) * HS : (3 * h + p + 1) * HS]
                    if p == 0:
                        part = part * HS**-0.5
                    ref[h, at, :] = part.astype(BF)

        def qkv_block(block):
            lax.fori_loop(0, 2, lambda i, _: (qkv_rows(block * R + i * H), 0)[1], 0)

        qkv_block(t)
        own_copy.wait_recv()
        qkv_block(t1)
        fwd = []
        x_copies = []
        for k in range(2):
            y_copies[k].wait_recv()
            part = m.n1.at[rows(t2 * R + xh + k * half, half, half)]
            x_copies.append(send(part, part, xdev))
            fwd.append(send(part, part, core))
        part = m.cot.at[here]
        cot_y = send(part, part, ydev)
        for k in range(2):
            x_copies[k].wait_recv()
            part = m.n1.at[rows(t2 * R + oh + k * half, half, half)]
            fwd.append(send(part, part, core))
        qkv_block(t2)
        for copy in fwd:
            copy.wait_recv()
        qkv_block(t3)

        ends = [lens[0]]
        for i in range(1, 4):
            ends.append(ends[-1] + lens[i])

        def bias_of(b, kb):
            cut = (ends[0] > kb * R) & (ends[0] <= b * R)
            for e in ends[1:]:
                cut = cut | ((e > kb * R) & (e <= b * R))
            return jnp.where(cut, MASKED, 0.0).astype(F32)

        row_at = lax.broadcasted_iota(jnp.int32, (H, R), 0)
        col_at = lax.broadcasted_iota(jnp.int32, (H, R), 1)

        def unit(b, kb):
            return lax.div(b * (b + 1), 2) + kb

        def attend(b):
            mine = rows(b * R + xh, H, H)
            heads = [m.q[h, mine, :] for h in range(NH)]

            def scores(h, kb):
                return dot_nt(heads[h], m.k[h, rows(kb * R, R, R), :])

            def top(s, best):
                for g in lane_groups(s):
                    best = jnp.maximum(best, g)
                return best

            def masked(s):
                return jnp.where(col_at <= row_at + xh, s, MASKED)

            def peak(kb, best):
                bias = bias_of(b, kb)
                return tuple(top(scores(h, kb) + bias, best[h]) for h in range(NH))

            low = jnp.full((H, 128), MASKED, F32)
            best = tuple(top(masked(scores(h, b)), low) for h in range(NH))
            best = lax.fori_loop(0, b, peak, best)
            best = [jnp.max(v, axis=1, keepdims=True) for v in best]

            def weigh(h, kb, s, sums, acc):
                e = jnp.exp(s - best[h])
                for g in lane_groups(e):
                    sums = sums + g
                e = e.astype(BF)
                m.e[unit(b, kb) * NH + h] = e
                return sums, acc + dot_nn(e, m.v[h, rows(kb * R, R, R), :])

            def add(kb, carry):
                bias = bias_of(b, kb)
                return tuple(weigh(h, kb, scores(h, kb) + bias, *carry[h]) for h in range(NH))

            zero = (jnp.zeros((H, 128), F32), jnp.zeros((H, HS), F32))
            carry = tuple(weigh(h, b, masked(scores(h, b)), *zero) for h in range(NH))
            carry = lax.fori_loop(0, b, add, carry)
            at = rows(b * H, H, H)
            for h in range(NH):
                inverse = 1.0 / total(carry[h][0])
                m.il[h, at, :] = inverse
                m.att[at, h * HS : (h + 1) * HS] = (carry[h][1] * inverse).astype(BF)
            return dot_nn(m.att[at, :], m.wao[...]).astype(BF)

        C_PROJ = counter[0]
        counter[0] += 2

        def proj_copy(i):
            j = lax.div(i, 2)
            return link(m.proj.at[i], m.rsc.at[j], core, C_PROJ + j, C_PROJ + j)

        def add_rows(out, terms, count):
            def step(i, _):
                at = rows(i * 64, 64, 64)
                out[at, :] = sum(ref[at, :].astype(F32) for ref in terms).astype(BF)
                return 0

            lax.fori_loop(0, count // 64, step, 0)

        y_proj = link(m.ysnd, m.rsy, ydev)
        pending.append(y_proj)

        def attend_step(i, _):
            a, e = lax.div(i, 2), 1 - lax.rem(i, 2)
            g = (1 - y) * (1 - a) + y * a
            m.proj[i] = attend(2 * g + e)

            @pl.when(lax.rem(i, 2) == c)
            def _():
                proj_copy(i).start()

            @pl.when(i == 2)
            def _():
                proj_copy(c).wait_recv()
                add_rows(m.ysnd, (m.proj.at[1 - c], m.rsc.at[0]), H)
                y_proj.start()

            return 0

        lax.fori_loop(0, 4, attend_step, 0)
        proj_copy(2 + c).wait_recv()
        cot_core.wait_recv()
        cot_y.wait_recv()
        part = m.cot.at[rows(t2 * H, H, H)]
        cot_fwd = send(part, part, core)
        y_proj.wait_recv()

        def middle_step(i, squares):
            at = rows(i * 64, 64, 64)
            mid = m.sp[rows(xh + i * 64, 64, 64), :].astype(F32)
            mid = mid + m.proj[2 + 1 - c, at, :].astype(F32)
            mid = mid + m.rsc[1, at, :].astype(F32) + m.rsy[at, :].astype(F32)
            mid = mid.astype(BF)
            m.mid[at, :] = mid
            full, r = full_of(mid.astype(F32))
            m.n2[rows(t * H + i * 64, 64, 64), :] = (full * r * m.gbuf[1, :1, :]).astype(BF)
            return squares + jnp.sum(full * full, axis=0, keepdims=True)

        squares = lax.fori_loop(0, H // 64, middle_step, jnp.zeros((1, D), F32))
        m.sm[0] = jnp.zeros((8, D), F32)
        m.sm[0, 2:3, :] = squares

        n2_y = send(m.n2.at[here], m.n2.at[here], ydev)
        n2_core = send(m.n2.at[here], m.n2.at[here], core)

        def feed(s, i):
            at = rows(s * H, H, H)
            for f in range(FF // 256):
                cols = slice(f * 256, (f + 1) * 256)
                hidden = dot_nn(m.n2[at, :], w_up[:, cols])
                grad = dot_nt(m.cot[at, :], m.wdn[cols, :])
                square = hidden * hidden
                bent = jnp.tanh(ROOT * hidden * (1.0 + 0.044715 * square))
                gate = 0.5 * (1.0 + bent)
                m.act[at, cols] = (hidden * gate).astype(BF)
                slope = gate + (0.5 * ROOT) * hidden * (1.0 - bent * bent) * (
                    1.0 + (3 * 0.044715) * square
                )
                m.gh[at, cols] = (grad * slope).astype(BF)
            m.gp[i] = dot_nt(m.gh[at, :], w_up[...]).astype(BF)

        C_GP = counter[0]
        counter[0] += 2
        C_N2 = counter[0]
        counter[0] += 1
        gp_copies = [
            link(m.gp.at[2 * j + 1], m.rsc2.at[j], core, C_GP + j, C_GP + j) for j in range(2)
        ]
        part = m.n2.at[rows(t2 * H, H, H)]
        n2_fwd = link(part, part, core, C_N2, C_N2)
        pending.append(n2_fwd)
        pending.extend(gp_copies)

        def feed_step(i, _):
            a, e = lax.div(i, 2), lax.rem(i, 2)
            s = 2 * (y + a - 2 * y * a) + (c + e - 2 * c * e)

            @pl.when(i == 1)
            def _():
                n2_core.wait_recv()

            @pl.when(i == 2)
            def _():
                n2_y.wait_recv()
                n2_fwd.start()
                cot_fwd.wait_recv()

            @pl.when(i == 3)
            def _():
                n2_fwd.wait_recv()

            feed(s, i)

            @pl.when(i == 1)
            def _():
                gp_copies[0].start()

            @pl.when(i == 3)
            def _():
                gp_copies[1].start()

            return 0

        lax.fori_loop(0, 4, feed_step, 0)
        gp_copies[1].wait_recv()
        add_rows(m.ysnd2, (m.gp.at[2], m.rsc2.at[1]), H)
        gp_y = send(m.ysnd2, m.rsy2, ydev)

        is_mid = (d == half_n - 1) | (d == half_n)
        is_end = (d == 0) | (d == N - 1)
        side = jnp.where(d < half_n, 0, 1)
        step_in = 1 - 2 * side
        inner = (x, lax.rem(d + step_in + N, N), t)
        outer = (x, lax.rem(d - step_in + N, N), t)

        def piece(ref, p):
            return ref.at[rows(p * PIECE, PIECE, 16)]

        def in_copy(p):
            return link(piece(m.gsrc, p), piece(res, p), inner, S_SRC + p, R_A + p)

        def mid_copy(p):
            to = piece(m.gb, lax.div(p, 2))
            return link(piece(m.gsrc, p), to, inner, S_SRC + p, R_B + p)

        def x_copy(p):
            to = piece(m.gc, lax.div(p, 2))
            return link(piece(m.gsrc, p), to, xdev, S_SRC + p, R_C + p)

        def part_copy(p):
            return link(piece(res, p), piece(res, p), inner, S_PART + p, R_RES + p)

        def out_copy(p):
            return link(piece(res, p), piece(res, p), outer, S_OUT + p, R_RES + p)

        def gather_piece(out, p, ref, q):
            def step(i, _):
                at = rows(p * PIECE + i * 32, 32, 16)
                other = ref[rows(q * PIECE + i * 32, 32, 16), :].astype(F32)
                out[at, :] = (m.gsrc[at, :].astype(F32) + other).astype(BF)
                return 0

            lax.fori_loop(0, PIECE // 32, step, 0)

        def valid(p):
            return (p >= 0) & (p < PIECES)

        def owns(p):
            return is_mid & (side == lax.rem(p + 2 * PIECES, 2))

        def serve(s):
            @pl.when(valid(s) & jnp.logical_not(is_mid))
            def _():
                if N > 4:

                    @pl.when(jnp.logical_not(is_end))
                    def _():
                        in_copy(s).wait_recv()
                        gather_piece(m.gsrc, s, res, s)

                in_copy(s).start()

            p2 = s - 1

            @pl.when(valid(p2) & is_mid)
            def _():
                @pl.when(jnp.logical_not(is_end))
                def _():
                    in_copy(p2).wait_recv()
                    gather_piece(m.gsrc, p2, res, p2)

                @pl.when(jnp.logical_not(owns(p2)))
                def _():
                    mid_copy(p2).start()

            p3 = s - 2

            @pl.when(valid(p3) & owns(p3))
            def _():
                mid_copy(p3).wait_recv()
                gather_piece(m.gsrc, p3, m.gb, lax.div(p3, 2))
                x_copy(p3).start()

            p4 = s - 3

            @pl.when(valid(p4) & owns(p4))
            def _():
                x_copy(p4).wait_recv()
                gather_piece(res, p4, m.gc, lax.div(p4, 2))
                part_copy(p4).start()

                @pl.when(jnp.logical_not(is_end))
                def _():
                    out_copy(p4).start()

            p5 = s - 4

            @pl.when(valid(p5) & is_mid & jnp.logical_not(owns(p5)))
            def _():
                part_copy(p5).wait_recv()

                @pl.when(jnp.logical_not(is_end))
                def _():
                    out_copy(p5).start()

            if N > 4:
                p6 = s - 5

                @pl.when(valid(p6) & jnp.logical_not(is_mid) & jnp.logical_not(is_end))
                def _():
                    part_copy(p6).wait_recv()
                    out_copy(p6).start()

        def serve_all_sent():
            def step(p, _):
                @pl.when(is_end & jnp.logical_not(is_mid))
                def _():
                    part_copy(p).wait_recv()

                in_copy(p).wait_send()

                @pl.when(owns(p))
                def _():
                    part_copy(p).wait_send()

                @pl.when(jnp.logical_not(is_end))
                def _():
                    out_copy(p).wait_send()

                return 0

            lax.fori_loop(0, PIECES, step, 0)

        def down_step(f, _):
            at = pl.ds(pl.multiple_of(f * 256, 256), 256)
            m.gsrc[rows(DOWN + f * 256, 256, 16), :] = dot_tn(m.act[:, at], m.cot[...]).astype(BF)
            return 0

        def up_step(f, _):
            at = pl.ds(pl.multiple_of(f * 256, 256), 256)
            m.gsrc[rows(UP + f * 256, 256, 16), :] = dot_tn(m.n2[:, at], m.gh[...]).astype(BF)
            return 0

        lax.fori_loop(0, FF // 256, down_step, 0)
        serve(0)

        gp_copies[0].wait_recv()
        gp_y.wait_recv()

        def grad_middle_step(i, gain):
            at = rows(i * 64, 64, 64)
            grad = m.gp[0, at, :].astype(F32) + m.rsc2[0, at, :].astype(F32)
            grad = grad + m.rsy2[at, :].astype(F32)
            full, r = full_of(m.mid[at, :].astype(F32))
            back = crms_back(grad, full, r, m.gbuf[1, :1, :])
            mine = rows(t * H + i * 64, 64, 64)
            m.gm[mine, :] = (m.cot[mine, :].astype(F32) + back).astype(BF)
            return gain + jnp.sum(grad * full * r, axis=0, keepdims=True)

        gain_two = lax.fori_loop(0, H // 64, grad_middle_step, jnp.zeros((1, D), F32))
        m.sm[0, 1:2, :] = gain_two
        gm_y = send(m.gm.at[here], m.gm.at[here], ydev)
        gm_core = send(m.gm.at[here], m.gm.at[here], core)
        gm_x = link(m.gm.at[here], m.gother, xdev)

        @pl.when(x == 1)
        def _():
            gm_x.start()

        lax.fori_loop(0, D // 256, up_step, 0)
        serve(1)

        def mlp_step(i, _):
            a, e = lax.div(i, 2), lax.rem(i, 2)
            s = 2 * (y + a - 2 * y * a) + (c + e - 2 * c * e)
            m.proj[i] = dot_nn(m.act[rows(s * H, H, H), :], m.wdn[...]).astype(BF)
            return 0

        proj_copy(c).wait_send()
        proj_copy(2 + c).wait_send()
        lax.fori_loop(0, 4, mlp_step, 0)
        mp_copies = [send(m.proj.at[2 * j + 1], m.rsc.at[j], core) for j in range(2)]
        serve(2)
        gm_y.wait_recv()
        part = m.gm.at[rows(t2 * H, H, H)]
        gm_fwd = send(part, part, core)
        mp_copies[1].wait_recv()
        y_proj.wait_send()
        add_rows(m.ysnd, (m.proj.at[2], m.rsc.at[1]), H)
        mp_y = send(m.ysnd, m.rsy, ydev)
        gm_core.wait_recv()
        gm_fwd.wait_recv()

        m.gsrc[OUT : OUT + AW, :] = dot_tn(m.att[...], m.gm[...]).astype(BF)
        m.dkt[...] = jnp.zeros_like(m.dkt)
        m.dvt[...] = jnp.zeros_like(m.dvt)
        m.gq[...] = jnp.zeros_like(m.gq)

        C_GN = counter[0]
        counter[0] += 2

        def pair_rows(j):
            return rows(j * R, R, R)

        def gn_copy(j):
            return link(m.gh.at[pair_rows(j)], m.rscf.at[j], core, C_GN + j, C_GN + j)

        C_YF = counter[0]
        counter[0] += 4
        chunk = R // 4

        def yf_copy(k):
            src = m.act.at[rows((1 - y) * R + k * chunk, chunk, chunk)]
            dst = m.rsyf.at[rows(k * chunk, chunk, chunk)]
            return link(src, dst, ydev, C_YF + k, C_YF + k)

        def send_far():
            gn_copy(1 - y).wait_recv()

            def step(k, _):
                def inside(i, _):
                    r0 = k * chunk + i * 64
                    at = rows((1 - y) * R + r0, 64, 64)
                    both = m.act[at, :].astype(F32) + m.rscf[1 - y, rows(r0, 64, 64), :].astype(F32)
                    m.act[at, :] = both.astype(BF)
                    return 0

                lax.fori_loop(0, chunk // 64, inside, 0)
                yf_copy(k).start()
                return 0

            lax.fori_loop(0, 4, step, 0)

        far_step = 3 - (2 * (1 - y) + c)

        def back_block(i, _):
            b = 3 - i
            at = rows(b * H, H, H)
            mine = rows(b * R + xh, H, H)
            grad_att = dot_nt(m.gm[at, :], m.wao[...])
            outs, offs, out_ts, q_ts = [], [], [], []
            for h in range(NH):
                cols = slice(h * HS, (h + 1) * HS)
                inverse = m.il[h, at, :]
                out = grad_att[:, cols].astype(BF).astype(F32)
                delta = total(out * m.att[at, cols].astype(F32))
                offs.append(delta * inverse)
                out = (out * inverse).astype(BF)
                outs.append(out)
                out_ts.append(jnp.transpose(out))
                q_ts.append(jnp.transpose(m.q[h, mine, :]))

            def keys(kb, grads):
                new = []
                for h in range(NH):
                    e = m.e[unit(b, kb) * NH + h]
                    at_k = rows(kb * R, R, R)
                    dp = dot_nt(outs[h], m.v[h, at_k, :])
                    ds = (e.astype(F32) * (dp - offs[h])).astype(BF)
                    new.append(grads[h] + dot_nn(ds, m.k[h, at_k, :]))
                    m.dkt[kb, h] += dot_nn(q_ts[h], ds)
                    m.dvt[kb, h] += dot_nn(out_ts[h], e)
                serve(3 + 4 * i - lax.div(i * (i - 1), 2) + kb)
                return tuple(new)

            grads = lax.fori_loop(0, b + 1, keys, (jnp.zeros((H, HS), F32),) * NH)
            for h in range(NH):
                base = 3 * h * HS
                grad_q = jnp.transpose(grads[h] * HS**-0.5).astype(BF)
                m.dmt[base : base + HS, rows(xh, H, H)] = grad_q
                m.dmt[base : base + HS, rows(oh, H, H)] = jnp.zeros((HS, H), BF)
                m.dmt[base + HS : base + 2 * HS, :] = m.dkt[b, h].astype(BF)
                m.dmt[base + 2 * HS : base + 3 * HS, :] = m.dvt[b, h].astype(BF)
            n1_rows = rows(b * R, R, R)
            m.gq[...] += dot_nn(m.dmt[...], m.n1[n1_rows, :])
            back = dot_nt(jnp.transpose(m.dmt[...]), w_qkv[...]).astype(BF)
            j = lax.div(b, 2)

            @pl.when(lax.rem(b, 2) == c)
            def _():
                m.act[pair_rows(j), :] = back

            @pl.when(lax.rem(b, 2) != c)
            def _():
                m.gh[pair_rows(j), :] = back
                gn_copy(j).start()

            @pl.when(i == far_step + 1)
            def _():
                send_far()

            return 0

        lax.fori_loop(0, 4, back_block, 0)
        pl.when(far_step == 3)(send_far)
        m.gsrc[QKV : QKV + QW, :] = m.gq[...].astype(BF)
        served = 13

        mp_copies[0].wait_recv()
        mp_y.wait_recv()
        n2_y.wait_send()
        n2_core.wait_send()
        add_rows(m.n2.at[here], (m.mid, m.proj.at[0], m.rsc.at[0], m.rsy), H)
        bo_x = link(m.n2.at[here], m.gother, xdev)

        @pl.when(x == 0)
        def _():
            bo_x.start()

        lax.fori_loop(served, 18, lambda s, _: (serve(s), 0)[1], 0)

        gn_copy(y).wait_recv()

        C_XF = counter[0]
        counter[0] += 4

        def xf_copy(k):
            src = m.act.at[rows(y * R + k * chunk, chunk, chunk)]
            dst = m.rsxf.at[rows(k * chunk, chunk, chunk)]
            return link(src, dst, xdev, C_XF + k, C_XF + k)

        def near_sum(k):
            yf_copy(k).wait_recv()

            def inside(i, _):
                r0 = k * chunk + i * 64
                at = rows(y * R + r0, 64, 64)
                here_rows = rows(r0, 64, 64)
                both = m.act[at, :].astype(F32) + m.rscf[y, here_rows, :].astype(F32)
                m.act[at, :] = (both + m.rsyf[here_rows, :].astype(F32)).astype(BF)
                return 0

            lax.fori_loop(0, chunk // 64, inside, 0)

        @pl.when(x == 1)
        def _():
            def step(k, _):
                near_sum(k)
                xf_copy(k).start()
                return 0

            lax.fori_loop(0, 4, step, 0)

        @pl.when(x == 0)
        def _():
            gm_x.wait_recv()
            m.sm[0, 0:1, :] = jnp.zeros((1, D), F32)

            def step(k, _):
                near_sum(k)
                xf_copy(k).wait_recv()

                def inside(i, gain):
                    r0 = k * chunk + i * 64
                    here_rows = rows(r0, 64, 64)
                    grad = m.act[rows(y * R + r0, 64, 64), :].astype(F32)
                    grad = grad + m.rsxf[here_rows, :].astype(F32)
                    full, r = full_of(m.sp[here_rows, :].astype(F32))
                    back = crms_back(grad, full, r, m.gbuf[0, :1, :])
                    m.rsyf[here_rows, :] = back.astype(BF)
                    return gain + jnp.sum(grad * full * r, axis=0, keepdims=True)

                gain = lax.fori_loop(0, chunk // 64, inside, jnp.zeros((1, D), F32))
                m.sm[0, 0:1, :] += gain
                return 0

            lax.fori_loop(0, 4, step, 0)

            def out_step(i, _):
                at = rows(i * 64, 64, 64)
                one = m.gm[rows(t * H + i * 64, 64, 64), :].astype(F32) + m.rsyf[at, :].astype(F32)
                o_io[0, at, :] = one[:, :C].astype(BF)
                below = rows(H + i * 64, 64, 64)
                two = m.gother[at, :].astype(F32) + m.rsyf[below, :].astype(F32)
                o_io[0, below, :] = two[:, :C].astype(BF)
                return 0

            lax.fori_loop(0, H // 64, out_step, 0)

        @pl.when(x == 1)
        def _():
            bo_x.wait_recv()
            o_io[0, 0:H, :] = m.gother[:, :C]
            o_io[0, H:R, :] = m.n2[here, :C]

        for j, peer in enumerate((core, ydev, xdev)):
            copy = send(m.sm.at[j], m.smr.at[j], peer)
            copy.wait_recv()
            m.sm[j + 1] = m.sm[j] + m.smr[j]
        z_copies = []
        for j in range(1, N):
            z_copies.append(send(m.sm.at[3], m.smz.at[j], (x, lax.rem(d + j, N), t)))
        lax.fori_loop(18, PIECES + 6, lambda s, _: (serve(s), 0)[1], 0)
        everything = m.sm[3]
        for j in range(1, N):
            z_copies[j - 1].wait_recv()
            everything = everything + m.smz[j]
        o_sm[...] = everything

        serve_all_sent()
        waited = {id(n2_y), id(n2_core), id(y_proj)}
        for copy in pending:
            if id(copy) not in waited:
                copy.wait_send()
        for j in range(2):
            gn_copy(j).wait_send()
        for k in range(4):
            yf_copy(k).wait_send()

        @pl.when(x == 1)
        def _():
            gm_x.wait_send()
            for k in range(4):
                xf_copy(k).wait_send()

        @pl.when(x == 0)
        def _():
            bo_x.wait_send()

        assert counter[0] <= N_SEM

    return body, scratch_shapes, PIECES * PIECE, (DOWN, UP, OUT, QKV)


def per_device(mesh):
    N = mesh.shape["dp"]
    assert mesh.shape["blk"] == 2 and mesh.shape["tensor"] == 4 and N % 2 == 0

    def run(stream_in, lengths, norm_gains, w_qkv, w_attn_out, w_up, w_down, cotangent):
        R, C = stream_in.shape
        D = norm_gains.shape[1]
        FF = w_up.shape[1]
        NH = w_qkv.shape[1] // (3 * HS)
        body, scratch, grad_rows, (DOWN, UP, OUT, QKV) = kernel_for(
            dict(R=R, H=R // 2, D=D, C=C, FF=FF, NH=NH, N=N)
        )
        vmem = pl.BlockSpec(memory_space=pltpu.VMEM)
        block_io, grads, small = pl.pallas_call(
            body,
            out_shape=(
                jax.ShapeDtypeStruct((1, R, C), BF),
                jax.ShapeDtypeStruct((grad_rows, D), BF),
                jax.ShapeDtypeStruct((8, D), F32),
            ),
            in_specs=[pl.BlockSpec(memory_space=pltpu.SMEM)] + [vmem] * 7,
            out_specs=(vmem,) * 3,
            scratch_shapes=scratch,
            compiler_params=pltpu.CompilerParams(
                collective_id=0, has_side_effects=True, vmem_limit_bytes=62 << 20
            ),
        )(lengths, norm_gains, stream_in, cotangent, w_qkv, w_attn_out, w_up, w_down)
        gain = jnp.where(lax.axis_index("blk") == 0, small[0:1], small[1:2])
        entries = 4 * R * N * D
        stream_rms = jnp.sqrt(jnp.sum(small[2]) / entries)
        return (
            block_io,
            gain,
            grads[QKV:].T.astype(F32),
            grads[OUT:QKV, :C].astype(F32),
            grads[UP:OUT].astype(F32),
            grads[DOWN:UP, :C].astype(F32),
            stream_rms,
        )

    return run


def solution(mesh):
    in_specs = (
        P(("dp", "tensor"), None),
        P("dp"),
        P("blk", None),
        P(None, "tensor"),
        P("tensor", None),
        P(None, "tensor"),
        P("tensor", None),
        P(("dp", "tensor"), None),
    )
    out_specs = (
        P("blk", ("dp", "tensor"), None),
        P("blk", None),
        P(None, "tensor"),
        P("tensor", None),
        P(None, "tensor"),
        P("tensor", None),
        P(),
    )
    return jax.shard_map(
        per_device(mesh), mesh=mesh, in_specs=in_specs, out_specs=out_specs, check_vma=False
    )
```

```python
from types import SimpleNamespace

import jax
import jax.numpy as jnp
from jax import lax
from jax.experimental import pallas as pl
from jax.experimental.pallas import tpu as pltpu
from jax.sharding import PartitionSpec as P

HS = 64
EPSILON = 1e-05
MASKED = -1e30
BF = jnp.bfloat16
F32 = jnp.float32
MESH = pl.DeviceIdType.MESH
PIECE = 96
ROOT = 0.7978845608028654


def dot_nn(a, b):
    return jnp.dot(a, b, preferred_element_type=F32)


def dot_nt(a, b):
    return lax.dot_general(a, b, (((1,), (1,)), ((), ())), preferred_element_type=F32)


def dot_tn(a, b):
    return lax.dot_general(a, b, (((0,), (0,)), ((), ())), preferred_element_type=F32)


def rows(start, count, multiple):
    return pl.ds(pl.multiple_of(start, multiple), count)


def lane_groups(value):
    return [value[:, i : i + 128] for i in range(0, value.shape[1], 128)]


def kernel_for(sizes):
    R, H, D, C, FF, NH, N = (sizes[k] for k in ("R", "H", "D", "C", "FF", "NH", "N"))
    QW = NH * 3 * HS
    AW = NH * HS
    PIECES = (2 * D + AW + QW) // PIECE
    DOWN, UP, OUT, QKV = 0, FF, FF + D, FF + D + AW
    half_n = N // 2

    names = {}

    def scratch(name, shape, dtype):
        names[name] = pltpu.VMEM(shape, dtype)

    scratch("gbuf", (2, 8, D), F32)
    scratch("stream", (R, C), BF)
    scratch("cot_in", (H, C), BF)
    scratch("wqkv", (QW, D), BF)
    scratch("wao_in", (AW, C), BF)
    scratch("wup", (D, FF), BF)
    scratch("wdn_in", (FF, C), BF)
    scratch("sp", (R, D), BF)
    scratch("wao", (AW, D), BF)
    scratch("wdn", (FF, D), BF)
    scratch("n1", (4 * R, D), BF)
    scratch("q", (NH, 4 * R, HS), BF)
    scratch("k", (NH, 4 * R, HS), BF)
    scratch("v", (NH, 4 * R, HS), BF)
    scratch("e", (10 * NH, H, R), BF)
    scratch("il", (NH, 4 * H, 1), F32)
    scratch("att", (4 * H, AW), BF)
    scratch("proj", (4, H, D), BF)
    scratch("rsc", (2, H, D), BF)
    scratch("ysnd", (H, D), BF)
    scratch("rsy", (H, D), BF)
    scratch("mid", (H, D), BF)
    scratch("n2", (4 * H, D), BF)
    scratch("cot", (4 * H, D), BF)
    scratch("act", (4 * H, FF), BF)
    scratch("gh", (4 * H, FF), BF)
    scratch("gp", (4, H, D), BF)
    scratch("rsc2", (2, H, D), BF)
    scratch("ysnd2", (H, D), BF)
    scratch("rsy2", (H, D), BF)
    scratch("gm", (4 * H, D), BF)
    scratch("gother", (H, D), BF)
    scratch("dmt", (QW, R), BF)
    scratch("dkt", (4, NH, HS, R), F32)
    scratch("dvt", (4, NH, HS, R), F32)
    scratch("gq", (QW, D), F32)
    scratch("rscf", (2, R, D), BF)
    scratch("rsyf", (R, D), BF)
    scratch("rsxf", (R, D), BF)
    scratch("gsrc", (PIECES * PIECE, D), BF)
    scratch("gb", (PIECES * PIECE // 2, D), BF)
    scratch("gc", (PIECES * PIECE // 2, D), BF)
    scratch("sm", (5, 8, D), F32)
    scratch("smr", (3, 8, D), F32)
    scratch("smz", (N, 8, D), F32)
    n_vmem = len(names)
    S_SRC, S_PART, S_OUT = 0, PIECES, 2 * PIECES
    R_A, R_B, R_C, R_RES = 0, PIECES, 2 * PIECES, 3 * PIECES
    FIRST = 4 * PIECES
    N_SEM = FIRST + 64 + N
    scratch_shapes = list(names.values()) + [
        pltpu.SemaphoreType.DMA((N_SEM,)),
        pltpu.SemaphoreType.DMA((N_SEM,)),
        pltpu.SemaphoreType.DMA((6,)),
    ]

    def body(
        lens, gains, stream, cot_in, w_qkv, w_ao, w_up, w_dn, o_io, o_gr, o_sm, *refs
    ):
        m = SimpleNamespace(**dict(zip(names, refs[:n_vmem], strict=True)))
        ssem, rsem, lsem = refs[n_vmem:]
        res = o_gr
        x = lax.axis_index("blk")
        d = lax.axis_index("dp")
        t = lax.axis_index("tensor")
        y = lax.div(t, 2)
        c = lax.rem(t, 2)
        t1 = 2 * y + 1 - c
        t2 = 2 * (1 - y) + c
        t3 = 2 * (1 - y) + 1 - c
        core, ydev, xdev = (x, d, t1), (x, d, t2), (1 - x, d, t)
        xh, oh = x * H, (1 - x) * H

        counter = [FIRST]
        pending = []

        def link(src, dst, dev, s_idx=None, r_idx=None):
            if s_idx is None:
                s_idx = r_idx = counter[0]
                counter[0] += 1
            return pltpu.make_async_remote_copy(
                src_ref=src,
                dst_ref=dst,
                send_sem=ssem.at[s_idx],
                recv_sem=rsem.at[r_idx],
                device_id=dev,
                device_id_type=MESH,
            )

        def send(src, dst, dev):
            copy = link(src, dst, dev)
            copy.start()
            pending.append(copy)
            return copy

        loads = []
        for i, (src, dst) in enumerate(
            (
                (stream, m.stream),
                (w_qkv, m.wqkv),
                (cot_in.at[rows(xh, H, H)], m.cot_in),
                (w_ao, m.wao_in),
                (w_up, m.wup),
                (w_dn, m.wdn_in),
            )
        ):
            loads.append(pltpu.make_async_copy(src, dst, lsem.at[i]))
            loads[-1].start()

        barrier = pltpu.get_barrier_semaphore()
        for peer in (core, ydev, xdev):
            pl.semaphore_signal(barrier, inc=1, device_id=peer, device_id_type=MESH)
        for j in range(1, N):
            pl.semaphore_signal(
                barrier,
                inc=1,
                device_id=(x, lax.rem(d + j, N), t),
                device_id_type=MESH,
            )
        pl.semaphore_wait(barrier, 3 + N - 1)

        lane = lax.broadcasted_iota(jnp.int32, (1, D), 1)
        last = lane == D - 1

        def total(value):
            return jnp.sum(value, axis=1, keepdims=True)

        def full_of(stream_rows):
            full = jnp.where(last, -total(stream_rows), stream_rows)
            return full, lax.rsqrt(total(full * full) * (1.0 / D) + EPSILON)

        def crms_back(grad, full, r, gain):
            a = grad * gain
            mean = total(a * full) * (1.0 / D)
            df = r * (a - full * (r * r * mean))
            tail = total(jnp.where(last, df, 0.0))
            return jnp.where(last, 0.0, df - tail)

        m.gbuf[x] = jnp.broadcast_to(gains[...], (8, D))
        gain_copy = send(m.gbuf.at[x], m.gbuf.at[x], xdev)
        m.sp[:, D - 128 :] = jnp.zeros((R, 128), BF)
        loads[0].wait()
        m.sp[:, :C] = m.stream[...]
        here = rows(t * H, H, H)
        gain_copy.wait_recv()

        def norm_one(start, count):
            def step(i, _):
                r0 = start + i * 64
                full, r = full_of(m.sp[rows(r0, 64, 64), :].astype(F32))
                m.n1[rows(t * R + r0, 64, 64), :] = (full * r * m.gbuf[0, :1, :]).astype(BF)
                return 0

            lax.fori_loop(0, count // 64, step, 0)

        half = H // 4
        y_copies = []
        for k in range(4):
            norm_one(xh + k * half, half)
            part = m.n1.at[rows(t * R + xh + k * half, half, half)]
            y_copies.append(send(part, part, ydev))
        norm_one(oh, H)
        part = m.n1.at[rows(t * R, R, R)]
        own_copy = send(part, part, core)
        loads[2].wait()
        m.cot[here, D - 128 :] = jnp.zeros((H, 128), BF)
        m.cot[here, :C] = m.cot_in[...]
        part = m.cot.at[here]
        cot_core = send(part, part, core)

        def qkv_rows(start):
            mixed = dot_nt(m.n1[rows(start, H, H), :], m.wqkv[...])
            at = rows(start, H, H)
            for h in range(NH):
                for p, ref in enumerate((m.q, m.k, m.v)):
                    part = mixed[:, (3 * h + p) * HS : (3 * h + p + 1) * HS]
                    if p == 0:
                        part = part * HS**-0.5
                    ref[h, at, :] = part.astype(BF)

        def qkv_block(block):
            lax.fori_loop(0, 2, lambda i, _: (qkv_rows(block * R + i * H), 0)[1], 0)

        loads[1].wait()
        qkv_block(t)
        own_copy.wait_recv()
        qkv_block(t1)
        for load in loads[3:]:
            load.wait()
        m.wao[:, D - 128 :] = jnp.zeros((AW, 128), BF)
        m.wao[:, :C] = m.wao_in[...]
        m.wdn[:, D - 128 :] = jnp.zeros((FF, 128), BF)
        m.wdn[:, :C] = m.wdn_in[...]
        fwd = []
        x_copies = []
        for k in range(4):
            y_copies[k].wait_recv()
            part = m.n1.at[rows(t2 * R + xh + k * half, half, half)]
            x_copies.append(send(part, part, xdev))
            fwd.append(send(part, part, core))
        part = m.cot.at[here]
        cot_y = send(part, part, ydev)
        for k in range(4):
            x_copies[k].wait_recv()
            part = m.n1.at[rows(t2 * R + oh + k * half, half, half)]
            fwd.append(send(part, part, core))
        qkv_block(t2)
        for copy in fwd:
            copy.wait_recv()
        qkv_block(t3)

        ends = [lens[0]]
        for i in range(1, 4):
            ends.append(ends[-1] + lens[i])

        def bias_of(b, kb):
            cut = (ends[0] > kb * R) & (ends[0] <= b * R)
            for e in ends[1:]:
                cut = cut | ((e > kb * R) & (e <= b * R))
            return jnp.where(cut, MASKED, 0.0).astype(F32)

        row_at = lax.broadcasted_iota(jnp.int32, (H, R), 0)
        col_at = lax.broadcasted_iota(jnp.int32, (H, R), 1)

        def unit(b, kb):
            return lax.div(b * (b + 1), 2) + kb

        def attend(b):
            mine = rows(b * R + xh, H, H)
            heads = [m.q[h, mine, :] for h in range(NH)]

            def scores(h, kb):
                return dot_nt(heads[h], m.k[h, rows(kb * R, R, R), :])

            def top(s, best):
                for g in lane_groups(s):
                    best = jnp.maximum(best, g)
                return best

            def masked(s):
                return jnp.where(col_at <= row_at + xh, s, MASKED)

            def peak(kb, best):
                bias = bias_of(b, kb)
                return tuple(top(scores(h, kb) + bias, best[h]) for h in range(NH))

            low = jnp.full((H, 128), MASKED, F32)
            best = tuple(top(masked(scores(h, b)), low) for h in range(NH))
            best = lax.fori_loop(0, b, peak, best)
            best = [jnp.max(v, axis=1, keepdims=True) for v in best]

            def weigh(h, kb, s, sums, acc):
                e = jnp.exp(s - best[h])
                for g in lane_groups(e):
                    sums = sums + g
                e = e.astype(BF)
                m.e[unit(b, kb) * NH + h] = e
                return sums, acc + dot_nn(e, m.v[h, rows(kb * R, R, R), :])

            def add(kb, carry):
                bias = bias_of(b, kb)
                return tuple(weigh(h, kb, scores(h, kb) + bias, *carry[h]) for h in range(NH))

            zero = (jnp.zeros((H, 128), F32), jnp.zeros((H, HS), F32))
            carry = tuple(weigh(h, b, masked(scores(h, b)), *zero) for h in range(NH))
            carry = lax.fori_loop(0, b, add, carry)
            at = rows(b * H, H, H)
            for h in range(NH):
                inverse = 1.0 / total(carry[h][0])
                m.il[h, at, :] = inverse
                m.att[at, h * HS : (h + 1) * HS] = (carry[h][1] * inverse).astype(BF)
            return dot_nn(m.att[at, :], m.wao[...]).astype(BF)

        C_PROJ = counter[0]
        counter[0] += 2

        def proj_copy(i):
            j = lax.div(i, 2)
            return link(m.proj.at[i], m.rsc.at[j], core, C_PROJ + j, C_PROJ + j)

        def add_rows(out, terms, count):
            def step(i, _):
                at = rows(i * 64, 64, 64)
                out[at, :] = sum(ref[at, :].astype(F32) for ref in terms).astype(BF)
                return 0

            lax.fori_loop(0, count // 64, step, 0)

        y_proj = link(m.ysnd, m.rsy, ydev)
        pending.append(y_proj)

        def attend_step(i, _):
            a, e = lax.div(i, 2), 1 - lax.rem(i, 2)
            g = (1 - y) * (1 - a) + y * a
            m.proj[i] = attend(2 * g + e)

            @pl.when(lax.rem(i, 2) == c)
            def _():
                proj_copy(i).start()

            @pl.when(i == 2)
            def _():
                proj_copy(c).wait_recv()
                add_rows(m.ysnd, (m.proj.at[1 - c], m.rsc.at[0]), H)
                y_proj.start()

            return 0

        lax.fori_loop(0, 4, attend_step, 0)
        proj_copy(2 + c).wait_recv()
        cot_core.wait_recv()
        cot_y.wait_recv()
        part = m.cot.at[rows(t2 * H, H, H)]
        cot_fwd = send(part, part, core)
        y_proj.wait_recv()

        def middle_step(i, squares):
            at = rows(i * 64, 64, 64)
            mid = m.sp[rows(xh + i * 64, 64, 64), :].astype(F32)
            mid = mid + m.proj[2 + 1 - c, at, :].astype(F32)
            mid = mid + m.rsc[1, at, :].astype(F32) + m.rsy[at, :].astype(F32)
            mid = mid.astype(BF)
            m.mid[at, :] = mid
            full, r = full_of(mid.astype(F32))
            m.n2[rows(t * H + i * 64, 64, 64), :] = (full * r * m.gbuf[1, :1, :]).astype(BF)
            return squares + jnp.sum(full * full, axis=0, keepdims=True)

        squares = lax.fori_loop(0, H // 64, middle_step, jnp.zeros((1, D), F32))
        m.sm[0] = jnp.zeros((8, D), F32)
        m.sm[0, 2:3, :] = squares

        n2_y = send(m.n2.at[here], m.n2.at[here], ydev)
        n2_core = send(m.n2.at[here], m.n2.at[here], core)

        def feed(s, i):
            at = rows(s * H, H, H)
            for f in range(FF // 256):
                cols = slice(f * 256, (f + 1) * 256)
                hidden = dot_nn(m.n2[at, :], m.wup[:, cols])
                grad = dot_nt(m.cot[at, :], m.wdn[cols, :])
                square = hidden * hidden
                bent = jnp.tanh(ROOT * hidden * (1.0 + 0.044715 * square))
                gate = 0.5 * (1.0 + bent)
                m.act[at, cols] = (hidden * gate).astype(BF)
                slope = gate + (0.5 * ROOT) * hidden * (1.0 - bent * bent) * (
                    1.0 + (3 * 0.044715) * square
                )
                m.gh[at, cols] = (grad * slope).astype(BF)
            m.gp[i] = dot_nt(m.gh[at, :], m.wup[...]).astype(BF)

        C_GP = counter[0]
        counter[0] += 2
        C_N2 = counter[0]
        counter[0] += 1
        gp_copies = [
            link(m.gp.at[2 * j + 1], m.rsc2.at[j], core, C_GP + j, C_GP + j) for j in range(2)
        ]
        part = m.n2.at[rows(t2 * H, H, H)]
        n2_fwd = link(part, part, core, C_N2, C_N2)
        pending.append(n2_fwd)
        pending.extend(gp_copies)

        def feed_step(i, _):
            a, e = lax.div(i, 2), lax.rem(i, 2)
            s = 2 * (y + a - 2 * y * a) + (c + e - 2 * c * e)

            @pl.when(i == 1)
            def _():
                n2_core.wait_recv()

            @pl.when(i == 2)
            def _():
                n2_y.wait_recv()
                n2_fwd.start()
                cot_fwd.wait_recv()

            @pl.when(i == 3)
            def _():
                n2_fwd.wait_recv()

            feed(s, i)

            @pl.when(i == 1)
            def _():
                gp_copies[0].start()

            @pl.when(i == 3)
            def _():
                gp_copies[1].start()

            return 0

        lax.fori_loop(0, 4, feed_step, 0)
        gp_copies[1].wait_recv()
        add_rows(m.ysnd2, (m.gp.at[2], m.rsc2.at[1]), H)
        gp_y = send(m.ysnd2, m.rsy2, ydev)

        is_mid = (d == half_n - 1) | (d == half_n)
        is_end = (d == 0) | (d == N - 1)
        side = jnp.where(d < half_n, 0, 1)
        step_in = 1 - 2 * side
        inner = (x, lax.rem(d + step_in + N, N), t)
        outer = (x, lax.rem(d - step_in + N, N), t)

        def piece(ref, p):
            return ref.at[rows(p * PIECE, PIECE, 16)]

        def in_copy(p):
            return link(piece(m.gsrc, p), piece(res, p), inner, S_SRC + p, R_A + p)

        def mid_copy(p):
            to = piece(m.gb, lax.div(p, 2))
            return link(piece(m.gsrc, p), to, inner, S_SRC + p, R_B + p)

        def x_copy(p):
            to = piece(m.gc, lax.div(p, 2))
            return link(piece(m.gsrc, p), to, xdev, S_SRC + p, R_C + p)

        def part_copy(p):
            return link(piece(res, p), piece(res, p), inner, S_PART + p, R_RES + p)

        def out_copy(p):
            return link(piece(res, p), piece(res, p), outer, S_OUT + p, R_RES + p)

        def gather_piece(out, p, ref, q):
            def step(i, _):
                at = rows(p * PIECE + i * 32, 32, 16)
                other = ref[rows(q * PIECE + i * 32, 32, 16), :].astype(F32)
                out[at, :] = (m.gsrc[at, :].astype(F32) + other).astype(BF)
                return 0

            lax.fori_loop(0, PIECE // 32, step, 0)

        def valid(p):
            return (p >= 0) & (p < PIECES)

        def owns(p):
            return is_mid & (side == lax.rem(p + 2 * PIECES, 2))

        def serve(s):
            @pl.when(valid(s) & jnp.logical_not(is_mid))
            def _():
                if N > 4:

                    @pl.when(jnp.logical_not(is_end))
                    def _():
                        in_copy(s).wait_recv()
                        gather_piece(m.gsrc, s, res, s)

                in_copy(s).start()

            p2 = s - 2

            @pl.when(valid(p2) & is_mid)
            def _():
                @pl.when(jnp.logical_not(is_end))
                def _():
                    in_copy(p2).wait_recv()
                    gather_piece(m.gsrc, p2, res, p2)

                @pl.when(jnp.logical_not(owns(p2)))
                def _():
                    mid_copy(p2).start()

            p3 = s - 4

            @pl.when(valid(p3) & owns(p3))
            def _():
                mid_copy(p3).wait_recv()
                gather_piece(m.gsrc, p3, m.gb, lax.div(p3, 2))
                x_copy(p3).start()

            p4 = s - 6

            @pl.when(valid(p4) & owns(p4))
            def _():
                x_copy(p4).wait_recv()
                gather_piece(res, p4, m.gc, lax.div(p4, 2))
                part_copy(p4).start()

                @pl.when(jnp.logical_not(is_end))
                def _():
                    out_copy(p4).start()

            p5 = s - 8

            @pl.when(valid(p5) & is_mid & jnp.logical_not(owns(p5)))
            def _():
                part_copy(p5).wait_recv()

                @pl.when(jnp.logical_not(is_end))
                def _():
                    out_copy(p5).start()

            if N > 4:
                p6 = s - 10

                @pl.when(valid(p6) & jnp.logical_not(is_mid) & jnp.logical_not(is_end))
                def _():
                    part_copy(p6).wait_recv()
                    out_copy(p6).start()

        def serve_all_sent():
            def step(p, _):
                @pl.when(is_end & jnp.logical_not(is_mid))
                def _():
                    part_copy(p).wait_recv()

                in_copy(p).wait_send()

                @pl.when(owns(p))
                def _():
                    part_copy(p).wait_send()

                @pl.when(jnp.logical_not(is_end))
                def _():
                    out_copy(p).wait_send()

                return 0

            lax.fori_loop(0, PIECES, step, 0)

        def down_step(f, _):
            at = pl.ds(pl.multiple_of(f * 256, 256), 256)
            m.gsrc[rows(DOWN + f * 256, 256, 16), :] = dot_tn(m.act[:, at], m.cot[...]).astype(BF)
            return 0

        def up_step(f, _):
            at = pl.ds(pl.multiple_of(f * 256, 256), 256)
            m.gsrc[rows(UP + f * 256, 256, 16), :] = dot_tn(m.n2[:, at], m.gh[...]).astype(BF)
            return 0

        lax.fori_loop(0, FF // 256, down_step, 0)
        serve(0)

        gp_copies[0].wait_recv()
        gp_y.wait_recv()

        def grad_middle_step(i, gain):
            at = rows(i * 64, 64, 64)
            grad = m.gp[0, at, :].astype(F32) + m.rsc2[0, at, :].astype(F32)
            grad = grad + m.rsy2[at, :].astype(F32)
            full, r = full_of(m.mid[at, :].astype(F32))
            back = crms_back(grad, full, r, m.gbuf[1, :1, :])
            mine = rows(t * H + i * 64, 64, 64)
            m.gm[mine, :] = (m.cot[mine, :].astype(F32) + back).astype(BF)
            return gain + jnp.sum(grad * full * r, axis=0, keepdims=True)

        gain_two = lax.fori_loop(0, H // 64, grad_middle_step, jnp.zeros((1, D), F32))
        m.sm[0, 1:2, :] = gain_two
        gm_y = send(m.gm.at[here], m.gm.at[here], ydev)
        gm_core = send(m.gm.at[here], m.gm.at[here], core)
        gm_x = link(m.gm.at[here], m.gother, xdev)

        @pl.when(x == 1)
        def _():
            gm_x.start()

        lax.fori_loop(0, D // 256, up_step, 0)
        serve(1)

        def mlp_step(i, _):
            a, e = lax.div(i, 2), lax.rem(i, 2)
            s = 2 * (y + a - 2 * y * a) + (c + e - 2 * c * e)
            m.proj[i] = dot_nn(m.act[rows(s * H, H, H), :], m.wdn[...]).astype(BF)
            return 0

        proj_copy(c).wait_send()
        proj_copy(2 + c).wait_send()
        lax.fori_loop(0, 4, mlp_step, 0)
        mp_copies = [send(m.proj.at[2 * j + 1], m.rsc.at[j], core) for j in range(2)]
        serve(2)
        gm_y.wait_recv()
        part = m.gm.at[rows(t2 * H, H, H)]
        gm_fwd = send(part, part, core)
        mp_copies[1].wait_recv()
        y_proj.wait_send()
        add_rows(m.ysnd, (m.proj.at[2], m.rsc.at[1]), H)
        mp_y = send(m.ysnd, m.rsy, ydev)
        gm_core.wait_recv()
        gm_fwd.wait_recv()

        m.gsrc[OUT : OUT + AW, :] = dot_tn(m.att[...], m.gm[...]).astype(BF)
        m.dkt[...] = jnp.zeros_like(m.dkt)
        m.dvt[...] = jnp.zeros_like(m.dvt)
        m.gq[...] = jnp.zeros_like(m.gq)

        C_GN = counter[0]
        counter[0] += 2

        def pair_rows(j):
            return rows(j * R, R, R)

        def gn_copy(j):
            return link(m.gh.at[pair_rows(j)], m.rscf.at[j], core, C_GN + j, C_GN + j)

        C_YF = counter[0]
        counter[0] += 4
        chunk = R // 4

        def yf_copy(k):
            src = m.act.at[rows((1 - y) * R + k * chunk, chunk, chunk)]
            dst = m.rsyf.at[rows(k * chunk, chunk, chunk)]
            return link(src, dst, ydev, C_YF + k, C_YF + k)

        def send_far():
            gn_copy(1 - y).wait_recv()

            def step(k, _):
                def inside(i, _):
                    r0 = k * chunk + i * 64
                    at = rows((1 - y) * R + r0, 64, 64)
                    both = m.act[at, :].astype(F32) + m.rscf[1 - y, rows(r0, 64, 64), :].astype(F32)
                    m.act[at, :] = both.astype(BF)
                    return 0

                lax.fori_loop(0, chunk // 64, inside, 0)
                yf_copy(k).start()
                return 0

            lax.fori_loop(0, 4, step, 0)

        far_step = 3 - (2 * (1 - y) + c)

        def back_block(i, _):
            b = 3 - i
            at = rows(b * H, H, H)
            mine = rows(b * R + xh, H, H)
            grad_att = dot_nt(m.gm[at, :], m.wao[...])
            outs, offs, out_ts, q_ts = [], [], [], []
            for h in range(NH):
                cols = slice(h * HS, (h + 1) * HS)
                inverse = m.il[h, at, :]
                out = grad_att[:, cols].astype(BF).astype(F32)
                delta = total(out * m.att[at, cols].astype(F32))
                offs.append(delta * inverse)
                out = (out * inverse).astype(BF)
                outs.append(out)
                out_ts.append(jnp.transpose(out))
                q_ts.append(jnp.transpose(m.q[h, mine, :]))

            def keys(kb, grads):
                new = []
                for h in range(NH):
                    e = m.e[unit(b, kb) * NH + h]
                    at_k = rows(kb * R, R, R)
                    dp = dot_nt(outs[h], m.v[h, at_k, :])
                    ds = (e.astype(F32) * (dp - offs[h])).astype(BF)
                    new.append(grads[h] + dot_nn(ds, m.k[h, at_k, :]))
                    m.dkt[kb, h] += dot_nn(q_ts[h], ds)
                    m.dvt[kb, h] += dot_nn(out_ts[h], e)
                serve(3 + 4 * i - lax.div(i * (i - 1), 2) + kb)
                return tuple(new)

            grads = lax.fori_loop(0, b + 1, keys, (jnp.zeros((H, HS), F32),) * NH)
            for h in range(NH):
                base = 3 * h * HS
                grad_q = jnp.transpose(grads[h] * HS**-0.5).astype(BF)
                m.dmt[base : base + HS, rows(xh, H, H)] = grad_q
                m.dmt[base : base + HS, rows(oh, H, H)] = jnp.zeros((HS, H), BF)
                m.dmt[base + HS : base + 2 * HS, :] = m.dkt[b, h].astype(BF)
                m.dmt[base + 2 * HS : base + 3 * HS, :] = m.dvt[b, h].astype(BF)
            n1_rows = rows(b * R, R, R)
            m.gq[...] += dot_nn(m.dmt[...], m.n1[n1_rows, :])
            back = dot_nn(jnp.transpose(m.dmt[...]), m.wqkv[...]).astype(BF)
            j = lax.div(b, 2)

            @pl.when(lax.rem(b, 2) == c)
            def _():
                m.act[pair_rows(j), :] = back

            @pl.when(lax.rem(b, 2) != c)
            def _():
                m.gh[pair_rows(j), :] = back
                gn_copy(j).start()

            @pl.when(i == far_step + 1)
            def _():
                send_far()

            return 0

        lax.fori_loop(0, 4, back_block, 0)
        pl.when(far_step == 3)(send_far)
        m.gsrc[QKV : QKV + QW, :] = m.gq[...].astype(BF)
        served = 13

        mp_copies[0].wait_recv()
        mp_y.wait_recv()
        n2_y.wait_send()
        n2_core.wait_send()
        add_rows(m.n2.at[here], (m.mid, m.proj.at[0], m.rsc.at[0], m.rsy), H)
        bo_x = link(m.n2.at[here], m.gother, xdev)

        @pl.when(x == 0)
        def _():
            bo_x.start()

        lax.fori_loop(served, 18, lambda s, _: (serve(s), 0)[1], 0)

        gn_copy(y).wait_recv()

        C_XF = counter[0]
        counter[0] += 4

        def xf_copy(k):
            src = m.act.at[rows(y * R + k * chunk, chunk, chunk)]
            dst = m.rsxf.at[rows(k * chunk, chunk, chunk)]
            return link(src, dst, xdev, C_XF + k, C_XF + k)

        def near_sum(k):
            yf_copy(k).wait_recv()

            def inside(i, _):
                r0 = k * chunk + i * 64
                at = rows(y * R + r0, 64, 64)
                here_rows = rows(r0, 64, 64)
                both = m.act[at, :].astype(F32) + m.rscf[y, here_rows, :].astype(F32)
                m.act[at, :] = (both + m.rsyf[here_rows, :].astype(F32)).astype(BF)
                return 0

            lax.fori_loop(0, chunk // 64, inside, 0)

        @pl.when(x == 1)
        def _():
            def step(k, _):
                near_sum(k)
                xf_copy(k).start()
                return 0

            lax.fori_loop(0, 4, step, 0)

        @pl.when(x == 0)
        def _():
            gm_x.wait_recv()
            m.sm[0, 0:1, :] = jnp.zeros((1, D), F32)

            def step(k, _):
                near_sum(k)
                xf_copy(k).wait_recv()

                def inside(i, gain):
                    r0 = k * chunk + i * 64
                    here_rows = rows(r0, 64, 64)
                    grad = m.act[rows(y * R + r0, 64, 64), :].astype(F32)
                    grad = grad + m.rsxf[here_rows, :].astype(F32)
                    full, r = full_of(m.sp[here_rows, :].astype(F32))
                    back = crms_back(grad, full, r, m.gbuf[0, :1, :])
                    m.rsyf[here_rows, :] = back.astype(BF)
                    return gain + jnp.sum(grad * full * r, axis=0, keepdims=True)

                gain = lax.fori_loop(0, chunk // 64, inside, jnp.zeros((1, D), F32))
                m.sm[0, 0:1, :] += gain
                return 0

            lax.fori_loop(0, 4, step, 0)

            def out_step(i, _):
                at = rows(i * 64, 64, 64)
                one = m.gm[rows(t * H + i * 64, 64, 64), :].astype(F32) + m.rsyf[at, :].astype(F32)
                o_io[0, at, :] = one[:, :C].astype(BF)
                below = rows(H + i * 64, 64, 64)
                two = m.gother[at, :].astype(F32) + m.rsyf[below, :].astype(F32)
                o_io[0, below, :] = two[:, :C].astype(BF)
                return 0

            lax.fori_loop(0, H // 64, out_step, 0)

        @pl.when(x == 1)
        def _():
            bo_x.wait_recv()
            o_io[0, 0:H, :] = m.gother[:, :C]
            o_io[0, H:R, :] = m.n2[here, :C]

        for j, peer in enumerate((core, ydev, xdev)):
            copy = send(m.sm.at[j], m.smr.at[j], peer)
            copy.wait_recv()
            m.sm[j + 1] = m.sm[j] + m.smr[j]
        z_copies = []
        for j in range(1, N):
            z_copies.append(send(m.sm.at[3], m.smz.at[j], (x, lax.rem(d + j, N), t)))
        lax.fori_loop(18, PIECES + 12, lambda s, _: (serve(s), 0)[1], 0)
        everything = m.sm[3]
        for j in range(1, N):
            z_copies[j - 1].wait_recv()
            everything = everything + m.smz[j]
        o_sm[...] = jnp.zeros_like(o_sm)

        @pl.when(x == 0)
        def _():
            o_sm[0:1, :] = everything[0:1]

        @pl.when(x == 1)
        def _():
            o_sm[0:1, :] = everything[1:2]

        o_sm[1:2, :] = jnp.broadcast_to(
            jnp.sqrt(total(everything[2:3]) * (1.0 / (4 * R * N * D))), (1, D)
        )

        serve_all_sent()
        waited = {id(n2_y), id(n2_core), id(y_proj)}
        for copy in pending:
            if id(copy) not in waited:
                copy.wait_send()
        for j in range(2):
            gn_copy(j).wait_send()
        for k in range(4):
            yf_copy(k).wait_send()

        @pl.when(x == 1)
        def _():
            gm_x.wait_send()
            for k in range(4):
                xf_copy(k).wait_send()

        @pl.when(x == 0)
        def _():
            bo_x.wait_send()

        assert counter[0] <= N_SEM

    return body, scratch_shapes, PIECES * PIECE, (DOWN, UP, OUT, QKV)


def per_device(mesh):
    N = mesh.shape["dp"]
    assert mesh.shape["blk"] == 2 and mesh.shape["tensor"] == 4 and N % 2 == 0

    def run(stream_in, lengths, norm_gains, w_qkv, w_attn_out, w_up, w_down, cotangent):
        R, C = stream_in.shape
        D = norm_gains.shape[1]
        FF = w_up.shape[1]
        NH = w_qkv.shape[1] // (3 * HS)
        body, scratch, grad_rows, (DOWN, UP, OUT, QKV) = kernel_for(
            dict(R=R, H=R // 2, D=D, C=C, FF=FF, NH=NH, N=N)
        )
        vmem = pl.BlockSpec(memory_space=pltpu.VMEM)
        smem = pl.BlockSpec(memory_space=pltpu.SMEM)
        anywhere = pl.BlockSpec(memory_space=pl.ANY)
        block_io, grads, small = pl.pallas_call(
            body,
            out_shape=(
                jax.ShapeDtypeStruct((1, R, C), BF),
                jax.ShapeDtypeStruct((grad_rows, D), BF),
                jax.ShapeDtypeStruct((8, D), F32),
            ),
            in_specs=[smem, vmem] + [anywhere] * 6,
            out_specs=(vmem,) * 3,
            scratch_shapes=scratch,
            compiler_params=pltpu.CompilerParams(
                collective_id=0, has_side_effects=True, vmem_limit_bytes=62 << 20
            ),
        )(lengths, norm_gains, stream_in, cotangent, w_qkv.T, w_attn_out, w_up, w_down)

        def spread(io_in, down_in, up_in, out_in, qkv_in, small_in, io, gain, qkv, out, up, down, rms):
            io[...] = io_in[...]
            down[...] = down_in[:, :C].astype(F32)
            up[...] = up_in[...].astype(F32)
            out[...] = out_in[:, :C].astype(F32)
            qkv[...] = qkv_in[...].astype(F32)
            gain[...] = small_in[0:1, :]
            rms[0, 0] = jnp.max(small_in[1:2, :])

        steps = 6
        QW, AW = grad_rows - QKV, QKV - OUT
        sizes = (FF // steps, D // steps, AW // steps, QW // steps)
        firsts = (DOWN, UP, OUT, QKV)
        piece_specs = [
            pl.BlockSpec((n, D), lambda i, o=first // n: (o + i, 0))
            for n, first in zip(sizes, firsts, strict=True)
        ]
        io_spec = pl.BlockSpec((1, R // 4, C), lambda i: (0, jnp.minimum(i, 3), 0))
        whole = lambda i: (0, 0)
        block_io, gain, grad_qkv, grad_out, grad_up, grad_down, rms = pl.pallas_call(
            spread,
            grid=(steps,),
            out_shape=(
                jax.ShapeDtypeStruct((1, R, C), BF),
                jax.ShapeDtypeStruct((1, D), F32),
                jax.ShapeDtypeStruct((QW, D), F32),
                jax.ShapeDtypeStruct((AW, C), F32),
                jax.ShapeDtypeStruct((D, FF), F32),
                jax.ShapeDtypeStruct((FF, C), F32),
                jax.ShapeDtypeStruct((1, 1), F32),
            ),
            in_specs=[io_spec, *piece_specs, pl.BlockSpec((8, D), whole)],
            out_specs=(
                io_spec,
                pl.BlockSpec((1, D), whole),
                pl.BlockSpec((sizes[3], D), lambda i: (i, 0)),
                pl.BlockSpec((sizes[2], C), lambda i: (i, 0)),
                pl.BlockSpec((sizes[1], FF), lambda i: (i, 0)),
                pl.BlockSpec((sizes[0], C), lambda i: (i, 0)),
                smem,
            ),
        )(block_io, grads, grads, grads, grads, small)
        return (block_io, gain, grad_qkv.T, grad_out, grad_up, grad_down, rms.reshape(()))

    return run


def solution(mesh):
    in_specs = (
        P(("dp", "tensor"), None),
        P("dp"),
        P("blk", None),
        P(None, "tensor"),
        P("tensor", None),
        P(None, "tensor"),
        P("tensor", None),
        P(("dp", "tensor"), None),
    )
    out_specs = (
        P("blk", ("dp", "tensor"), None),
        P("blk", None),
        P(None, "tensor"),
        P("tensor", None),
        P(None, "tensor"),
        P("tensor", None),
        P(),
    )
    return jax.shard_map(
        per_device(mesh), mesh=mesh, in_specs=in_specs, out_specs=out_specs, check_vma=False
    )
```

```python
from types import SimpleNamespace

import jax
import jax.numpy as jnp
from jax import lax
from jax.experimental import pallas as pl
from jax.experimental.pallas import tpu as pltpu
from jax.sharding import PartitionSpec as P

HS = 64
EPSILON = 1e-05
MASKED = -1e30
BF = jnp.bfloat16
F32 = jnp.float32
MESH = pl.DeviceIdType.MESH
SUB = 48
LAG = 2
BEFORE = (1, 2, 1, 1, 2)
UNIT, BLOCK = 0, 1
ROOT = 0.7978845608028654


def dot_nn(a, b):
    return jnp.dot(a, b, preferred_element_type=F32)


def dot_nt(a, b):
    return lax.dot_general(a, b, (((1,), (1,)), ((), ())), preferred_element_type=F32)


def dot_tn(a, b):
    return lax.dot_general(a, b, (((0,), (0,)), ((), ())), preferred_element_type=F32)


def rows(start, count, multiple):
    return pl.ds(pl.multiple_of(start, multiple), count)


def lane_groups(value):
    return [value[:, i : i + 128] for i in range(0, value.shape[1], 128)]


def kernel_for(sizes):
    R, H, D, C, FF, NH, N = (sizes[k] for k in ("R", "H", "D", "C", "FF", "NH", "N"))
    QW = NH * 3 * HS
    AW = NH * HS
    GRADS = 2 * D + AW + QW
    GROUPS = GRADS // (3 * SUB)
    DOWN, UP, OUT, QKV = 0, FF, FF + D, FF + D + AW
    half_n = N // 2

    names = {}

    def scratch(name, shape, dtype):
        names[name] = pltpu.VMEM(shape, dtype)

    scratch("gbuf", (2, 8, D), F32)
    scratch("stream", (R, C), BF)
    scratch("cot_in", (H, C), BF)
    scratch("wqkv", (QW, D), BF)
    scratch("wao_in", (AW, C), BF)
    scratch("wup", (D, FF), BF)
    scratch("wdn_in", (FF, C), BF)
    scratch("normed", (4 * R, D), BF)
    scratch("wao", (AW, D), BF)
    scratch("wdn", (FF, D), BF)
    scratch("n1", (4 * R, D), BF)
    scratch("q", (NH, 4 * R, HS), BF)
    scratch("k", (NH, 4 * R, HS), BF)
    scratch("v", (NH, 4 * R, HS), BF)
    scratch("e", (10 * NH, H, R), BF)
    scratch("il", (4 * H, 128), F32)
    scratch("att", (4 * H, AW), BF)
    scratch("proj", (4, H, D), BF)
    scratch("rsc", (2, H, D), BF)
    scratch("ysnd", (H, D), BF)
    scratch("rsy", (H, D), BF)
    scratch("mid", (H, D), BF)
    scratch("n2", (4 * H, D), BF)
    scratch("cot", (4 * H, D), BF)
    scratch("act", (4 * H, FF), BF)
    scratch("gh", (4 * H, FF), BF)
    scratch("gp", (4, H, D), BF)
    scratch("rsc2", (2, H, D), BF)
    scratch("ysnd2", (H, D), BF)
    scratch("rsy2", (H, D), BF)
    scratch("gm", (4 * H, D), BF)
    scratch("gother", (H, D), BF)
    scratch("dmt", (QW, R), BF)
    scratch("dkt", (4, NH, HS, R), F32)
    scratch("dvt", (4, NH, HS, R), F32)
    scratch("gq", (QW, D), F32)
    scratch("rscf", (2, R, D), BF)
    scratch("rsyf", (R, D), BF)
    scratch("rsxf", (R, D), BF)
    scratch("gsrc", (GRADS, D), BF)
    scratch("gb", ((GROUPS + -(-GROUPS // 4)) * SUB, D), BF)
    scratch("gc", ((GROUPS + -(-GROUPS // 2)) * SUB, D), BF)
    scratch("sm", (5, 8, D), F32)
    scratch("smr", (3, 8, D), F32)
    scratch("smz", (N, 8, D), F32)
    n_vmem = len(names)
    N_SEM = 10 * GROUPS + 64 + N
    scratch_shapes = list(names.values()) + [
        pltpu.SemaphoreType.DMA((N_SEM,)),
        pltpu.SemaphoreType.DMA((N_SEM,)),
        pltpu.SemaphoreType.DMA((6,)),
    ]

    def body(
        lens, gains, stream, cot_in, w_qkv, w_ao, w_up, w_dn, o_io, o_gr, o_sm, *refs
    ):
        m = SimpleNamespace(**dict(zip(names, refs[:n_vmem], strict=True)))
        ssem, rsem, lsem = refs[n_vmem:]
        res = o_gr
        x = lax.axis_index("blk")
        d = lax.axis_index("dp")
        t = lax.axis_index("tensor")
        y = lax.div(t, 2)
        c = lax.rem(t, 2)
        t1 = 2 * y + 1 - c
        t2 = 2 * (1 - y) + c
        t3 = 2 * (1 - y) + 1 - c
        core, ydev, xdev = (x, d, t1), (x, d, t2), (1 - x, d, t)
        xh, oh = x * H, (1 - x) * H

        counter = [10 * GROUPS]
        pending = []

        def link(src, dst, dev, s_idx=None, r_idx=None):
            if s_idx is None:
                s_idx = r_idx = counter[0]
                counter[0] += 1
            return pltpu.make_async_remote_copy(
                src_ref=src,
                dst_ref=dst,
                send_sem=ssem.at[s_idx],
                recv_sem=rsem.at[r_idx],
                device_id=dev,
                device_id_type=MESH,
            )

        def send(src, dst, dev):
            copy = link(src, dst, dev)
            copy.start()
            pending.append(copy)
            return copy

        loads = []
        for i, (src, dst) in enumerate(
            (
                (stream, m.stream),
                (w_qkv, m.wqkv),
                (cot_in.at[rows(xh, H, H)], m.cot_in),
                (w_ao, m.wao_in),
                (w_up, m.wup),
                (w_dn, m.wdn_in),
            )
        ):
            loads.append(pltpu.make_async_copy(src, dst, lsem.at[i]))
            loads[-1].start()

        barrier = pltpu.get_barrier_semaphore()
        for peer in (core, ydev, xdev):
            pl.semaphore_signal(barrier, inc=1, device_id=peer, device_id_type=MESH)
        for j in range(1, N):
            pl.semaphore_signal(
                barrier,
                inc=1,
                device_id=(x, lax.rem(d + j, N), t),
                device_id_type=MESH,
            )
        pl.semaphore_wait(barrier, 3 + N - 1)

        lane = lax.broadcasted_iota(jnp.int32, (1, D), 1)
        last = lane == D - 1

        def total(value):
            return jnp.sum(value, axis=1, keepdims=True)

        def full_of(stream_rows):
            full = jnp.where(last, -total(stream_rows), stream_rows)
            return full, lax.rsqrt(total(full * full) * (1.0 / D) + EPSILON)

        def crms_back(grad, full, r, gain):
            a = grad * gain
            mean = total(a * full) * (1.0 / D)
            df = r * (a - full * (r * r * mean))
            tail = total(jnp.where(last, df, 0.0))
            return jnp.where(last, 0.0, df - tail)

        m.gbuf[x] = jnp.broadcast_to(gains[...], (8, D))
        gain_copy = send(m.gbuf.at[x], m.gbuf.at[x], xdev)
        loads[0].wait()
        own_rows = rows(t * R, R, R)
        m.n1[own_rows, D - 128 :] = jnp.zeros((R, 128), BF)
        m.n1[own_rows, :C] = m.stream[...]
        here = rows(t * H, H, H)

        half = H // 4
        y_copies = []
        for k in range(4):
            part = m.n1.at[rows(t * R + xh + k * half, half, half)]
            y_copies.append(send(part, part, ydev))
        part = m.n1.at[rows(t * R, R, R)]
        own_copy = send(part, part, core)
        loads[2].wait()
        m.cot[here, D - 128 :] = jnp.zeros((H, 128), BF)
        m.cot[here, :C] = m.cot_in[...]
        part = m.cot.at[here]
        cot_core = send(part, part, core)

        def qkv_rows(start):
            def step(i, _):
                some = rows(start + i * 64, 64, 64)
                full, r = full_of(m.n1[some, :].astype(F32))
                m.normed[some, :] = (full * r * m.gbuf[0, :1, :]).astype(BF)
                return 0

            lax.fori_loop(0, H // 64, step, 0)
            mixed = dot_nt(m.normed[rows(start, H, H), :], m.wqkv[...])
            at = rows(start, H, H)
            for h in range(NH):
                for p, ref in enumerate((m.q, m.k, m.v)):
                    part = mixed[:, (3 * h + p) * HS : (3 * h + p + 1) * HS]
                    if p == 0:
                        part = part * HS**-0.5
                    ref[h, at, :] = part.astype(BF)

        def qkv_block(block):
            lax.fori_loop(0, 2, lambda i, _: (qkv_rows(block * R + i * H), 0)[1], 0)

        loads[1].wait()
        gain_copy.wait_recv()
        qkv_block(t)
        own_copy.wait_recv()
        qkv_block(t1)
        for load in loads[3:]:
            load.wait()
        m.wao[:, D - 128 :] = jnp.zeros((AW, 128), BF)
        m.wao[:, :C] = m.wao_in[...]
        m.wdn[:, D - 128 :] = jnp.zeros((FF, 128), BF)
        m.wdn[:, :C] = m.wdn_in[...]
        fwd = []
        x_copies = []
        for k in range(4):
            y_copies[k].wait_recv()
            part = m.n1.at[rows(t2 * R + xh + k * half, half, half)]
            x_copies.append(send(part, part, xdev))
            fwd.append(send(part, part, core))
        part = m.cot.at[here]
        cot_y = send(part, part, ydev)
        for k in range(4):
            x_copies[k].wait_recv()
            part = m.n1.at[rows(t2 * R + oh + k * half, half, half)]
            fwd.append(send(part, part, core))
        qkv_block(t2)
        for copy in fwd:
            copy.wait_recv()
        qkv_block(t3)

        ends = [lens[0]]
        for i in range(1, 4):
            ends.append(ends[-1] + lens[i])

        def bias_of(b, kb):
            cut = (ends[0] > kb * R) & (ends[0] <= b * R)
            for e in ends[1:]:
                cut = cut | ((e > kb * R) & (e <= b * R))
            return jnp.where(cut, MASKED, 0.0).astype(F32)

        row_at = lax.broadcasted_iota(jnp.int32, (H, R), 0)
        col_at = lax.broadcasted_iota(jnp.int32, (H, R), 1)

        def unit(b, kb):
            return lax.div(b * (b + 1), 2) + kb

        def attend(b, between):
            mine = rows(b * R + xh, H, H)
            heads = [m.q[h, mine, :] for h in range(NH)]

            def scores(h, kb):
                return dot_nt(heads[h], m.k[h, rows(kb * R, R, R), :])

            def top(s, best):
                for g in lane_groups(s):
                    best = jnp.maximum(best, g)
                return best

            def masked(s):
                return jnp.where(col_at <= row_at + xh, s, MASKED)

            def peak(kb, best):
                bias = bias_of(b, kb)
                low = jnp.full((H, 128), -jnp.inf, F32)
                return tuple(
                    jnp.maximum(best[h], top(scores(h, kb), low) + bias) for h in range(NH)
                )

            low = jnp.full((H, 128), MASKED, F32)
            best = tuple(top(masked(scores(h, b)), low) for h in range(NH))
            best = lax.fori_loop(0, b, peak, best)
            best = [jnp.max(v, axis=1, keepdims=True) for v in best]
            between()

            def weigh(h, kb, s, off, sums, acc):
                e = jnp.exp(s - off)
                for g in lane_groups(e):
                    sums = sums + g
                e = e.astype(BF)
                m.e[unit(b, kb) * NH + h] = e
                return sums, acc + dot_nn(e, m.v[h, rows(kb * R, R, R), :])

            def add(kb, carry):
                bias = bias_of(b, kb)
                return tuple(
                    weigh(h, kb, scores(h, kb), best[h] - bias, *carry[h]) for h in range(NH)
                )

            zero = (jnp.zeros((H, 128), F32), jnp.zeros((H, HS), F32))
            carry = tuple(weigh(h, b, masked(scores(h, b)), best[h], *zero) for h in range(NH))
            carry = lax.fori_loop(0, b, add, carry)
            at = rows(b * H, H, H)
            for h in range(NH):
                inverse = 1.0 / total(carry[h][0])
                m.il[at, h : h + 1] = inverse
                m.att[at, h * HS : (h + 1) * HS] = (carry[h][1] * inverse).astype(BF)
            return dot_nn(m.att[at, :], m.wao[...]).astype(BF)

        C_PROJ = counter[0]
        counter[0] += 2

        def proj_copy(i):
            j = lax.div(i, 2)
            return link(m.proj.at[i], m.rsc.at[j], core, C_PROJ + j, C_PROJ + j)

        def add_rows(out, terms, count):
            def step(i, _):
                at = rows(i * 64, 64, 64)
                out[at, :] = sum(ref[at, :].astype(F32) for ref in terms).astype(BF)
                return 0

            lax.fori_loop(0, count // 64, step, 0)

        y_proj = link(m.ysnd, m.rsy, ydev)
        pending.append(y_proj)

        def attend_step(i, _):
            a, e = lax.div(i, 2), 1 - lax.rem(i, 2)
            g = (1 - y) * (1 - a) + y * a

            def between():
                @pl.when(i == 2 - c)
                def _():
                    proj_copy(c).wait_recv()
                    add_rows(m.ysnd, (m.proj.at[1 - c], m.rsc.at[0]), H)
                    y_proj.start()

            m.proj[i] = attend(2 * g + e, between)

            @pl.when(lax.rem(i, 2) == c)
            def _():
                proj_copy(i).start()

            return 0

        lax.fori_loop(0, 4, attend_step, 0)
        proj_copy(2 + c).wait_recv()
        cot_core.wait_recv()
        cot_y.wait_recv()
        part = m.cot.at[rows(t2 * H, H, H)]
        cot_fwd = send(part, part, core)
        y_proj.wait_recv()

        def middle_step(i, squares):
            at = rows(i * 64, 64, 64)
            mid = m.n1[rows(t * R + xh + i * 64, 64, 64), :].astype(F32)
            mid = mid + m.proj[2 + 1 - c, at, :].astype(F32)
            mid = mid + m.rsc[1, at, :].astype(F32) + m.rsy[at, :].astype(F32)
            mid = mid.astype(BF)
            m.mid[at, :] = mid
            full, r = full_of(mid.astype(F32))
            m.n2[rows(t * H + i * 64, 64, 64), :] = (full * r * m.gbuf[1, :1, :]).astype(BF)
            return squares + jnp.sum(full * full, axis=0, keepdims=True)

        squares = lax.fori_loop(0, H // 64, middle_step, jnp.zeros((1, D), F32))
        m.sm[0] = jnp.zeros((8, D), F32)
        m.sm[0, 2:3, :] = squares

        n2_y = send(m.n2.at[here], m.n2.at[here], ydev)
        n2_core = send(m.n2.at[here], m.n2.at[here], core)

        def feed(s, i):
            at = rows(s * H, H, H)
            for f in range(FF // 256):
                cols = slice(f * 256, (f + 1) * 256)
                hidden = dot_nn(m.n2[at, :], m.wup[:, cols])
                grad = dot_nt(m.cot[at, :], m.wdn[cols, :])
                square = hidden * hidden
                bent = jnp.tanh(ROOT * hidden * (1.0 + 0.044715 * square))
                gate = 0.5 * (1.0 + bent)
                m.act[at, cols] = (hidden * gate).astype(BF)
                slope = gate + (0.5 * ROOT) * hidden * (1.0 - bent * bent) * (
                    1.0 + (3 * 0.044715) * square
                )
                m.gh[at, cols] = (grad * slope).astype(BF)
            m.gp[i] = dot_nt(m.gh[at, :], m.wup[...]).astype(BF)

        C_GP = counter[0]
        counter[0] += 2
        C_N2 = counter[0]
        counter[0] += 1
        gp_copies = [
            link(m.gp.at[2 * j + 1], m.rsc2.at[j], core, C_GP + j, C_GP + j) for j in range(2)
        ]
        part = m.n2.at[rows(t2 * H, H, H)]
        n2_fwd = link(part, part, core, C_N2, C_N2)
        pending.append(n2_fwd)
        pending.extend(gp_copies)

        def feed_step(i, _):
            a, e = lax.div(i, 2), lax.rem(i, 2)
            s = 2 * (y + a - 2 * y * a) + (c + e - 2 * c * e)

            @pl.when(i == 1)
            def _():
                n2_core.wait_recv()

            @pl.when(i == 2)
            def _():
                n2_y.wait_recv()
                n2_fwd.start()
                cot_fwd.wait_recv()

            @pl.when(i == 3)
            def _():
                n2_fwd.wait_recv()

            feed(s, i)

            @pl.when(i == 1)
            def _():
                gp_copies[0].start()

            @pl.when(i == 3)
            def _():
                gp_copies[1].start()

            return 0

        lax.fori_loop(0, 4, feed_step, 0)
        gp_copies[1].wait_recv()
        add_rows(m.ysnd2, (m.gp.at[2], m.rsc2.at[1]), H)
        gp_y = send(m.ysnd2, m.rsy2, ydev)

        is_mid = (d == half_n - 1) | (d == half_n)
        is_end = (d == 0) | (d == N - 1)
        side = jnp.where(d < half_n, 0, 1)
        step_in = 1 - 2 * side
        inner = (x, lax.rem(d + step_in + N, N), t)
        outer = (x, lax.rem(d - step_in + N, N), t)

        not_end = jnp.logical_not(is_end)

        def sub_rows(ref, at, count):
            return ref.at[rows(at, count * SUB, 16)]

        def group_at(g):
            return g * (3 * SUB)

        def third_at(g):
            return group_at(g) + 2 * SUB

        def sub_at(g, who):
            return group_at(g) + who * SUB

        def sem(kind, g):
            return kind * GROUPS + g

        def in_copy(g):
            at = group_at(g)
            return link(sub_rows(m.gsrc, at, 2), sub_rows(res, at, 2), inner, sem(0, g), sem(0, g))

        def mid_copy(g):
            src = sub_rows(m.gsrc, sub_at(g, 1 - side), 1)
            return link(src, sub_rows(m.gb, g * SUB, 1), inner, sem(1, g), sem(1, g))

        def blk_copy(g):
            src = sub_rows(m.gsrc, sub_at(g, side), 1)
            return link(src, sub_rows(m.gc, g * SUB, 1), xdev, sem(2, g), sem(2, g))

        def res_link(g, who, dev, kind):
            at = sub_rows(res, sub_at(g, who), 1)
            return link(at, at, dev, sem(kind, g), sem(3, g) + GROUPS * who)

        def own_part(g):
            return res_link(g, side, inner, 3)

        def own_out(g):
            return res_link(g, side, outer, 4)

        def other_part(g):
            return res_link(g, 1 - side, inner, 3)

        def other_out(g):
            return res_link(g, 1 - side, outer, 5)

        def c_link(dst, dev, kind):
            def make(g):
                src = sub_rows(m.gsrc, third_at(g), 1)
                return link(src, dst(g), dev, sem(6, g), sem(kind, g))

            return make

        def c_res(dev, kind):
            def make(g):
                at = sub_rows(res, third_at(g), 1)
                return link(at, at, dev, sem(kind, g), sem(8, g))

            return make

        c_blk = c_link(lambda g: sub_rows(m.gc, (GROUPS + lax.div(g, 2)) * SUB, 1), xdev, 5)
        c_in = c_link(lambda g: sub_rows(res, third_at(g), 1), inner, 6)
        c_mid = c_link(lambda g: sub_rows(m.gb, (GROUPS + lax.div(g, 4)) * SUB, 1), inner, 7)
        c_part, c_out, c_back = c_res(inner, 7), c_res(outer, 8), c_res(xdev, 9)

        def add(out, at, other, count):
            for k in range(count):
                here_rows = rows(at + k * SUB, SUB, 16)
                there = other[k * SUB : (k + 1) * SUB, :].astype(F32)
                out[here_rows, :] = (m.gsrc[here_rows, :].astype(F32) + there).astype(BF)

        def valid(g):
            return (g >= 0) & (g < GROUPS)

        def mine(g):
            return x == lax.rem(g + 2 * GROUPS, 2)

        def late_owns(g):
            return side == lax.rem(lax.div(g + 4 * GROUPS, 2), 2)

        def serve(s):
            g1, g2, g3, g4, g5, g6 = (s - i * LAG for i in range(6))

            @pl.when(valid(g1) & jnp.logical_not(mine(g1)))
            def _():
                c_blk(g1).start()

            @pl.when(jnp.logical_not(is_mid))
            def _():
                @pl.when(valid(g1))
                def _():
                    if N > 4:

                        @pl.when(not_end)
                        def _():
                            in_copy(g1).wait_recv()
                            add(m.gsrc, group_at(g1), sub_rows(res, group_at(g1), 2), 2)

                    in_copy(g1).start()

                @pl.when(valid(g2) & mine(g2))
                def _():
                    c_blk(g2).wait_recv()
                    add(m.gsrc, third_at(g2), sub_rows(m.gc, (GROUPS + lax.div(g2, 2)) * SUB, 1), 1)
                    if N > 4:

                        @pl.when(not_end)
                        def _():
                            c_in(g2).wait_recv()
                            add(m.gsrc, third_at(g2), sub_rows(res, third_at(g2), 1), 1)

                    c_in(g2).start()

                @pl.when(valid(g6))
                def _():
                    if N > 4:

                        @pl.when(not_end)
                        def _():
                            own_out(g6).wait_recv()
                            own_out(g6).start()
                            other_out(g6).wait_recv()
                            other_out(g6).start()

                    @pl.when(mine(g6))
                    def _():
                        c_part(g6).wait_recv()
                        c_back(g6).start()
                        if N > 4:

                            @pl.when(not_end)
                            def _():
                                c_out(g6).start()

            @pl.when(is_mid)
            def _():
                @pl.when(valid(g2))
                def _():
                    if N > 2:

                        @pl.when(not_end)
                        def _():
                            in_copy(g2).wait_recv()
                            add(m.gsrc, group_at(g2), sub_rows(res, group_at(g2), 2), 2)

                    mid_copy(g2).start()

                    @pl.when(mine(g2))
                    def _():
                        c_blk(g2).wait_recv()
                        add(m.gsrc, third_at(g2), sub_rows(m.gc, (GROUPS + lax.div(g2, 2)) * SUB, 1), 1)

                @pl.when(valid(g3))
                def _():
                    mid_copy(g3).wait_recv()
                    add(m.gsrc, sub_at(g3, side), sub_rows(m.gb, g3 * SUB, 1), 1)
                    blk_copy(g3).start()

                    @pl.when(mine(g3))
                    def _():
                        if N > 2:

                            @pl.when(not_end)
                            def _():
                                c_in(g3).wait_recv()
                                add(m.gsrc, third_at(g3), sub_rows(res, third_at(g3), 1), 1)

                        @pl.when(jnp.logical_not(late_owns(g3)))
                        def _():
                            c_mid(g3).start()

                @pl.when(valid(g4))
                def _():
                    blk_copy(g4).wait_recv()
                    add(res, sub_at(g4, side), sub_rows(m.gc, g4 * SUB, 1), 1)
                    own_part(g4).start()
                    if N > 2:

                        @pl.when(not_end)
                        def _():
                            own_out(g4).start()

                    @pl.when(mine(g4) & late_owns(g4))
                    def _():
                        c_mid(g4).wait_recv()
                        add(res, third_at(g4), sub_rows(m.gb, (GROUPS + lax.div(g4, 4)) * SUB, 1), 1)
                        c_part(g4).start()
                        c_back(g4).start()
                        if N > 2:

                            @pl.when(not_end)
                            def _():
                                c_out(g4).start()

                @pl.when(valid(g5))
                def _():
                    other_part(g5).wait_recv()
                    if N > 2:

                        @pl.when(not_end)
                        def _():
                            other_out(g5).start()

                    @pl.when(mine(g5) & jnp.logical_not(late_owns(g5)))
                    def _():
                        c_part(g5).wait_recv()
                        c_back(g5).start()
                        if N > 2:

                            @pl.when(not_end)
                            def _():
                                c_out(g5).start()

        def serve_range(begin, end):
            lax.fori_loop(begin, end, lambda s, _: (serve(s), 0)[1], 0)

        def serve_all_sent():
            def step(g, _):
                @pl.when(jnp.logical_not(is_mid))
                def _():
                    @pl.when(is_end)
                    def _():
                        own_part(g).wait_recv()
                        other_part(g).wait_recv()

                    in_copy(g).wait_send()

                @pl.when(is_mid)
                def _():
                    mid_copy(g).wait_send()
                    blk_copy(g).wait_send()
                    own_part(g).wait_send()

                @pl.when(not_end)
                def _():
                    own_out(g).wait_send()
                    other_out(g).wait_send()

                ended = mine(g) & is_mid & late_owns(g)

                @pl.when(jnp.logical_not(ended))
                def _():
                    c_in(g).wait_send()

                @pl.when(ended)
                def _():
                    c_part(g).wait_send()

                @pl.when(mine(g))
                def _():
                    c_back(g).wait_send()

                @pl.when(mine(g) & not_end)
                def _():
                    c_out(g).wait_send()

                @pl.when(jnp.logical_not(mine(g)))
                def _():
                    c_part(g).wait_recv()

                return 0

            lax.fori_loop(0, GROUPS, step, 0)

        tail = [0]

        def serve_next(count):
            serve_range(tail[0], tail[0] + count)
            tail[0] += count

        def down_step(f, _):
            at = pl.ds(pl.multiple_of(f * 256, 256), 256)
            m.gsrc[rows(DOWN + f * 256, 256, 16), :] = dot_tn(m.act[:, at], m.cot[...]).astype(BF)
            return 0

        def up_step(f, _):
            at = pl.ds(pl.multiple_of(f * 256, 256), 256)
            m.gsrc[rows(UP + f * 256, 256, 16), :] = dot_tn(m.n2[:, at], m.gh[...]).astype(BF)
            return 0

        down_step(0, 0)
        serve_next(BEFORE[0])
        down_step(1, 0)
        down_step(2, 0)
        serve_next(BEFORE[1])
        lax.fori_loop(0, D // 256, up_step, 0)
        serve_next(BEFORE[2])

        def mlp_step(i, _):
            a, e = lax.div(i, 2), lax.rem(i, 2)
            s = 2 * (y + a - 2 * y * a) + (c + e - 2 * c * e)
            m.proj[i] = dot_nn(m.act[rows(s * H, H, H), :], m.wdn[...]).astype(BF)
            return 0

        proj_copy(c).wait_send()
        proj_copy(2 + c).wait_send()
        lax.fori_loop(0, 4, mlp_step, 0)
        mp_copies = [send(m.proj.at[2 * j + 1], m.rsc.at[j], core) for j in range(2)]
        serve_next(BEFORE[3])

        gp_copies[0].wait_recv()
        gp_y.wait_recv()

        def grad_middle_step(i, gain):
            at = rows(i * 64, 64, 64)
            grad = m.gp[0, at, :].astype(F32) + m.rsc2[0, at, :].astype(F32)
            grad = grad + m.rsy2[at, :].astype(F32)
            full, r = full_of(m.mid[at, :].astype(F32))
            back = crms_back(grad, full, r, m.gbuf[1, :1, :])
            mine = rows(t * H + i * 64, 64, 64)
            m.gm[mine, :] = (m.cot[mine, :].astype(F32) + back).astype(BF)
            return gain + jnp.sum(grad * full * r, axis=0, keepdims=True)

        gain_two = lax.fori_loop(0, H // 64, grad_middle_step, jnp.zeros((1, D), F32))
        m.sm[0, 1:2, :] = gain_two
        gm_y = send(m.gm.at[here], m.gm.at[here], ydev)
        gm_core = send(m.gm.at[here], m.gm.at[here], core)
        gm_x = link(m.gm.at[here], m.gother, xdev)

        @pl.when(x == 1)
        def _():
            gm_x.start()

        serve_next(BEFORE[4])
        gm_y.wait_recv()
        part = m.gm.at[rows(t2 * H, H, H)]
        gm_fwd = send(part, part, core)
        mp_copies[1].wait_recv()
        y_proj.wait_send()
        add_rows(m.ysnd, (m.proj.at[2], m.rsc.at[1]), H)
        mp_y = send(m.ysnd, m.rsy, ydev)
        gm_core.wait_recv()
        gm_fwd.wait_recv()

        m.gsrc[OUT : OUT + AW, :] = dot_tn(m.att[...], m.gm[...]).astype(BF)
        m.dkt[...] = jnp.zeros_like(m.dkt)
        m.dvt[...] = jnp.zeros_like(m.dvt)
        m.gq[...] = jnp.zeros_like(m.gq)

        C_GN = counter[0]
        counter[0] += 2

        def pair_rows(j):
            return rows(j * R, R, R)

        def gn_copy(j):
            return link(m.gh.at[pair_rows(j)], m.rscf.at[j], core, C_GN + j, C_GN + j)

        C_YF = counter[0]
        counter[0] += 4
        chunk = R // 4

        def yf_copy(k):
            src = m.act.at[rows((1 - y) * R + k * chunk, chunk, chunk)]
            dst = m.rsyf.at[rows(k * chunk, chunk, chunk)]
            return link(src, dst, ydev, C_YF + k, C_YF + k)

        def send_far():
            gn_copy(1 - y).wait_recv()

            def step(k, _):
                def inside(i, _):
                    r0 = k * chunk + i * 64
                    at = rows((1 - y) * R + r0, 64, 64)
                    both = m.act[at, :].astype(F32) + m.rscf[1 - y, rows(r0, 64, 64), :].astype(F32)
                    m.act[at, :] = both.astype(BF)
                    return 0

                lax.fori_loop(0, chunk // 64, inside, 0)
                yf_copy(k).start()
                return 0

            lax.fori_loop(0, 4, step, 0)

        far_step = 3 - (2 * (1 - y) + c)
        BACK = sum(BEFORE)

        def back_served(i, units):
            return BACK + UNIT * (4 * i - lax.div(i * (i - 1), 2) + units) + BLOCK * i

        def back_block(i, _):
            b = 3 - i
            at = rows(b * H, H, H)
            mine = rows(b * R + xh, H, H)
            grad_att = dot_nt(m.gm[at, :], m.wao[...])
            outs, offs, out_ts, q_ts = [], [], [], []
            for h in range(NH):
                cols = slice(h * HS, (h + 1) * HS)
                inverse = m.il[at, h : h + 1]
                out = grad_att[:, cols].astype(BF).astype(F32)
                delta = total(out * m.att[at, cols].astype(F32))
                offs.append(delta * inverse)
                out = (out * inverse).astype(BF)
                outs.append(out)
                out_ts.append(jnp.transpose(out))
                q_ts.append(jnp.transpose(m.q[h, mine, :]))

            def keys(kb, grads):
                new = []
                for h in range(NH):
                    e = m.e[unit(b, kb) * NH + h]
                    at_k = rows(kb * R, R, R)
                    dp = dot_nt(outs[h], m.v[h, at_k, :])
                    ds = (e.astype(F32) * (dp - offs[h])).astype(BF)
                    new.append(grads[h] + dot_nn(ds, m.k[h, at_k, :]))
                    m.dkt[kb, h] += dot_nn(q_ts[h], ds)
                    m.dvt[kb, h] += dot_nn(out_ts[h], e)
                serve_range(back_served(i, kb), back_served(i, kb + 1))
                return tuple(new)

            grads = lax.fori_loop(0, b + 1, keys, (jnp.zeros((H, HS), F32),) * NH)
            for h in range(NH):
                base = 3 * h * HS
                grad_q = jnp.transpose(grads[h] * HS**-0.5).astype(BF)
                m.dmt[base : base + HS, rows(xh, H, H)] = grad_q
                m.dmt[base : base + HS, rows(oh, H, H)] = jnp.zeros((HS, H), BF)
                m.dmt[base + HS : base + 2 * HS, :] = m.dkt[b, h].astype(BF)
                m.dmt[base + 2 * HS : base + 3 * HS, :] = m.dvt[b, h].astype(BF)
            n1_rows = rows(b * R, R, R)
            m.gq[...] += dot_nn(m.dmt[...], m.normed[n1_rows, :])
            back = dot_nn(jnp.transpose(m.dmt[...]), m.wqkv[...]).astype(BF)
            j = lax.div(b, 2)

            @pl.when(lax.rem(b, 2) == c)
            def _():
                m.act[pair_rows(j), :] = back

            @pl.when(lax.rem(b, 2) != c)
            def _():
                m.gh[pair_rows(j), :] = back
                gn_copy(j).start()

            serve_range(back_served(i, b + 1), back_served(i + 1, 0))

            @pl.when(i == far_step + 1)
            def _():
                send_far()

            return 0

        lax.fori_loop(0, 4, back_block, 0)
        pl.when(far_step == 3)(send_far)
        m.gsrc[QKV : QKV + QW, :] = m.gq[...].astype(BF)
        tail[0] = BACK + 10 * UNIT + 4 * BLOCK
        mp_copies[0].wait_recv()
        mp_y.wait_recv()
        n2_y.wait_send()
        n2_core.wait_send()
        add_rows(m.n2.at[here], (m.mid, m.proj.at[0], m.rsc.at[0], m.rsy), H)
        bo_x = link(m.n2.at[here], m.gother, xdev)

        @pl.when(x == 0)
        def _():
            bo_x.start()

        serve_next(2)

        gn_copy(y).wait_recv()

        C_XF = counter[0]
        counter[0] += 4

        def xf_copy(k):
            src = m.act.at[rows(y * R + k * chunk, chunk, chunk)]
            dst = m.rsxf.at[rows(k * chunk, chunk, chunk)]
            return link(src, dst, xdev, C_XF + k, C_XF + k)

        def near_sum(k):
            yf_copy(k).wait_recv()

            def inside(i, _):
                r0 = k * chunk + i * 64
                at = rows(y * R + r0, 64, 64)
                here_rows = rows(r0, 64, 64)
                both = m.act[at, :].astype(F32) + m.rscf[y, here_rows, :].astype(F32)
                m.act[at, :] = (both + m.rsyf[here_rows, :].astype(F32)).astype(BF)
                return 0

            lax.fori_loop(0, chunk // 64, inside, 0)

        first = tail[0]
        tail[0] += 2

        def near_step(k, _):
            serve_range(first + lax.div(k, 2), first + lax.div(k + 1, 2))
            near_sum(k)

            @pl.when(x == 1)
            def _():
                xf_copy(k).start()

            return 0

        lax.fori_loop(0, 4, near_step, 0)
        m.sm[0, 0:1, :] = jnp.zeros((1, D), F32)
        then = tail[0]
        tail[0] += 2

        def grad_in_step(k, _):
            serve_range(then + lax.div(k, 2), then + lax.div(k + 1, 2))

            @pl.when(x == 0)
            def _():
                xf_copy(k).wait_recv()

                def inside(i, gain):
                    r0 = k * chunk + i * 64
                    here_rows = rows(r0, 64, 64)
                    grad = m.act[rows(y * R + r0, 64, 64), :].astype(F32)
                    grad = grad + m.rsxf[here_rows, :].astype(F32)
                    full, r = full_of(m.n1[rows(t * R + r0, 64, 64), :].astype(F32))
                    back = crms_back(grad, full, r, m.gbuf[0, :1, :])
                    m.rsyf[here_rows, :] = back.astype(BF)
                    return gain + jnp.sum(grad * full * r, axis=0, keepdims=True)

                gain = lax.fori_loop(0, chunk // 64, inside, jnp.zeros((1, D), F32))
                m.sm[0, 0:1, :] += gain

            return 0

        lax.fori_loop(0, 4, grad_in_step, 0)

        @pl.when(x == 0)
        def _():
            gm_x.wait_recv()

            def out_step(i, _):
                at = rows(i * 64, 64, 64)
                one = m.gm[rows(t * H + i * 64, 64, 64), :].astype(F32) + m.rsyf[at, :].astype(F32)
                o_io[0, at, :] = one[:, :C].astype(BF)
                below = rows(H + i * 64, 64, 64)
                two = m.gother[at, :].astype(F32) + m.rsyf[below, :].astype(F32)
                o_io[0, below, :] = two[:, :C].astype(BF)
                return 0

            lax.fori_loop(0, H // 64, out_step, 0)

        @pl.when(x == 1)
        def _():
            bo_x.wait_recv()
            o_io[0, 0:H, :] = m.gother[:, :C]
            o_io[0, H:R, :] = m.n2[here, :C]

        for j, peer in enumerate((core, ydev, xdev)):
            copy = send(m.sm.at[j], m.smr.at[j], peer)
            serve_next(1)
            copy.wait_recv()
            m.sm[j + 1] = m.sm[j] + m.smr[j]
        z_copies = []
        for j in range(1, N):
            z_copies.append(send(m.sm.at[3], m.smz.at[j], (x, lax.rem(d + j, N), t)))
        serve_range(tail[0], GROUPS + 5 * LAG)
        everything = m.sm[3]
        for j in range(1, N):
            z_copies[j - 1].wait_recv()
            everything = everything + m.smz[j]
        o_sm[...] = jnp.zeros_like(o_sm)

        @pl.when(x == 0)
        def _():
            o_sm[0:1, :] = everything[0:1]

        @pl.when(x == 1)
        def _():
            o_sm[0:1, :] = everything[1:2]

        o_sm[1:2, :] = jnp.broadcast_to(
            jnp.sqrt(total(everything[2:3]) * (1.0 / (4 * R * N * D))), (1, D)
        )

        serve_all_sent()
        waited = {id(n2_y), id(n2_core), id(y_proj)}
        for copy in pending:
            if id(copy) not in waited:
                copy.wait_send()
        for j in range(2):
            gn_copy(j).wait_send()
        for k in range(4):
            yf_copy(k).wait_send()

        @pl.when(x == 1)
        def _():
            gm_x.wait_send()
            for k in range(4):
                xf_copy(k).wait_send()

        @pl.when(x == 0)
        def _():
            bo_x.wait_send()

        assert counter[0] <= N_SEM

    return body, scratch_shapes, GRADS, (DOWN, UP, OUT, QKV)


def per_device(mesh):
    N = mesh.shape["dp"]
    assert mesh.shape["blk"] == 2 and mesh.shape["tensor"] == 4 and N % 2 == 0

    def run(stream_in, lengths, norm_gains, w_qkv, w_attn_out, w_up, w_down, cotangent):
        R, C = stream_in.shape
        D = norm_gains.shape[1]
        FF = w_up.shape[1]
        NH = w_qkv.shape[1] // (3 * HS)
        body, scratch, grad_rows, (DOWN, UP, OUT, QKV) = kernel_for(
            dict(R=R, H=R // 2, D=D, C=C, FF=FF, NH=NH, N=N)
        )
        vmem = pl.BlockSpec(memory_space=pltpu.VMEM)
        smem = pl.BlockSpec(memory_space=pltpu.SMEM)
        anywhere = pl.BlockSpec(memory_space=pl.ANY)
        block_io, grads, small = pl.pallas_call(
            body,
            out_shape=(
                jax.ShapeDtypeStruct((1, R, C), BF),
                jax.ShapeDtypeStruct((grad_rows, D), BF),
                jax.ShapeDtypeStruct((8, D), F32),
            ),
            in_specs=[smem, vmem] + [anywhere] * 6,
            out_specs=(vmem,) * 3,
            scratch_shapes=scratch,
            compiler_params=pltpu.CompilerParams(
                collective_id=0, has_side_effects=True, vmem_limit_bytes=63 << 20
            ),
        )(lengths, norm_gains, stream_in, cotangent, w_qkv.T, w_attn_out, w_up, w_down)

        def spread(io_in, down_in, up_in, out_in, qkv_in, small_in, io, gain, qkv, out, up, down, rms):
            io[...] = io_in[...]
            down[...] = down_in[:, :C].astype(F32)
            up[...] = up_in[...].astype(F32)
            out[...] = out_in[:, :C].astype(F32)
            qkv[...] = qkv_in[...].astype(F32)
            gain[...] = small_in[0:1, :]
            rms[0, 0] = jnp.max(small_in[1:2, :])

        steps = 6
        QW, AW = grad_rows - QKV, QKV - OUT
        sizes = (FF // steps, D // steps, AW // steps, QW // steps)
        firsts = (DOWN, UP, OUT, QKV)
        piece_specs = [
            pl.BlockSpec((n, D), lambda i, o=first // n: (o + i, 0))
            for n, first in zip(sizes, firsts, strict=True)
        ]
        io_spec = pl.BlockSpec((1, R // 4, C), lambda i: (0, jnp.minimum(i, 3), 0))
        whole = lambda i: (0, 0)
        block_io, gain, grad_qkv, grad_out, grad_up, grad_down, rms = pl.pallas_call(
            spread,
            grid=(steps,),
            out_shape=(
                jax.ShapeDtypeStruct((1, R, C), BF),
                jax.ShapeDtypeStruct((1, D), F32),
                jax.ShapeDtypeStruct((QW, D), F32),
                jax.ShapeDtypeStruct((AW, C), F32),
                jax.ShapeDtypeStruct((D, FF), F32),
                jax.ShapeDtypeStruct((FF, C), F32),
                jax.ShapeDtypeStruct((1, 1), F32),
            ),
            in_specs=[io_spec, *piece_specs, pl.BlockSpec((8, D), whole)],
            out_specs=(
                io_spec,
                pl.BlockSpec((1, D), whole),
                pl.BlockSpec((sizes[3], D), lambda i: (i, 0)),
                pl.BlockSpec((sizes[2], C), lambda i: (i, 0)),
                pl.BlockSpec((sizes[1], FF), lambda i: (i, 0)),
                pl.BlockSpec((sizes[0], C), lambda i: (i, 0)),
                smem,
            ),
        )(block_io, grads, grads, grads, grads, small)
        return (block_io, gain, grad_qkv.T, grad_out, grad_up, grad_down, rms.reshape(()))

    return run


def solution(mesh):
    in_specs = (
        P(("dp", "tensor"), None),
        P("dp"),
        P("blk", None),
        P(None, "tensor"),
        P("tensor", None),
        P(None, "tensor"),
        P("tensor", None),
        P(("dp", "tensor"), None),
    )
    out_specs = (
        P("blk", ("dp", "tensor"), None),
        P("blk", None),
        P(None, "tensor"),
        P("tensor", None),
        P(None, "tensor"),
        P("tensor", None),
        P(),
    )
    return jax.shard_map(
        per_device(mesh), mesh=mesh, in_specs=in_specs, out_specs=out_specs, check_vma=False
    )
```

```python
from types import SimpleNamespace

import jax
import jax.numpy as jnp
from jax import lax
from jax.experimental import pallas as pl
from jax.experimental.pallas import tpu as pltpu
from jax.sharding import PartitionSpec as P

HS = 64
EPSILON = 1e-05
MASKED = -1e30
BF = jnp.bfloat16
F32 = jnp.float32
MESH = pl.DeviceIdType.MESH
SUB = 48
LAG = 2
BEFORE = (1, 2, 1, 1, 1)
WITHIN = 6
ROOT = 0.7978845608028654


def dot_nn(a, b):
    return jnp.dot(a, b, preferred_element_type=F32)


def dot_nt(a, b):
    return lax.dot_general(a, b, (((1,), (1,)), ((), ())), preferred_element_type=F32)


def dot_tn(a, b):
    return lax.dot_general(a, b, (((0,), (0,)), ((), ())), preferred_element_type=F32)


def rows(start, count, multiple):
    return pl.ds(pl.multiple_of(start, multiple), count)


def lane_groups(value):
    return [value[:, i : i + 128] for i in range(0, value.shape[1], 128)]


def kernel_for(sizes):
    R, H, D, C, FF, NH, N = (sizes[k] for k in ("R", "H", "D", "C", "FF", "NH", "N"))
    QW = NH * 3 * HS
    AW = NH * HS
    GRADS = 2 * D + AW + QW
    GROUPS = GRADS // (3 * SUB)
    DOWN, UP, OUT, QKV = 0, FF, FF + D, FF + D + AW
    half_n = N // 2

    names = {}

    def scratch(name, shape, dtype):
        names[name] = pltpu.VMEM(shape, dtype)

    scratch("gbuf", (2, 8, D), F32)
    scratch("stream", (R, C), BF)
    scratch("cot_in", (H, C), BF)
    scratch("wqkv", (QW, D), BF)
    scratch("wao_in", (AW, C), BF)
    scratch("wup", (D, FF), BF)
    scratch("wdn_in", (FF, C), BF)
    scratch("normed", (4 * R, D), BF)
    scratch("wao", (AW, D), BF)
    scratch("wdn", (FF, D), BF)
    scratch("n1", (4 * R, D), BF)
    scratch("q", (NH, 4 * R, HS), BF)
    scratch("k", (NH, 4 * R, HS), BF)
    scratch("v", (NH, 4 * R, HS), BF)
    scratch("e", (10 * NH, H, R), BF)
    scratch("il", (4 * H, 128), F32)
    scratch("att", (4 * H, AW), BF)
    scratch("proj", (4, H, D), BF)
    scratch("rsc", (2, H, D), BF)
    scratch("ysnd", (H, D), BF)
    scratch("rsy", (H, D), BF)
    scratch("mid", (H, D), BF)
    scratch("n2", (4 * H, D), BF)
    scratch("cot", (4 * H, D), BF)
    scratch("act", (4 * H, FF), BF)
    scratch("gh", (4 * H, FF), BF)
    scratch("gp", (4, H, D), BF)
    scratch("rsc2", (2, H, D), BF)
    scratch("ysnd2", (H, D), BF)
    scratch("rsy2", (H, D), BF)
    scratch("gm", (4 * H, D), BF)
    scratch("gother", (H, D), BF)
    scratch("dmt", (QW, R), BF)
    scratch("dqt", (4, AW, H), BF)
    scratch("dkt", (4, NH, HS, R), F32)
    scratch("dvt", (4, NH, HS, R), F32)
    scratch("gq", (QW, D), F32)
    scratch("rscf", (2, R, D), BF)
    scratch("rsyf", (R, D), BF)
    scratch("rsxf", (R, D), BF)
    scratch("gsrc", (GRADS, D), BF)
    scratch("res", (GRADS, D), BF)
    scratch("gb", ((GROUPS + -(-GROUPS // 4)) * SUB, D), BF)
    scratch("gc", ((GROUPS + -(-GROUPS // 2)) * SUB, D), BF)
    scratch("sm", (5, 8, D), F32)
    scratch("smr", (3, 8, D), F32)
    scratch("smz", (N, 8, D), F32)
    n_vmem = len(names)
    N_SEM = 10 * GROUPS + 64 + N
    scratch_shapes = list(names.values()) + [
        pltpu.SemaphoreType.DMA((N_SEM,)),
        pltpu.SemaphoreType.DMA((N_SEM,)),
        pltpu.SemaphoreType.DMA((6,)),
        pltpu.SemaphoreType.DMA((GROUPS,)),
    ]

    def body(
        lens, gains, stream, cot_in, w_qkv, w_ao, w_up, w_dn, o_io, o_gr, o_sm, *refs
    ):
        m = SimpleNamespace(**dict(zip(names, refs[:n_vmem], strict=True)))
        ssem, rsem, lsem, osem = refs[n_vmem:]
        res = m.res
        x = lax.axis_index("blk")
        d = lax.axis_index("dp")
        t = lax.axis_index("tensor")
        y = lax.div(t, 2)
        c = lax.rem(t, 2)
        t1 = 2 * y + 1 - c
        t2 = 2 * (1 - y) + c
        t3 = 2 * (1 - y) + 1 - c
        core, ydev, xdev = (x, d, t1), (x, d, t2), (1 - x, d, t)
        xh, oh = x * H, (1 - x) * H

        counter = [10 * GROUPS]
        pending = []

        def link(src, dst, dev, s_idx=None, r_idx=None):
            if s_idx is None:
                s_idx = r_idx = counter[0]
                counter[0] += 1
            return pltpu.make_async_remote_copy(
                src_ref=src,
                dst_ref=dst,
                send_sem=ssem.at[s_idx],
                recv_sem=rsem.at[r_idx],
                device_id=dev,
                device_id_type=MESH,
            )

        def send(src, dst, dev):
            copy = link(src, dst, dev)
            copy.start()
            pending.append(copy)
            return copy

        loads = []
        for i, (src, dst) in enumerate(
            (
                (stream, m.stream),
                (w_qkv, m.wqkv),
                (cot_in.at[rows(xh, H, H)], m.cot_in),
                (w_ao, m.wao_in),
                (w_up, m.wup),
                (w_dn, m.wdn_in),
            )
        ):
            loads.append(pltpu.make_async_copy(src, dst, lsem.at[i]))
            loads[-1].start()

        barrier = pltpu.get_barrier_semaphore()
        for peer in (core, ydev, xdev):
            pl.semaphore_signal(barrier, inc=1, device_id=peer, device_id_type=MESH)
        for j in range(1, N):
            pl.semaphore_signal(
                barrier,
                inc=1,
                device_id=(x, lax.rem(d + j, N), t),
                device_id_type=MESH,
            )
        pl.semaphore_wait(barrier, 3 + N - 1)

        lane = lax.broadcasted_iota(jnp.int32, (1, D), 1)
        last = lane == D - 1

        def total(value):
            return jnp.sum(value, axis=1, keepdims=True)

        def full_of(stream_rows):
            full = jnp.where(last, -total(stream_rows), stream_rows)
            return full, lax.rsqrt(total(full * full) * (1.0 / D) + EPSILON)

        def crms_back(grad, full, r, gain):
            a = grad * gain
            mean = total(a * full) * (1.0 / D)
            df = r * (a - full * (r * r * mean))
            tail = total(jnp.where(last, df, 0.0))
            return jnp.where(last, 0.0, df - tail)

        m.gbuf[x] = jnp.broadcast_to(gains[...], (8, D))
        gain_copy = send(m.gbuf.at[x], m.gbuf.at[x], xdev)
        loads[0].wait()
        own_rows = rows(t * R, R, R)
        m.n1[own_rows, D - 128 :] = jnp.zeros((R, 128), BF)
        m.n1[own_rows, :C] = m.stream[...]
        here = rows(t * H, H, H)

        half = H // 4
        y_copies = []
        for k in range(4):
            part = m.n1.at[rows(t * R + xh + k * half, half, half)]
            y_copies.append(send(part, part, ydev))
        part = m.n1.at[rows(t * R, R, R)]
        own_copy = send(part, part, core)
        loads[2].wait()
        m.cot[here, D - 128 :] = jnp.zeros((H, 128), BF)
        m.cot[here, :C] = m.cot_in[...]
        part = m.cot.at[here]
        cot_core = send(part, part, core)

        def qkv_rows(start):
            def step(i, _):
                some = rows(start + i * 64, 64, 64)
                full, r = full_of(m.n1[some, :].astype(F32))
                m.normed[some, :] = (full * r * m.gbuf[0, :1, :]).astype(BF)
                return 0

            lax.fori_loop(0, H // 64, step, 0)
            mixed = dot_nt(m.normed[rows(start, H, H), :], m.wqkv[...])
            at = rows(start, H, H)
            for h in range(NH):
                for p, ref in enumerate((m.q, m.k, m.v)):
                    part = mixed[:, (3 * h + p) * HS : (3 * h + p + 1) * HS]
                    if p == 0:
                        part = part * HS**-0.5
                    ref[h, at, :] = part.astype(BF)

        def qkv_block(block):
            lax.fori_loop(0, 2, lambda i, _: (qkv_rows(block * R + i * H), 0)[1], 0)

        loads[1].wait()
        gain_copy.wait_recv()
        qkv_block(t)
        own_copy.wait_recv()
        qkv_block(t1)
        for load in loads[3:]:
            load.wait()
        m.wao[:, D - 128 :] = jnp.zeros((AW, 128), BF)
        m.wao[:, :C] = m.wao_in[...]
        m.wdn[:, D - 128 :] = jnp.zeros((FF, 128), BF)
        m.wdn[:, :C] = m.wdn_in[...]
        fwd = []
        x_copies = []
        for k in range(4):
            y_copies[k].wait_recv()
            part = m.n1.at[rows(t2 * R + xh + k * half, half, half)]
            x_copies.append(send(part, part, xdev))
            fwd.append(send(part, part, core))
        part = m.cot.at[here]
        cot_y = send(part, part, ydev)
        for k in range(4):
            x_copies[k].wait_recv()
            part = m.n1.at[rows(t2 * R + oh + k * half, half, half)]
            fwd.append(send(part, part, core))
        qkv_block(t2)
        for copy in fwd:
            copy.wait_recv()
        qkv_block(t3)

        ends = [lens[0]]
        for i in range(1, 4):
            ends.append(ends[-1] + lens[i])

        def bias_of(b, kb):
            cut = (ends[0] > kb * R) & (ends[0] <= b * R)
            for e in ends[1:]:
                cut = cut | ((e > kb * R) & (e <= b * R))
            return jnp.where(cut, MASKED, 0.0).astype(F32)

        row_at = lax.broadcasted_iota(jnp.int32, (H, R), 0)
        col_at = lax.broadcasted_iota(jnp.int32, (H, R), 1)

        def unit(b, kb):
            return lax.div(b * (b + 1), 2) + kb

        def attend(b, between):
            mine = rows(b * R + xh, H, H)
            heads = [m.q[h, mine, :] for h in range(NH)]

            def scores(h, kb):
                return dot_nt(heads[h], m.k[h, rows(kb * R, R, R), :])

            def top(s, best):
                for g in lane_groups(s):
                    best = jnp.maximum(best, g)
                return best

            def masked(s):
                return jnp.where(col_at <= row_at + xh, s, MASKED)

            def peak(kb, best):
                bias = bias_of(b, kb)
                low = jnp.full((H, 128), -jnp.inf, F32)
                return tuple(
                    jnp.maximum(best[h], top(scores(h, kb), low) + bias) for h in range(NH)
                )

            low = jnp.full((H, 128), MASKED, F32)
            best = tuple(top(masked(scores(h, b)), low) for h in range(NH))
            best = lax.fori_loop(0, b, peak, best)
            best = [jnp.max(v, axis=1, keepdims=True) for v in best]
            between()

            def weigh(h, kb, s, off, sums, acc):
                e = jnp.exp(s - off)
                for g in lane_groups(e):
                    sums = sums + g
                e = e.astype(BF)
                m.e[unit(b, kb) * NH + h] = e
                return sums, acc + dot_nn(e, m.v[h, rows(kb * R, R, R), :])

            def add(kb, carry):
                bias = bias_of(b, kb)
                return tuple(
                    weigh(h, kb, scores(h, kb), best[h] - bias, *carry[h]) for h in range(NH)
                )

            zero = (jnp.zeros((H, 128), F32), jnp.zeros((H, HS), F32))
            carry = tuple(weigh(h, b, masked(scores(h, b)), best[h], *zero) for h in range(NH))
            carry = lax.fori_loop(0, b, add, carry)
            at = rows(b * H, H, H)
            for h in range(NH):
                inverse = 1.0 / total(carry[h][0])
                m.il[at, h : h + 1] = inverse
                m.att[at, h * HS : (h + 1) * HS] = (carry[h][1] * inverse).astype(BF)
            return dot_nn(m.att[at, :], m.wao[...]).astype(BF)

        C_PROJ = counter[0]
        counter[0] += 2

        def proj_copy(i):
            j = lax.div(i, 2)
            return link(m.proj.at[i], m.rsc.at[j], core, C_PROJ + j, C_PROJ + j)

        def add_rows(out, terms, count):
            def step(i, _):
                at = rows(i * 64, 64, 64)
                out[at, :] = sum(ref[at, :].astype(F32) for ref in terms).astype(BF)
                return 0

            lax.fori_loop(0, count // 64, step, 0)

        y_proj = link(m.ysnd, m.rsy, ydev)
        pending.append(y_proj)

        def attend_step(i, _):
            a, e = lax.div(i, 2), 1 - lax.rem(i, 2)
            g = (1 - y) * (1 - a) + y * a

            def between():
                @pl.when(i == 2 - c)
                def _():
                    proj_copy(c).wait_recv()
                    add_rows(m.ysnd, (m.proj.at[1 - c], m.rsc.at[0]), H)
                    y_proj.start()

            m.proj[i] = attend(2 * g + e, between)

            @pl.when(lax.rem(i, 2) == c)
            def _():
                proj_copy(i).start()

            return 0

        lax.fori_loop(0, 4, attend_step, 0)
        proj_copy(2 + c).wait_recv()
        cot_core.wait_recv()
        cot_y.wait_recv()
        part = m.cot.at[rows(t2 * H, H, H)]
        cot_fwd = send(part, part, core)
        y_proj.wait_recv()

        def middle_step(i, squares):
            at = rows(i * 64, 64, 64)
            mid = m.n1[rows(t * R + xh + i * 64, 64, 64), :].astype(F32)
            mid = mid + m.proj[2 + 1 - c, at, :].astype(F32)
            mid = mid + m.rsc[1, at, :].astype(F32) + m.rsy[at, :].astype(F32)
            mid = mid.astype(BF)
            m.mid[at, :] = mid
            full, r = full_of(mid.astype(F32))
            m.n2[rows(t * H + i * 64, 64, 64), :] = (full * r * m.gbuf[1, :1, :]).astype(BF)
            return squares + jnp.sum(full * full, axis=0, keepdims=True)

        squares = lax.fori_loop(0, H // 64, middle_step, jnp.zeros((1, D), F32))
        m.sm[0] = jnp.zeros((8, D), F32)
        m.sm[0, 2:3, :] = squares

        n2_y = send(m.n2.at[here], m.n2.at[here], ydev)
        n2_core = send(m.n2.at[here], m.n2.at[here], core)

        def feed(s, i):
            at = rows(s * H, H, H)
            for f in range(FF // 256):
                cols = slice(f * 256, (f + 1) * 256)
                hidden = dot_nn(m.n2[at, :], m.wup[:, cols])
                grad = dot_nt(m.cot[at, :], m.wdn[cols, :])
                square = hidden * hidden
                bent = jnp.tanh(ROOT * hidden * (1.0 + 0.044715 * square))
                gate = 0.5 * (1.0 + bent)
                m.act[at, cols] = (hidden * gate).astype(BF)
                slope = gate + (0.5 * ROOT) * hidden * (1.0 - bent * bent) * (
                    1.0 + (3 * 0.044715) * square
                )
                m.gh[at, cols] = (grad * slope).astype(BF)
            m.gp[i] = dot_nt(m.gh[at, :], m.wup[...]).astype(BF)

        C_GP = counter[0]
        counter[0] += 2
        C_N2 = counter[0]
        counter[0] += 1
        gp_copies = [
            link(m.gp.at[2 * j + 1], m.rsc2.at[j], core, C_GP + j, C_GP + j) for j in range(2)
        ]
        part = m.n2.at[rows(t2 * H, H, H)]
        n2_fwd = link(part, part, core, C_N2, C_N2)
        pending.append(n2_fwd)
        pending.extend(gp_copies)

        def feed_step(i, _):
            a, e = lax.div(i, 2), lax.rem(i, 2)
            s = 2 * (y + a - 2 * y * a) + (c + e - 2 * c * e)

            @pl.when(i == 1)
            def _():
                n2_core.wait_recv()

            @pl.when(i == 2)
            def _():
                n2_y.wait_recv()
                n2_fwd.start()
                cot_fwd.wait_recv()

            @pl.when(i == 3)
            def _():
                n2_fwd.wait_recv()

            feed(s, i)

            @pl.when(i == 1)
            def _():
                gp_copies[0].start()

            @pl.when(i == 3)
            def _():
                gp_copies[1].start()

            return 0

        lax.fori_loop(0, 4, feed_step, 0)
        gp_copies[1].wait_recv()
        add_rows(m.ysnd2, (m.gp.at[2], m.rsc2.at[1]), H)
        gp_y = send(m.ysnd2, m.rsy2, ydev)

        is_mid = (d == half_n - 1) | (d == half_n)
        is_end = (d == 0) | (d == N - 1)
        side = jnp.where(d < half_n, 0, 1)
        step_in = 1 - 2 * side
        inner = (x, lax.rem(d + step_in + N, N), t)
        outer = (x, lax.rem(d - step_in + N, N), t)

        not_end = jnp.logical_not(is_end)

        def sub_rows(ref, at, count):
            return ref.at[rows(at, count * SUB, 16)]

        def group_at(g):
            return g * (3 * SUB)

        def third_at(g):
            return group_at(g) + 2 * SUB

        def sub_at(g, who):
            return group_at(g) + who * SUB

        def sem(kind, g):
            return kind * GROUPS + g

        def in_copy(g):
            at = group_at(g)
            return link(sub_rows(m.gsrc, at, 2), sub_rows(res, at, 2), inner, sem(0, g), sem(0, g))

        def mid_copy(g):
            src = sub_rows(m.gsrc, sub_at(g, 1 - side), 1)
            return link(src, sub_rows(m.gb, g * SUB, 1), inner, sem(1, g), sem(1, g))

        def blk_copy(g):
            src = sub_rows(m.gsrc, sub_at(g, side), 1)
            return link(src, sub_rows(m.gc, g * SUB, 1), xdev, sem(2, g), sem(2, g))

        def res_link(g, who, dev, kind):
            at = sub_rows(res, sub_at(g, who), 1)
            return link(at, at, dev, sem(kind, g), sem(3, g) + GROUPS * who)

        def own_part(g):
            return res_link(g, side, inner, 3)

        def own_out(g):
            return res_link(g, side, outer, 4)

        def other_part(g):
            return res_link(g, 1 - side, inner, 3)

        def other_out(g):
            return res_link(g, 1 - side, outer, 5)

        def c_link(dst, dev, kind):
            def make(g):
                src = sub_rows(m.gsrc, third_at(g), 1)
                return link(src, dst(g), dev, sem(6, g), sem(kind, g))

            return make

        def c_res(dev, kind):
            def make(g):
                at = sub_rows(res, third_at(g), 1)
                return link(at, at, dev, sem(kind, g), sem(8, g))

            return make

        c_blk = c_link(lambda g: sub_rows(m.gc, (GROUPS + lax.div(g, 2)) * SUB, 1), xdev, 5)
        c_in = c_link(lambda g: sub_rows(res, third_at(g), 1), inner, 6)
        c_mid = c_link(lambda g: sub_rows(m.gb, (GROUPS + lax.div(g, 4)) * SUB, 1), inner, 7)
        c_part, c_out, c_back = c_res(inner, 7), c_res(outer, 8), c_res(xdev, 9)

        def add(out, at, other, count):
            for k in range(count):
                here_rows = rows(at + k * SUB, SUB, 16)
                there = other[k * SUB : (k + 1) * SUB, :].astype(F32)
                out[here_rows, :] = (m.gsrc[here_rows, :].astype(F32) + there).astype(BF)

        def valid(g):
            return (g >= 0) & (g < GROUPS)

        def mine(g):
            return x == lax.rem(g + 2 * GROUPS, 2)

        def late_owns(g):
            return side == lax.rem(lax.div(g + 4 * GROUPS, 2), 2)

        def serve(s):
            g1, g2, g3, g4, g5, g6 = (s - i * LAG for i in range(6))

            @pl.when(valid(g1) & jnp.logical_not(mine(g1)))
            def _():
                c_blk(g1).start()

            @pl.when(jnp.logical_not(is_mid))
            def _():
                @pl.when(valid(g1))
                def _():
                    if N > 4:

                        @pl.when(not_end)
                        def _():
                            in_copy(g1).wait_recv()
                            add(m.gsrc, group_at(g1), sub_rows(res, group_at(g1), 2), 2)

                    in_copy(g1).start()

                @pl.when(valid(g2) & mine(g2))
                def _():
                    c_blk(g2).wait_recv()
                    add(m.gsrc, third_at(g2), sub_rows(m.gc, (GROUPS + lax.div(g2, 2)) * SUB, 1), 1)
                    if N > 4:

                        @pl.when(not_end)
                        def _():
                            c_in(g2).wait_recv()
                            add(m.gsrc, third_at(g2), sub_rows(res, third_at(g2), 1), 1)

                    c_in(g2).start()

                @pl.when(valid(g6))
                def _():
                    if N > 4:

                        @pl.when(not_end)
                        def _():
                            own_out(g6).wait_recv()
                            own_out(g6).start()
                            other_out(g6).wait_recv()
                            other_out(g6).start()

                    @pl.when(mine(g6))
                    def _():
                        c_part(g6).wait_recv()
                        c_back(g6).start()
                        if N > 4:

                            @pl.when(not_end)
                            def _():
                                c_out(g6).start()

            @pl.when(is_mid)
            def _():
                @pl.when(valid(g2))
                def _():
                    if N > 2:

                        @pl.when(not_end)
                        def _():
                            in_copy(g2).wait_recv()
                            add(m.gsrc, group_at(g2), sub_rows(res, group_at(g2), 2), 2)

                    mid_copy(g2).start()

                    @pl.when(mine(g2))
                    def _():
                        c_blk(g2).wait_recv()
                        add(m.gsrc, third_at(g2), sub_rows(m.gc, (GROUPS + lax.div(g2, 2)) * SUB, 1), 1)

                @pl.when(valid(g3))
                def _():
                    mid_copy(g3).wait_recv()
                    add(m.gsrc, sub_at(g3, side), sub_rows(m.gb, g3 * SUB, 1), 1)
                    blk_copy(g3).start()

                    @pl.when(mine(g3))
                    def _():
                        if N > 2:

                            @pl.when(not_end)
                            def _():
                                c_in(g3).wait_recv()
                                add(m.gsrc, third_at(g3), sub_rows(res, third_at(g3), 1), 1)

                        @pl.when(jnp.logical_not(late_owns(g3)))
                        def _():
                            c_mid(g3).start()

                @pl.when(valid(g4))
                def _():
                    blk_copy(g4).wait_recv()
                    add(res, sub_at(g4, side), sub_rows(m.gc, g4 * SUB, 1), 1)
                    own_part(g4).start()
                    if N > 2:

                        @pl.when(not_end)
                        def _():
                            own_out(g4).start()

                    @pl.when(mine(g4) & late_owns(g4))
                    def _():
                        c_mid(g4).wait_recv()
                        add(res, third_at(g4), sub_rows(m.gb, (GROUPS + lax.div(g4, 4)) * SUB, 1), 1)
                        c_part(g4).start()
                        c_back(g4).start()
                        if N > 2:

                            @pl.when(not_end)
                            def _():
                                c_out(g4).start()

                @pl.when(valid(g5))
                def _():
                    other_part(g5).wait_recv()
                    if N > 2:

                        @pl.when(not_end)
                        def _():
                            other_out(g5).start()

                    @pl.when(mine(g5) & jnp.logical_not(late_owns(g5)))
                    def _():
                        c_part(g5).wait_recv()
                        c_back(g5).start()
                        if N > 2:

                            @pl.when(not_end)
                            def _():
                                c_out(g5).start()

        def serve_range(begin, end):
            lax.fori_loop(begin, end, lambda s, _: (serve(s), 0)[1], 0)

        def leave(g):
            at = rows(group_at(g), 3 * SUB, 16)
            return pltpu.make_async_copy(res.at[at], o_gr.at[at], osem.at[g])

        def settle(begin, end):
            def step(g, _):
                @pl.when(jnp.logical_not(is_mid))
                def _():
                    @pl.when(is_end)
                    def _():
                        own_part(g).wait_recv()
                        other_part(g).wait_recv()

                    in_copy(g).wait_send()

                @pl.when(is_mid)
                def _():
                    mid_copy(g).wait_send()
                    blk_copy(g).wait_send()
                    own_part(g).wait_send()

                @pl.when(not_end)
                def _():
                    own_out(g).wait_send()
                    other_out(g).wait_send()

                ended = mine(g) & is_mid & late_owns(g)

                @pl.when(jnp.logical_not(ended))
                def _():
                    c_in(g).wait_send()

                @pl.when(ended)
                def _():
                    c_part(g).wait_send()

                @pl.when(mine(g))
                def _():
                    c_back(g).wait_send()

                @pl.when(mine(g) & not_end)
                def _():
                    c_out(g).wait_send()

                @pl.when(jnp.logical_not(mine(g)))
                def _():
                    c_part(g).wait_recv()

                leave(g).start()
                return 0

            lax.fori_loop(begin, end, step, 0)

        tail = [0]

        def serve_next(count):
            serve_range(tail[0], tail[0] + count)
            tail[0] += count

        def down_step(f, _):
            at = pl.ds(pl.multiple_of(f * 256, 256), 256)
            m.gsrc[rows(DOWN + f * 256, 256, 16), :] = dot_tn(m.act[:, at], m.cot[...]).astype(BF)
            return 0

        def up_step(f, _):
            at = pl.ds(pl.multiple_of(f * 256, 256), 256)
            m.gsrc[rows(UP + f * 256, 256, 16), :] = dot_tn(m.n2[:, at], m.gh[...]).astype(BF)
            return 0

        down_step(0, 0)
        serve_next(BEFORE[0])
        down_step(1, 0)
        down_step(2, 0)
        serve_next(BEFORE[1])
        lax.fori_loop(0, D // 256, up_step, 0)
        serve_next(BEFORE[2])

        def mlp_step(i, _):
            a, e = lax.div(i, 2), lax.rem(i, 2)
            s = 2 * (y + a - 2 * y * a) + (c + e - 2 * c * e)
            m.proj[i] = dot_nn(m.act[rows(s * H, H, H), :], m.wdn[...]).astype(BF)
            return 0

        proj_copy(c).wait_send()
        proj_copy(2 + c).wait_send()
        lax.fori_loop(0, 4, mlp_step, 0)
        mp_copies = [send(m.proj.at[2 * j + 1], m.rsc.at[j], core) for j in range(2)]
        serve_next(BEFORE[3])

        gp_copies[0].wait_recv()
        gp_y.wait_recv()

        def grad_middle_step(i, gain):
            at = rows(i * 64, 64, 64)
            grad = m.gp[0, at, :].astype(F32) + m.rsc2[0, at, :].astype(F32)
            grad = grad + m.rsy2[at, :].astype(F32)
            full, r = full_of(m.mid[at, :].astype(F32))
            back = crms_back(grad, full, r, m.gbuf[1, :1, :])
            mine = rows(t * H + i * 64, 64, 64)
            m.gm[mine, :] = (m.cot[mine, :].astype(F32) + back).astype(BF)
            return gain + jnp.sum(grad * full * r, axis=0, keepdims=True)

        gain_two = lax.fori_loop(0, H // 64, grad_middle_step, jnp.zeros((1, D), F32))
        m.sm[0, 1:2, :] = gain_two
        gm_y = send(m.gm.at[here], m.gm.at[here], ydev)
        gm_core = send(m.gm.at[here], m.gm.at[here], core)
        gm_x = link(m.gm.at[here], m.gother, xdev)

        @pl.when(x == 1)
        def _():
            gm_x.start()

        serve_next(BEFORE[4])
        part = m.gm.at[rows(t2 * H, H, H)]
        gm_fwd = link(part, part, core)
        mp_y = link(m.ysnd, m.rsy, ydev)
        pending.extend((gm_fwd, mp_y))
        gm_core.wait_recv()

        def far_gradient():
            gm_y.wait_recv()
            gm_fwd.start()
            mp_copies[1].wait_recv()
            y_proj.wait_send()
            add_rows(m.ysnd, (m.proj.at[2], m.rsc.at[1]), H)
            mp_y.start()
            gm_fwd.wait_recv()
            m.gsrc[OUT : OUT + AW, :] = dot_tn(m.att[...], m.gm[...]).astype(BF)

        m.dkt[...] = jnp.zeros_like(m.dkt)
        m.dvt[...] = jnp.zeros_like(m.dvt)
        m.gq[...] = jnp.zeros_like(m.gq)

        C_GN = counter[0]
        counter[0] += 2

        def pair_rows(j):
            return rows(j * R, R, R)

        def gn_copy(j):
            return link(m.gh.at[pair_rows(j)], m.rscf.at[j], core, C_GN + j, C_GN + j)

        C_YF = counter[0]
        counter[0] += 4
        chunk = R // 4

        def yf_copy(k):
            src = m.act.at[rows((1 - y) * R + k * chunk, chunk, chunk)]
            dst = m.rsyf.at[rows(k * chunk, chunk, chunk)]
            return link(src, dst, ydev, C_YF + k, C_YF + k)

        def send_far():
            gn_copy(1 - y).wait_recv()

            def step(k, _):
                def inside(i, _):
                    r0 = k * chunk + i * 64
                    at = rows((1 - y) * R + r0, 64, 64)
                    both = m.act[at, :].astype(F32) + m.rscf[1 - y, rows(r0, 64, 64), :].astype(F32)
                    m.act[at, :] = both.astype(BF)
                    return 0

                lax.fori_loop(0, chunk // 64, inside, 0)
                yf_copy(k).start()
                return 0

            lax.fori_loop(0, 4, step, 0)

        BACK = sum(BEFORE)

        def back_block(i, _):
            g = jnp.where(i < 2, y, 1 - y)
            b = 2 * g + 1 - lax.rem(i, 2)
            pl.when(i == 2)(far_gradient)
            at = rows(b * H, H, H)
            mine = rows(b * R + xh, H, H)
            grad_att = dot_nt(m.gm[at, :], m.wao[...])
            outs, offs, out_ts, q_ts = [], [], [], []
            for h in range(NH):
                cols = slice(h * HS, (h + 1) * HS)
                inverse = m.il[at, h : h + 1]
                out = grad_att[:, cols].astype(BF).astype(F32)
                delta = total(out * m.att[at, cols].astype(F32))
                offs.append(delta * inverse)
                out = (out * inverse).astype(BF)
                outs.append(out)
                out_ts.append(jnp.transpose(out))
                q_ts.append(jnp.transpose(m.q[h, mine, :]))

            def keys(kb, grads):
                new = []
                for h in range(NH):
                    e = m.e[unit(b, kb) * NH + h]
                    at_k = rows(kb * R, R, R)
                    dp = dot_nt(outs[h], m.v[h, at_k, :])
                    ds = (e.astype(F32) * (dp - offs[h])).astype(BF)
                    new.append(grads[h] + dot_nn(ds, m.k[h, at_k, :]))
                    m.dkt[kb, h] += dot_nn(q_ts[h], ds)
                    m.dvt[kb, h] += dot_nn(out_ts[h], e)
                serve_range(BACK + lax.div(WITHIN * (done + kb), 10), BACK + lax.div(WITHIN * (done + kb + 1), 10))
                return tuple(new)

            done = jnp.where(y == 1, 4 * i - lax.div(i * (i - 1), 2), jnp.where(i < 2, 2 * i, 4 * i - 5))
            grads = lax.fori_loop(0, b + 1, keys, (jnp.zeros((H, HS), F32),) * NH)
            for h in range(NH):
                grad_q = jnp.transpose(grads[h] * HS**-0.5).astype(BF)
                m.dqt[b, h * HS : (h + 1) * HS, :] = grad_q
            pl.when((i == 3) & (c == 1))(send_far)
            begin = jnp.where(y == 1, i, jnp.where(i == 3, 1, 0))
            end = jnp.where(y == 1, i + 1, jnp.where(i == 3, 4, jnp.where(i == 2, 1, 0)))
            lax.fori_loop(begin, end, block_done, 0)
            return 0

        def block_done(f, _):
            b = 3 - f
            for h in range(NH):
                base = 3 * h * HS
                m.dmt[base : base + HS, rows(xh, H, H)] = m.dqt[b, h * HS : (h + 1) * HS, :]
                m.dmt[base : base + HS, rows(oh, H, H)] = jnp.zeros((HS, H), BF)
                m.dmt[base + HS : base + 2 * HS, :] = m.dkt[b, h].astype(BF)
                m.dmt[base + 2 * HS : base + 3 * HS, :] = m.dvt[b, h].astype(BF)
            m.gq[...] += dot_nn(m.dmt[...], m.normed[rows(b * R, R, R), :])
            back = dot_nn(jnp.transpose(m.dmt[...]), m.wqkv[...]).astype(BF)
            j = lax.div(b, 2)

            @pl.when(lax.rem(b, 2) == c)
            def _():
                m.act[pair_rows(j), :] = back

            @pl.when(lax.rem(b, 2) != c)
            def _():
                m.gh[pair_rows(j), :] = back
                gn_copy(j).start()

            pl.when((y == 0) & (c == 0) & (f == 2))(send_far)
            return 0

        lax.fori_loop(0, 4, back_block, 0)
        pl.when((y == 1) & (c == 0))(send_far)
        m.gsrc[QKV : QKV + QW, :] = m.gq[...].astype(BF)
        tail[0] = BACK + WITHIN
        mp_copies[0].wait_recv()
        mp_y.wait_recv()
        n2_y.wait_send()
        n2_core.wait_send()
        add_rows(m.n2.at[here], (m.mid, m.proj.at[0], m.rsc.at[0], m.rsy), H)
        bo_x = link(m.n2.at[here], m.gother, xdev)

        @pl.when(x == 0)
        def _():
            bo_x.start()

        serve_next(2)

        gn_copy(y).wait_recv()

        C_XF = counter[0]
        counter[0] += 4

        def xf_copy(k):
            src = m.act.at[rows(y * R + k * chunk, chunk, chunk)]
            dst = m.rsxf.at[rows(k * chunk, chunk, chunk)]
            return link(src, dst, xdev, C_XF + k, C_XF + k)

        def near_sum(k):
            yf_copy(k).wait_recv()

            def inside(i, _):
                r0 = k * chunk + i * 64
                at = rows(y * R + r0, 64, 64)
                here_rows = rows(r0, 64, 64)
                both = m.act[at, :].astype(F32) + m.rscf[y, here_rows, :].astype(F32)
                m.act[at, :] = (both + m.rsyf[here_rows, :].astype(F32)).astype(BF)
                return 0

            lax.fori_loop(0, chunk // 64, inside, 0)

        first = tail[0]
        tail[0] += 2

        def near_step(k, _):
            serve_range(first + lax.div(k, 2), first + lax.div(k + 1, 2))
            near_sum(k)

            @pl.when(x == 1)
            def _():
                xf_copy(k).start()

            return 0

        lax.fori_loop(0, 4, near_step, 0)
        m.sm[0, 0:1, :] = jnp.zeros((1, D), F32)
        then = tail[0]
        tail[0] += 2

        def grad_in_step(k, _):
            serve_range(then + lax.div(k, 2), then + lax.div(k + 1, 2))

            @pl.when(x == 0)
            def _():
                xf_copy(k).wait_recv()

                def inside(i, gain):
                    r0 = k * chunk + i * 64
                    here_rows = rows(r0, 64, 64)
                    grad = m.act[rows(y * R + r0, 64, 64), :].astype(F32)
                    grad = grad + m.rsxf[here_rows, :].astype(F32)
                    full, r = full_of(m.n1[rows(t * R + r0, 64, 64), :].astype(F32))
                    back = crms_back(grad, full, r, m.gbuf[0, :1, :])
                    m.rsyf[here_rows, :] = back.astype(BF)
                    return gain + jnp.sum(grad * full * r, axis=0, keepdims=True)

                gain = lax.fori_loop(0, chunk // 64, inside, jnp.zeros((1, D), F32))
                m.sm[0, 0:1, :] += gain

            return 0

        lax.fori_loop(0, 4, grad_in_step, 0)

        @pl.when(x == 0)
        def _():
            gm_x.wait_recv()

            def out_step(i, _):
                at = rows(i * 64, 64, 64)
                one = m.gm[rows(t * H + i * 64, 64, 64), :].astype(F32) + m.rsyf[at, :].astype(F32)
                o_io[0, at, :] = one[:, :C].astype(BF)
                below = rows(H + i * 64, 64, 64)
                two = m.gother[at, :].astype(F32) + m.rsyf[below, :].astype(F32)
                o_io[0, below, :] = two[:, :C].astype(BF)
                return 0

            lax.fori_loop(0, H // 64, out_step, 0)

        @pl.when(x == 1)
        def _():
            bo_x.wait_recv()
            o_io[0, 0:H, :] = m.gother[:, :C]
            o_io[0, H:R, :] = m.n2[here, :C]

        for j, peer in enumerate((core, ydev, xdev)):
            copy = send(m.sm.at[j], m.smr.at[j], peer)
            serve_next(1)
            copy.wait_recv()
            m.sm[j + 1] = m.sm[j] + m.smr[j]
        z_copies = []
        for j in range(1, N):
            z_copies.append(send(m.sm.at[3], m.smz.at[j], (x, lax.rem(d + j, N), t)))
        settled = max(0, min(tail[0] - 5 * LAG - 1, GROUPS))
        settle(0, settled)
        serve_range(tail[0], GROUPS + 5 * LAG)
        everything = m.sm[3]
        for j in range(1, N):
            z_copies[j - 1].wait_recv()
            everything = everything + m.smz[j]
        o_sm[...] = jnp.zeros_like(o_sm)

        @pl.when(x == 0)
        def _():
            o_sm[0:1, :] = everything[0:1]

        @pl.when(x == 1)
        def _():
            o_sm[0:1, :] = everything[1:2]

        o_sm[1:2, :] = jnp.broadcast_to(
            jnp.sqrt(total(everything[2:3]) * (1.0 / (4 * R * N * D))), (1, D)
        )

        settle(settled, GROUPS)
        lax.fori_loop(0, GROUPS, lambda g, _: (leave(g).wait(), 0)[1], 0)
        waited = {id(n2_y), id(n2_core), id(y_proj)}
        for copy in pending:
            if id(copy) not in waited:
                copy.wait_send()
        for j in range(2):
            gn_copy(j).wait_send()
        for k in range(4):
            yf_copy(k).wait_send()

        @pl.when(x == 1)
        def _():
            gm_x.wait_send()
            for k in range(4):
                xf_copy(k).wait_send()

        @pl.when(x == 0)
        def _():
            bo_x.wait_send()

        assert counter[0] <= N_SEM

    return body, scratch_shapes, GRADS, (DOWN, UP, OUT, QKV)


def per_device(mesh):
    N = mesh.shape["dp"]
    assert mesh.shape["blk"] == 2 and mesh.shape["tensor"] == 4 and N % 2 == 0

    def run(stream_in, lengths, norm_gains, w_qkv, w_attn_out, w_up, w_down, cotangent):
        R, C = stream_in.shape
        D = norm_gains.shape[1]
        FF = w_up.shape[1]
        NH = w_qkv.shape[1] // (3 * HS)
        body, scratch, grad_rows, (DOWN, UP, OUT, QKV) = kernel_for(
            dict(R=R, H=R // 2, D=D, C=C, FF=FF, NH=NH, N=N)
        )
        vmem = pl.BlockSpec(memory_space=pltpu.VMEM)
        smem = pl.BlockSpec(memory_space=pltpu.SMEM)
        anywhere = pl.BlockSpec(memory_space=pl.ANY)
        block_io, grads, small = pl.pallas_call(
            body,
            out_shape=(
                jax.ShapeDtypeStruct((1, R, C), BF),
                jax.ShapeDtypeStruct((grad_rows, D), BF),
                jax.ShapeDtypeStruct((8, D), F32),
            ),
            in_specs=[smem, vmem] + [anywhere] * 6,
            out_specs=(vmem, anywhere, vmem),
            scratch_shapes=scratch,
            compiler_params=pltpu.CompilerParams(
                collective_id=0, has_side_effects=True, vmem_limit_bytes=63 << 20
            ),
        )(lengths, norm_gains, stream_in, cotangent, w_qkv.T, w_attn_out, w_up, w_down)

        QW, AW = grad_rows - QKV, QKV - OUT
        CUT = 192

        def spread(small_in, io_in, grads_in, gain, rms, io, qkv, out, up, down, *refs):
            held, io_held, wide, wide_up, wide_out, wide_down, isem, osem, csem = refs
            io_load = pltpu.make_async_copy(io_in, io_held, csem.at[0])
            io_copy = pltpu.make_async_copy(io_held, io, csem.at[1])

            def load(i):
                at = pl.ds(i * CUT, CUT)
                return pltpu.make_async_copy(grads_in.at[at], held.at[at], isem.at[i])

            for i in range(grad_rows // CUT):
                load(i).start()
            io_load.start()
            gain[...] = small_in[0:1, :]
            rms[0, 0] = jnp.max(small_in[1:2, :])
            stores = []
            for i in range(grad_rows // CUT):
                load(i).wait()
                at = i * CUT
                for first, ref, dst in (
                    (QKV, wide, qkv),
                    (OUT, wide_out, out),
                    (UP, wide_up, up),
                    (DOWN, wide_down, down),
                ):
                    if at >= first:
                        here = pl.ds(at - first, CUT)
                        ref[here, :] = held[at : at + CUT, : ref.shape[1]].astype(F32)
                        copy = pltpu.make_async_copy(ref.at[here], dst.at[here], osem.at[i])
                        break
                copy.start()
                stores.append(copy)
            io_load.wait()
            io_copy.start()
            for copy in stores:
                copy.wait()
            io_copy.wait()

        shapes = ((QW, D), (AW, C), (D, FF), (FF, C))
        cuts = grad_rows // CUT
        gain, rms, block_io, grad_qkv, grad_out, grad_up, grad_down = pl.pallas_call(
            spread,
            out_shape=(
                jax.ShapeDtypeStruct((1, D), F32),
                jax.ShapeDtypeStruct((1, 1), F32),
                jax.ShapeDtypeStruct((1, R, C), BF),
                *(jax.ShapeDtypeStruct(shape, F32) for shape in shapes),
            ),
            in_specs=[vmem, anywhere, anywhere],
            out_specs=(vmem, smem) + (anywhere,) * 5,
            scratch_shapes=[
                pltpu.VMEM((grad_rows, D), BF),
                pltpu.VMEM((1, R, C), BF),
                pltpu.VMEM((QW, D), F32),
                pltpu.VMEM((D, FF), F32),
                pltpu.VMEM((AW, C), F32),
                pltpu.VMEM((FF, C), F32),
                pltpu.SemaphoreType.DMA((cuts,)),
                pltpu.SemaphoreType.DMA((cuts,)),
                pltpu.SemaphoreType.DMA((2,)),
            ],
            compiler_params=pltpu.CompilerParams(vmem_limit_bytes=63 << 20),
        )(small, block_io, grads)
        return (block_io, gain, grad_qkv.T, grad_out, grad_up, grad_down, rms.reshape(()))

    return run


def solution(mesh):
    in_specs = (
        P(("dp", "tensor"), None),
        P("dp"),
        P("blk", None),
        P(None, "tensor"),
        P("tensor", None),
        P(None, "tensor"),
        P("tensor", None),
        P(("dp", "tensor"), None),
    )
    out_specs = (
        P("blk", ("dp", "tensor"), None),
        P("blk", None),
        P(None, "tensor"),
        P("tensor", None),
        P(None, "tensor"),
        P("tensor", None),
        P(),
    )
    return jax.shard_map(
        per_device(mesh), mesh=mesh, in_specs=in_specs, out_specs=out_specs, check_vma=False
    )
```

```python
from types import SimpleNamespace

import jax
import jax.numpy as jnp
from jax import lax
from jax.experimental import pallas as pl
from jax.experimental.pallas import tpu as pltpu
from jax.sharding import PartitionSpec as P

HS = 64
EPSILON = 1e-05
MASKED = -1e30
BF = jnp.bfloat16
F32 = jnp.float32
MESH = pl.DeviceIdType.MESH
SUB = 32
THIRD = 80
LAG = 2
BEFORE = (1, 2, 1, 1, 0)
WITHIN = 7
ROOT = 0.7978845608028654


def dot_nn(a, b):
    return jnp.dot(a, b, preferred_element_type=F32)


def dot_nt(a, b):
    return lax.dot_general(a, b, (((1,), (1,)), ((), ())), preferred_element_type=F32)


def dot_tn(a, b):
    return lax.dot_general(a, b, (((0,), (0,)), ((), ())), preferred_element_type=F32)


def rows(start, count, multiple):
    return pl.ds(pl.multiple_of(start, multiple), count)


def lane_groups(value):
    return [value[:, i : i + 128] for i in range(0, value.shape[1], 128)]


def kernel_for(sizes):
    R, H, D, C, FF, NH, N = (sizes[k] for k in ("R", "H", "D", "C", "FF", "NH", "N"))
    QW = NH * 3 * HS
    AW = NH * HS
    GRADS = 2 * D + AW + QW
    GROUPS = GRADS // (2 * SUB + THIRD)
    DOWN, UP, OUT, QKV = 0, FF, FF + D, FF + D + AW
    half_n = N // 2

    names = {}

    def scratch(name, shape, dtype):
        names[name] = pltpu.VMEM(shape, dtype)

    scratch("gbuf", (2, 8, D), F32)
    scratch("cot_in", (H, C), BF)
    scratch("wqkv", (QW, D), BF)
    scratch("wao_in", (AW, C), BF)
    scratch("wup", (D, FF), BF)
    scratch("wdn_in", (FF, C), BF)
    scratch("normed", (4 * R, D), BF)
    scratch("wao", (AW, D), BF)
    scratch("wdn", (FF, D), BF)
    scratch("n1", (4 * R, D), BF)
    scratch("q", (NH, 4 * R, HS), BF)
    scratch("k", (NH, 4 * R, HS), BF)
    scratch("v", (NH, 4 * R, 2 * HS), BF)
    scratch("e", (10 * NH, H, R), BF)
    scratch("il", (4 * H, 128), F32)
    scratch("att", (4 * H, AW), BF)
    scratch("proj", (4, H, D), BF)
    scratch("rsc", (2, H, D), BF)
    scratch("ysnd", (H, D), BF)
    scratch("rsy", (H, D), BF)
    scratch("mid", (H, D), BF)
    scratch("n2", (4 * H, D), BF)
    scratch("cot", (4 * H, D), BF)
    scratch("act", (4 * H, FF), BF)
    scratch("gh", (4 * H, FF), BF)
    scratch("gp", (4, H, D), BF)
    scratch("rsc2", (2, H, D), BF)
    scratch("ysnd2", (H, D), BF)
    scratch("rsy2", (H, D), BF)
    scratch("gm", (4 * H, D), BF)
    scratch("gother", (H, D), BF)
    scratch("dmt", (QW, R), BF)
    scratch("dqt", (4, AW, H), BF)
    scratch("dkt", (4, NH, HS, R), F32)
    scratch("dvt", (4, NH, HS, R), F32)
    scratch("gq", (QW, D), F32)
    scratch("rscf", (2, R, D), BF)
    scratch("rsyf", (R, D), BF)
    scratch("rsxf", (R, D), BF)
    scratch("gsrc", (GRADS, D), BF)
    scratch("res", (GRADS, D), BF)
    scratch("gb", (GROUPS * SUB + -(-GROUPS // 4) * THIRD, D), BF)
    scratch("gc", (GROUPS * SUB + -(-GROUPS // 2) * THIRD, D), BF)
    scratch("sm", (5, 8, D), F32)
    scratch("smr", (3, 8, D), F32)
    scratch("smz", (N, 8, D), F32)
    n_vmem = len(names)
    N_SEM = 10 * GROUPS + 64 + N
    scratch_shapes = list(names.values()) + [
        pltpu.SemaphoreType.DMA((N_SEM,)),
        pltpu.SemaphoreType.DMA((N_SEM,)),
        pltpu.SemaphoreType.DMA((6,)),
        pltpu.SemaphoreType.DMA((GROUPS,)),
    ]

    def body(
        lens, gains, stream, cot_in, w_qkv, w_ao, w_up, w_dn, o_io, o_gr, o_sm, *refs
    ):
        m = SimpleNamespace(**dict(zip(names, refs[:n_vmem], strict=True)))
        ssem, rsem, lsem, osem = refs[n_vmem:]
        res = m.res
        x = lax.axis_index("blk")
        d = lax.axis_index("dp")
        t = lax.axis_index("tensor")
        y = lax.div(t, 2)
        c = lax.rem(t, 2)
        t1 = 2 * y + 1 - c
        t2 = 2 * (1 - y) + c
        t3 = 2 * (1 - y) + 1 - c
        core, ydev, xdev = (x, d, t1), (x, d, t2), (1 - x, d, t)
        xh, oh = x * H, (1 - x) * H

        counter = [10 * GROUPS]
        pending = []

        def link(src, dst, dev, s_idx=None, r_idx=None):
            if s_idx is None:
                s_idx = r_idx = counter[0]
                counter[0] += 1
            return pltpu.make_async_remote_copy(
                src_ref=src,
                dst_ref=dst,
                send_sem=ssem.at[s_idx],
                recv_sem=rsem.at[r_idx],
                device_id=dev,
                device_id_type=MESH,
            )

        def send(src, dst, dev):
            copy = link(src, dst, dev)
            copy.start()
            pending.append(copy)
            return copy

        loads = []
        for i, (src, dst) in enumerate(
            (
                (stream, o_io.at[0]),
                (w_qkv, m.wqkv),
                (cot_in.at[rows(xh, H, H)], m.cot_in),
                (w_ao, m.wao_in),
                (w_up, m.wup),
                (w_dn, m.wdn_in),
            )
        ):
            loads.append(pltpu.make_async_copy(src, dst, lsem.at[i]))
            loads[-1].start()

        barrier = pltpu.get_barrier_semaphore()
        for peer in (core, ydev, xdev):
            pl.semaphore_signal(barrier, inc=1, device_id=peer, device_id_type=MESH)
        for j in range(1, N):
            pl.semaphore_signal(
                barrier,
                inc=1,
                device_id=(x, lax.rem(d + j, N), t),
                device_id_type=MESH,
            )
        pl.semaphore_wait(barrier, 3 + N - 1)

        lane = lax.broadcasted_iota(jnp.int32, (1, D), 1)
        last = lane == D - 1

        def total(value):
            return jnp.sum(value, axis=1, keepdims=True)

        def full_of(stream_rows):
            full = jnp.where(last, -total(stream_rows), stream_rows)
            return full, lax.rsqrt(total(full * full) * (1.0 / D) + EPSILON)

        def crms_back(grad, full, r, gain):
            a = grad * gain
            mean = total(a * full) * (1.0 / D)
            df = r * (a - full * (r * r * mean))
            tail = total(jnp.where(last, df, 0.0))
            return jnp.where(last, 0.0, df - tail)

        m.gbuf[x] = jnp.broadcast_to(gains[...], (8, D))
        gain_copy = send(m.gbuf.at[x], m.gbuf.at[x], xdev)
        loads[0].wait()
        own_rows = rows(t * R, R, R)
        m.n1[own_rows, D - 128 :] = jnp.zeros((R, 128), BF)
        m.n1[own_rows, :C] = o_io[0]
        here = rows(t * H, H, H)

        half = H // 4
        y_copies = []
        for k in range(4):
            part = m.n1.at[rows(t * R + xh + k * half, half, half)]
            y_copies.append(send(part, part, ydev))
        part = m.n1.at[rows(t * R, R, R)]
        own_copy = send(part, part, core)
        loads[2].wait()
        m.cot[here, D - 128 :] = jnp.zeros((H, 128), BF)
        m.cot[here, :C] = m.cot_in[...]
        part = m.cot.at[here]
        cot_core = send(part, part, core)

        def turned(kb, h):
            return rows((kb * NH + h) * HS, HS, HS)

        def qkv_rows(start):
            def step(i, _):
                some = rows(start + i * 64, 64, 64)
                full, r = full_of(m.n1[some, :].astype(F32))
                m.normed[some, :] = (full * r * m.gbuf[0, :1, :]).astype(BF)
                return 0

            lax.fori_loop(0, H // 64, step, 0)
            mixed = dot_nt(m.normed[rows(start, H, H), :], m.wqkv[...])
            at = rows(start, H, H)
            for h in range(NH):
                for p, ref in enumerate((m.q, m.k, m.v)):
                    part = mixed[:, (3 * h + p) * HS : (3 * h + p + 1) * HS]
                    if p == 0:
                        part = part * HS**-0.5
                    part = part.astype(BF)
                    if p == 2:
                        ref[h, at, :HS] = part
                        ref[h, at, HS:] = jnp.ones((H, HS), BF)
                    else:
                        ref[h, at, :] = part
                    if p == 1:
                        within = rows(lax.rem(start, R), H, H)
                        m.act[turned(lax.div(start, R), h), within] = jnp.transpose(part)

        def qkv_block(block):
            lax.fori_loop(0, 2, lambda i, _: (qkv_rows(block * R + i * H), 0)[1], 0)

        loads[1].wait()
        gain_copy.wait_recv()
        qkv_block(t)
        own_copy.wait_recv()
        qkv_block(t1)
        for load in loads[3:]:
            load.wait()
        m.wao[:, D - 128 :] = jnp.zeros((AW, 128), BF)
        m.wao[:, :C] = m.wao_in[...]
        m.wdn[:, D - 128 :] = jnp.zeros((FF, 128), BF)
        m.wdn[:, :C] = m.wdn_in[...]
        fwd = []
        x_copies = []
        for k in range(4):
            y_copies[k].wait_recv()
            part = m.n1.at[rows(t2 * R + xh + k * half, half, half)]
            x_copies.append(send(part, part, xdev))
            fwd.append(send(part, part, core))
        part = m.cot.at[here]
        cot_y = send(part, part, ydev)
        qkv_rows(t2 * R + xh)
        for copy in fwd:
            copy.wait_recv()
        qkv_rows(t3 * R + xh)
        passed = x_copies + fwd
        fwd = []
        for k in range(4):
            x_copies[k].wait_recv()
            part = m.n1.at[rows(t2 * R + oh + k * half, half, half)]
            fwd.append(send(part, part, core))
        qkv_rows(t2 * R + oh)
        for copy in fwd:
            copy.wait_recv()
        qkv_rows(t3 * R + oh)
        passed += fwd

        ends = [lens[0]]
        for i in range(1, 4):
            ends.append(ends[-1] + lens[i])

        def bias_of(b, kb):
            cut = (ends[0] > kb * R) & (ends[0] <= b * R)
            for e in ends[1:]:
                cut = cut | ((e > kb * R) & (e <= b * R))
            return jnp.where(cut, MASKED, 0.0).astype(F32)

        row_at = lax.broadcasted_iota(jnp.int32, (H, R), 0)
        col_at = lax.broadcasted_iota(jnp.int32, (H, R), 1)

        def unit(b, kb):
            return lax.div(b * (b + 1), 2) + kb

        def attend(b, between):
            mine = rows(b * R + xh, H, H)
            heads = [m.q[h, mine, :] for h in range(NH)]

            def scores(h, kb):
                return dot_nn(heads[h], m.act[turned(kb, h), :R])

            def top(s, best):
                for g in lane_groups(s):
                    best = jnp.maximum(best, g)
                return best

            def masked(s):
                return jnp.where(col_at <= row_at + xh, s, MASKED)

            def peak(kb, best):
                bias = bias_of(b, kb)
                low = jnp.full((H, 128), -jnp.inf, F32)
                return tuple(
                    jnp.maximum(best[h], top(scores(h, kb), low) + bias) for h in range(NH)
                )

            low = jnp.full((H, 128), MASKED, F32)
            best = tuple(top(masked(scores(h, b)), low) for h in range(NH))
            best = lax.fori_loop(0, b, peak, best)
            best = [jnp.max(v, axis=1, keepdims=True) for v in best]
            between()

            def weigh(h, kb, s, off, acc):
                e = jnp.exp(s - off).astype(BF)
                m.e[unit(b, kb) * NH + h] = e
                return acc + dot_nn(e, m.v[h, rows(kb * R, R, R), :])

            def add(kb, carry):
                bias = bias_of(b, kb)
                return tuple(
                    weigh(h, kb, scores(h, kb), best[h] - bias, carry[h]) for h in range(NH)
                )

            zero = jnp.zeros((H, 2 * HS), F32)
            carry = tuple(weigh(h, b, masked(scores(h, b)), best[h], zero) for h in range(NH))
            carry = lax.fori_loop(0, b, add, carry)
            at = rows(b * H, H, H)
            for h in range(NH):
                inverse = 1.0 / carry[h][:, HS : HS + 1]
                m.il[at, h : h + 1] = inverse
                m.att[at, h * HS : (h + 1) * HS] = (carry[h][:, :HS] * inverse).astype(BF)
            return dot_nn(m.att[at, :], m.wao[...]).astype(BF)

        C_PROJ = counter[0]
        counter[0] += 2

        def proj_copy(i):
            j = lax.div(i, 2)
            return link(m.proj.at[i], m.rsc.at[j], core, C_PROJ + j, C_PROJ + j)

        def add_rows(out, terms, count):
            def step(i, _):
                at = rows(i * 64, 64, 64)
                out[at, :] = sum(ref[at, :].astype(F32) for ref in terms).astype(BF)
                return 0

            lax.fori_loop(0, count // 64, step, 0)

        y_proj = link(m.ysnd, m.rsy, ydev)
        pending.append(y_proj)

        def attend_step(i, _):
            a, e = lax.div(i, 2), 1 - lax.rem(i, 2)
            g = (1 - y) * (1 - a) + y * a

            def between():
                @pl.when(i == 2 - c)
                def _():
                    proj_copy(c).wait_recv()
                    add_rows(m.ysnd, (m.proj.at[1 - c], m.rsc.at[0]), H)
                    y_proj.start()

            m.proj[i] = attend(2 * g + e, between)

            @pl.when(lax.rem(i, 2) == c)
            def _():
                proj_copy(i).start()

            return 0

        lax.fori_loop(0, 4, attend_step, 0)
        proj_copy(2 + c).wait_recv()
        cot_core.wait_recv()
        cot_y.wait_recv()
        part = m.cot.at[rows(t2 * H, H, H)]
        cot_fwd = send(part, part, core)
        y_proj.wait_recv()

        def middle_step(i, squares):
            at = rows(i * 64, 64, 64)
            mid = m.n1[rows(t * R + xh + i * 64, 64, 64), :].astype(F32)
            mid = mid + m.proj[2 + 1 - c, at, :].astype(F32)
            mid = mid + m.rsc[1, at, :].astype(F32) + m.rsy[at, :].astype(F32)
            mid = mid.astype(BF)
            m.mid[at, :] = mid
            full, r = full_of(mid.astype(F32))
            m.n2[rows(t * H + i * 64, 64, 64), :] = (full * r * m.gbuf[1, :1, :]).astype(BF)
            return squares + jnp.sum(full * full, axis=0, keepdims=True)

        squares = lax.fori_loop(0, H // 64, middle_step, jnp.zeros((1, D), F32))
        m.sm[0] = jnp.zeros((8, D), F32)
        m.sm[0, 2:3, :] = squares

        C_N2Y = counter[0]
        counter[0] += 6
        side_rows = H // 2

        def n2y_copy(k):
            part = m.n2.at[rows(t * H + k * side_rows, side_rows, side_rows)]
            return link(part, part, ydev, C_N2Y + k, C_N2Y + k)

        n2y_copy(0).start()
        n2y_copy(1).start()
        n2_core = send(m.n2.at[here], m.n2.at[here], core)

        def feed(start, count, i, to):
            at = rows(start, count, count)
            for f in range(FF // 256):
                cols = slice(f * 256, (f + 1) * 256)
                hidden = dot_nn(m.n2[at, :], m.wup[:, cols])
                grad = dot_nt(m.cot[at, :], m.wdn[cols, :])
                square = hidden * hidden
                bent = jnp.tanh(ROOT * hidden * (1.0 + 0.044715 * square))
                gate = 0.5 * (1.0 + bent)
                m.act[at, cols] = (hidden * gate).astype(BF)
                slope = gate + (0.5 * ROOT) * hidden * (1.0 - bent * bent) * (
                    1.0 + (3 * 0.044715) * square
                )
                m.gh[at, cols] = (grad * slope).astype(BF)
            m.gp[i, rows(to, count, count), :] = dot_nt(m.gh[at, :], m.wup[...]).astype(BF)

        gp_near = link(m.gp.at[1], m.rsc2.at[0], core)
        pending.append(gp_near)

        def n2f_copy(k):
            part = m.n2.at[rows(t2 * H + k * side_rows, side_rows, side_rows)]
            return link(part, part, core, C_N2Y + 2 + k, C_N2Y + 2 + k)

        def gp3_copy(k):
            at = rows(k * side_rows, side_rows, side_rows)
            return link(m.gp.at[3, at], m.rsc2.at[1, at], core, C_N2Y + 4 + k, C_N2Y + 4 + k)

        C_GPY = counter[0]
        counter[0] += 2

        def gpy_copy(k):
            at = rows(k * side_rows, side_rows, side_rows)
            return link(m.ysnd2.at[at], m.rsy2.at[at], ydev, C_GPY + k, C_GPY + k)

        def far_half(k):
            gp3_copy(k).wait_recv()
            at = rows(k * side_rows, side_rows, side_rows)
            add_rows(m.ysnd2.at[at], (m.gp.at[2, at], m.rsc2.at[1, at]), side_rows)
            gpy_copy(k).start()

        def near_feed(i, _):
            @pl.when(i == 1)
            def _():
                n2_core.wait_recv()

            feed((2 * y + c + i - 2 * c * i) * H, H, i, 0)
            return 0

        def far_feed(q, _):
            k, w = lax.div(q, 2), lax.rem(q, 2)

            @pl.when(w == 0)
            def _():
                n2y_copy(k).wait_recv()
                n2f_copy(k).start()

            @pl.when(q == 0)
            def _():
                cot_fwd.wait_recv()

            @pl.when(w == 1)
            def _():
                n2f_copy(k).wait_recv()

            @pl.when(q == 3)
            def _():
                far_half(0)

            s = 2 * (1 - y) + c + w - 2 * c * w
            feed(s * H + k * side_rows, side_rows, 2 + w, k * side_rows)

            @pl.when(w == 1)
            def _():
                gp3_copy(k).start()

            return 0

        lax.fori_loop(0, 2, near_feed, 0)
        gp_near.start()
        lax.fori_loop(0, 4, far_feed, 0)
        far_half(1)

        is_mid = (d == half_n - 1) | (d == half_n)
        is_end = (d == 0) | (d == N - 1)
        side = jnp.where(d < half_n, 0, 1)
        step_in = 1 - 2 * side
        inner = (x, lax.rem(d + step_in + N, N), t)
        outer = (x, lax.rem(d - step_in + N, N), t)

        not_end = jnp.logical_not(is_end)

        def sub_rows(ref, at, count):
            return ref.at[rows(at, count * SUB, 16)]

        def third_rows(ref, at):
            return ref.at[rows(at, THIRD, 16)]

        def b_third(g):
            return third_rows(m.gb, GROUPS * SUB + lax.div(g, 4) * THIRD)

        def c_third(g):
            return third_rows(m.gc, GROUPS * SUB + lax.div(g, 2) * THIRD)

        def group_at(g):
            return g * (2 * SUB + THIRD)

        def third_at(g):
            return group_at(g) + 2 * SUB

        def sub_at(g, who):
            return group_at(g) + who * SUB

        def sem(kind, g):
            return kind * GROUPS + g

        def in_copy(g):
            at = group_at(g)
            return link(sub_rows(m.gsrc, at, 2), sub_rows(res, at, 2), inner, sem(0, g), sem(0, g))

        def mid_copy(g):
            src = sub_rows(m.gsrc, sub_at(g, 1 - side), 1)
            return link(src, sub_rows(m.gb, g * SUB, 1), inner, sem(1, g), sem(1, g))

        def blk_copy(g):
            src = sub_rows(m.gsrc, sub_at(g, side), 1)
            return link(src, sub_rows(m.gc, g * SUB, 1), xdev, sem(2, g), sem(2, g))

        def res_link(g, who, dev, kind):
            at = sub_rows(res, sub_at(g, who), 1)
            return link(at, at, dev, sem(kind, g), sem(3, g) + GROUPS * who)

        def own_part(g):
            return res_link(g, side, inner, 3)

        def own_out(g):
            return res_link(g, side, outer, 4)

        def other_part(g):
            return res_link(g, 1 - side, inner, 3)

        def other_out(g):
            return res_link(g, 1 - side, outer, 5)

        def c_link(dst, dev, kind):
            def make(g):
                src = third_rows(m.gsrc, third_at(g))
                return link(src, dst(g), dev, sem(6, g), sem(kind, g))

            return make

        def c_res(dev, kind):
            def make(g):
                at = third_rows(res, third_at(g))
                return link(at, at, dev, sem(kind, g), sem(8, g))

            return make

        c_blk = c_link(c_third, xdev, 5)
        c_in = c_link(lambda g: third_rows(res, third_at(g)), inner, 6)
        c_mid = c_link(b_third, inner, 7)
        c_part, c_out, c_back = c_res(inner, 7), c_res(outer, 8), c_res(xdev, 9)

        def add(out, at, other, count):
            for k in range(count):
                here_rows = rows(at + k * SUB, SUB, 16)
                there = other[k * SUB : (k + 1) * SUB, :].astype(F32)
                out[here_rows, :] = (m.gsrc[here_rows, :].astype(F32) + there).astype(BF)

        def add_third(out, g, other):
            here_rows = rows(third_at(g), THIRD, 16)
            both = m.gsrc[here_rows, :].astype(F32) + other[...].astype(F32)
            out[here_rows, :] = both.astype(BF)

        def valid(g):
            return (g >= 0) & (g < GROUPS)

        def mine(g):
            return x == lax.rem(g + 2 * GROUPS, 2)

        def late_owns(g):
            return side == lax.rem(lax.div(g + 4 * GROUPS, 2), 2)

        def serve(s):
            g1, g2, g3, g4, g5, g6 = (s - i * LAG for i in range(6))

            @pl.when(valid(g1) & jnp.logical_not(mine(g1)))
            def _():
                c_blk(g1).start()

            @pl.when(jnp.logical_not(is_mid))
            def _():
                @pl.when(valid(g1))
                def _():
                    if N > 4:

                        @pl.when(not_end)
                        def _():
                            in_copy(g1).wait_recv()
                            add(m.gsrc, group_at(g1), sub_rows(res, group_at(g1), 2), 2)

                    in_copy(g1).start()

                @pl.when(valid(g2) & mine(g2))
                def _():
                    c_blk(g2).wait_recv()
                    add_third(m.gsrc, g2, c_third(g2))
                    if N > 4:

                        @pl.when(not_end)
                        def _():
                            c_in(g2).wait_recv()
                            add_third(m.gsrc, g2, third_rows(res, third_at(g2)))

                    c_in(g2).start()

                @pl.when(valid(g6))
                def _():
                    if N > 4:

                        @pl.when(not_end)
                        def _():
                            own_out(g6).wait_recv()
                            own_out(g6).start()
                            other_out(g6).wait_recv()
                            other_out(g6).start()

                    @pl.when(mine(g6))
                    def _():
                        c_part(g6).wait_recv()
                        c_back(g6).start()
                        if N > 4:

                            @pl.when(not_end)
                            def _():
                                c_out(g6).start()

            @pl.when(is_mid)
            def _():
                @pl.when(valid(g2))
                def _():
                    if N > 2:

                        @pl.when(not_end)
                        def _():
                            in_copy(g2).wait_recv()
                            add(m.gsrc, group_at(g2), sub_rows(res, group_at(g2), 2), 2)

                    mid_copy(g2).start()

                    @pl.when(mine(g2))
                    def _():
                        c_blk(g2).wait_recv()
                        add_third(m.gsrc, g2, c_third(g2))

                @pl.when(valid(g3))
                def _():
                    mid_copy(g3).wait_recv()
                    add(m.gsrc, sub_at(g3, side), sub_rows(m.gb, g3 * SUB, 1), 1)
                    blk_copy(g3).start()

                    @pl.when(mine(g3))
                    def _():
                        if N > 2:

                            @pl.when(not_end)
                            def _():
                                c_in(g3).wait_recv()
                                add_third(m.gsrc, g3, third_rows(res, third_at(g3)))

                        @pl.when(jnp.logical_not(late_owns(g3)))
                        def _():
                            c_mid(g3).start()

                @pl.when(valid(g4))
                def _():
                    blk_copy(g4).wait_recv()
                    add(res, sub_at(g4, side), sub_rows(m.gc, g4 * SUB, 1), 1)
                    own_part(g4).start()
                    if N > 2:

                        @pl.when(not_end)
                        def _():
                            own_out(g4).start()

                    @pl.when(mine(g4) & late_owns(g4))
                    def _():
                        c_mid(g4).wait_recv()
                        add_third(res, g4, b_third(g4))
                        c_part(g4).start()
                        c_back(g4).start()
                        if N > 2:

                            @pl.when(not_end)
                            def _():
                                c_out(g4).start()

                @pl.when(valid(g5))
                def _():
                    other_part(g5).wait_recv()
                    if N > 2:

                        @pl.when(not_end)
                        def _():
                            other_out(g5).start()

                    @pl.when(mine(g5) & jnp.logical_not(late_owns(g5)))
                    def _():
                        c_part(g5).wait_recv()
                        c_back(g5).start()
                        if N > 2:

                            @pl.when(not_end)
                            def _():
                                c_out(g5).start()

        def serve_range(begin, end):
            lax.fori_loop(begin, end, lambda s, _: (serve(s), 0)[1], 0)

        def leave(g):
            at = rows(group_at(g), 2 * SUB + THIRD, 16)
            return pltpu.make_async_copy(res.at[at], o_gr.at[at], osem.at[g])

        def settle(begin, end):
            def step(g, _):
                @pl.when(jnp.logical_not(is_mid))
                def _():
                    @pl.when(is_end)
                    def _():
                        own_part(g).wait_recv()
                        other_part(g).wait_recv()

                    in_copy(g).wait_send()

                @pl.when(is_mid)
                def _():
                    mid_copy(g).wait_send()
                    blk_copy(g).wait_send()
                    own_part(g).wait_send()

                @pl.when(not_end)
                def _():
                    own_out(g).wait_send()
                    other_out(g).wait_send()

                ended = mine(g) & is_mid & late_owns(g)

                @pl.when(jnp.logical_not(ended))
                def _():
                    c_in(g).wait_send()

                @pl.when(ended)
                def _():
                    c_part(g).wait_send()

                @pl.when(mine(g))
                def _():
                    c_back(g).wait_send()

                @pl.when(mine(g) & not_end)
                def _():
                    c_out(g).wait_send()

                @pl.when(jnp.logical_not(mine(g)))
                def _():
                    c_part(g).wait_recv()

                leave(g).start()
                return 0

            lax.fori_loop(begin, end, step, 0)

        tail = [0]

        def serve_next(count):
            serve_range(tail[0], tail[0] + count)
            tail[0] += count

        def down_step(f, _):
            at = pl.ds(pl.multiple_of(f * 256, 256), 256)
            m.gsrc[rows(DOWN + f * 256, 256, 16), :] = dot_tn(m.act[:, at], m.cot[...]).astype(BF)
            return 0

        def up_step(f, _):
            at = pl.ds(pl.multiple_of(f * 256, 256), 256)
            m.gsrc[rows(UP + f * 256, 256, 16), :] = dot_tn(m.n2[:, at], m.gh[...]).astype(BF)
            return 0

        down_step(0, 0)
        serve_next(BEFORE[0])
        down_step(1, 0)
        down_step(2, 0)
        serve_next(BEFORE[1])
        lax.fori_loop(0, D // 256, up_step, 0)
        serve_next(BEFORE[2])

        def mlp_step(i, _):
            a, e = lax.div(i, 2), lax.rem(i, 2)
            s = 2 * (y + a - 2 * y * a) + (c + e - 2 * c * e)
            m.proj[i] = dot_nn(m.act[rows(s * H, H, H), :], m.wdn[...]).astype(BF)
            return 0

        proj_copy(c).wait_send()
        proj_copy(2 + c).wait_send()
        lax.fori_loop(0, 4, mlp_step, 0)
        mp_copies = [send(m.proj.at[2 * j + 1], m.rsc.at[j], core) for j in range(2)]
        serve_next(BEFORE[3])

        gp_near.wait_recv()
        gpy_copy(0).wait_recv()
        gpy_copy(1).wait_recv()

        def grad_middle_step(i, gain):
            at = rows(i * 64, 64, 64)
            grad = m.gp[0, at, :].astype(F32) + m.rsc2[0, at, :].astype(F32)
            grad = grad + m.rsy2[at, :].astype(F32)
            full, r = full_of(m.mid[at, :].astype(F32))
            back = crms_back(grad, full, r, m.gbuf[1, :1, :])
            mine = rows(t * H + i * 64, 64, 64)
            m.gm[mine, :] = (m.cot[mine, :].astype(F32) + back).astype(BF)
            return gain + jnp.sum(grad * full * r, axis=0, keepdims=True)

        gain_two = lax.fori_loop(0, H // 64, grad_middle_step, jnp.zeros((1, D), F32))
        m.sm[0, 1:2, :] = gain_two
        gm_y = send(m.gm.at[here], m.gm.at[here], ydev)
        gm_core = send(m.gm.at[here], m.gm.at[here], core)
        gm_x = link(m.gm.at[here], m.gother, xdev)

        @pl.when(x == 1)
        def _():
            gm_x.start()

        serve_next(BEFORE[4])
        part = m.gm.at[rows(t2 * H, H, H)]
        gm_fwd = link(part, part, core)
        mp_y = link(m.ysnd, m.rsy, ydev)
        pending.extend((gm_fwd, mp_y))
        gm_core.wait_recv()

        def far_turned(kb, h):
            return rows(2 * R * (1 - y) + (kb * NH + h) * HS, HS, HS)

        def turn_values(i, _):
            kb = lax.div(i, NH)
            h = lax.rem(i, NH)
            m.n1[far_turned(kb, h), :R] = jnp.transpose(m.v[h, rows(kb * R, R, R), :HS])
            return 0

        for copy in passed:
            copy.wait_send()
        lax.fori_loop(0, 4 * NH, turn_values, 0)
        def far_gradient():
            gm_y.wait_recv()
            gm_fwd.start()
            mp_copies[1].wait_recv()
            y_proj.wait_send()
            add_rows(m.ysnd, (m.proj.at[2], m.rsc.at[1]), H)
            mp_y.start()
            gm_fwd.wait_recv()
            m.gsrc[OUT : OUT + AW, :] = dot_tn(m.att[...], m.gm[...]).astype(BF)

        m.dkt[...] = jnp.zeros_like(m.dkt)
        m.dvt[...] = jnp.zeros_like(m.dvt)
        m.gq[...] = jnp.zeros_like(m.gq)

        C_GN = counter[0]
        counter[0] += 2

        def pair_rows(j):
            return rows(j * R, R, R)

        def gn_copy(j):
            return link(m.gh.at[pair_rows(j)], m.rscf.at[j], core, C_GN + j, C_GN + j)

        C_YF = counter[0]
        counter[0] += 4
        chunk = R // 4

        def yf_copy(k):
            src = m.act.at[rows((1 - y) * R + k * chunk, chunk, chunk)]
            dst = m.rsyf.at[rows(k * chunk, chunk, chunk)]
            return link(src, dst, ydev, C_YF + k, C_YF + k)

        def send_far():
            gn_copy(1 - y).wait_recv()

            def step(k, _):
                def inside(i, _):
                    r0 = k * chunk + i * 64
                    at = rows((1 - y) * R + r0, 64, 64)
                    both = m.act[at, :].astype(F32) + m.rscf[1 - y, rows(r0, 64, 64), :].astype(F32)
                    m.act[at, :] = both.astype(BF)
                    return 0

                lax.fori_loop(0, chunk // 64, inside, 0)
                yf_copy(k).start()
                return 0

            lax.fori_loop(0, 4, step, 0)

        BACK = sum(BEFORE)

        def back_block(i, _):
            g = jnp.where(i < 2, y, 1 - y)
            b = 2 * g + 1 - lax.rem(i, 2)
            pl.when(i == 2)(far_gradient)
            at = rows(b * H, H, H)
            mine = rows(b * R + xh, H, H)
            grad_att = dot_nt(m.gm[at, :], m.wao[...])
            outs, offs, out_ts, q_ts = [], [], [], []
            for h in range(NH):
                cols = slice(h * HS, (h + 1) * HS)
                inverse = m.il[at, h : h + 1]
                out = grad_att[:, cols].astype(BF).astype(F32)
                delta = total(out * m.att[at, cols].astype(F32))
                offs.append(delta * inverse)
                out = (out * inverse).astype(BF)
                outs.append(out)
                out_ts.append(jnp.transpose(out))
                q_ts.append(jnp.transpose(m.q[h, mine, :]))

            def keys(kb, grads):
                new = []
                for h in range(NH):
                    e = m.e[unit(b, kb) * NH + h]
                    at_k = rows(kb * R, R, R)
                    dp = dot_nn(outs[h], m.n1[far_turned(kb, h), :R])
                    ds = (e.astype(F32) * (dp - offs[h])).astype(BF)
                    new.append(grads[h] + dot_nn(ds, m.k[h, at_k, :]))
                    m.dkt[kb, h] += dot_nn(q_ts[h], ds)
                    m.dvt[kb, h] += dot_nn(out_ts[h], e)
                serve_range(BACK + lax.div(WITHIN * (done + kb), 10), BACK + lax.div(WITHIN * (done + kb + 1), 10))
                return tuple(new)

            done = jnp.where(y == 1, 4 * i - lax.div(i * (i - 1), 2), jnp.where(i < 2, 2 * i, 4 * i - 5))
            grads = lax.fori_loop(0, b + 1, keys, (jnp.zeros((H, HS), F32),) * NH)
            for h in range(NH):
                grad_q = jnp.transpose(grads[h] * HS**-0.5).astype(BF)
                m.dqt[b, h * HS : (h + 1) * HS, :] = grad_q
            pl.when((i == 3) & (c == 1))(send_far)
            begin = jnp.where(y == 1, i, jnp.where(i == 3, 1, 0))
            end = jnp.where(y == 1, i + 1, jnp.where(i == 3, 4, jnp.where(i == 2, 1, 0)))
            lax.fori_loop(begin, end, block_done, 0)
            return 0

        def block_done(f, _):
            b = 3 - f
            for h in range(NH):
                base = 3 * h * HS
                m.dmt[base : base + HS, rows(xh, H, H)] = m.dqt[b, h * HS : (h + 1) * HS, :]
                m.dmt[base : base + HS, rows(oh, H, H)] = jnp.zeros((HS, H), BF)
                m.dmt[base + HS : base + 2 * HS, :] = m.dkt[b, h].astype(BF)
                m.dmt[base + 2 * HS : base + 3 * HS, :] = m.dvt[b, h].astype(BF)
            m.gq[...] += dot_nn(m.dmt[...], m.normed[rows(b * R, R, R), :])
            back = dot_nn(jnp.transpose(m.dmt[...]), m.wqkv[...]).astype(BF)
            j = lax.div(b, 2)

            @pl.when(lax.rem(b, 2) == c)
            def _():
                m.act[pair_rows(j), :] = back

            @pl.when(lax.rem(b, 2) != c)
            def _():
                m.gh[pair_rows(j), :] = back
                gn_copy(j).start()

            pl.when((y == 0) & (c == 0) & (f == 2))(send_far)
            return 0

        lax.fori_loop(0, 4, back_block, 0)
        pl.when((y == 1) & (c == 0))(send_far)
        m.gsrc[QKV : QKV + QW, :] = m.gq[...].astype(BF)
        tail[0] = BACK + WITHIN
        mp_copies[0].wait_recv()
        mp_y.wait_recv()
        n2y_copy(0).wait_send()
        n2y_copy(1).wait_send()
        n2_core.wait_send()
        add_rows(m.n2.at[here], (m.mid, m.proj.at[0], m.rsc.at[0], m.rsy), H)
        bo_x = link(m.n2.at[here], m.gother, xdev)

        @pl.when(x == 0)
        def _():
            bo_x.start()

        serve_next(2)

        gn_copy(y).wait_recv()

        C_XF = counter[0]
        counter[0] += 4

        def xf_copy(k):
            src = m.act.at[rows(y * R + k * chunk, chunk, chunk)]
            dst = m.rsxf.at[rows(k * chunk, chunk, chunk)]
            return link(src, dst, xdev, C_XF + k, C_XF + k)

        def near_sum(k):
            yf_copy(k).wait_recv()

            def inside(i, _):
                r0 = k * chunk + i * 64
                at = rows(y * R + r0, 64, 64)
                here_rows = rows(r0, 64, 64)
                both = m.act[at, :].astype(F32) + m.rscf[y, here_rows, :].astype(F32)
                m.act[at, :] = (both + m.rsyf[here_rows, :].astype(F32)).astype(BF)
                return 0

            lax.fori_loop(0, chunk // 64, inside, 0)

        first = tail[0]
        tail[0] += 2

        def near_step(k, _):
            serve_range(first + lax.div(k, 2), first + lax.div(k + 1, 2))
            near_sum(k)

            @pl.when(x == 1)
            def _():
                xf_copy(k).start()

            return 0

        lax.fori_loop(0, 4, near_step, 0)
        m.sm[0, 0:1, :] = jnp.zeros((1, D), F32)
        then = tail[0]
        tail[0] += 2

        def grad_in_step(k, _):
            serve_range(then + lax.div(k, 2), then + lax.div(k + 1, 2))

            @pl.when(x == 0)
            def _():
                xf_copy(k).wait_recv()

                def inside(i, gain):
                    r0 = k * chunk + i * 64
                    here_rows = rows(r0, 64, 64)
                    grad = m.act[rows(y * R + r0, 64, 64), :].astype(F32)
                    grad = grad + m.rsxf[here_rows, :].astype(F32)
                    full, r = full_of(m.n1[rows(t * R + r0, 64, 64), :].astype(F32))
                    back = crms_back(grad, full, r, m.gbuf[0, :1, :])
                    m.rsyf[here_rows, :] = back.astype(BF)
                    return gain + jnp.sum(grad * full * r, axis=0, keepdims=True)

                gain = lax.fori_loop(0, chunk // 64, inside, jnp.zeros((1, D), F32))
                m.sm[0, 0:1, :] += gain

            return 0

        lax.fori_loop(0, 4, grad_in_step, 0)

        @pl.when(x == 0)
        def _():
            gm_x.wait_recv()

            def out_step(i, _):
                at = rows(i * 64, 64, 64)
                one = m.gm[rows(t * H + i * 64, 64, 64), :].astype(F32) + m.rsyf[at, :].astype(F32)
                o_io[0, at, :] = one[:, :C].astype(BF)
                below = rows(H + i * 64, 64, 64)
                two = m.gother[at, :].astype(F32) + m.rsyf[below, :].astype(F32)
                o_io[0, below, :] = two[:, :C].astype(BF)
                return 0

            lax.fori_loop(0, H // 64, out_step, 0)

        @pl.when(x == 1)
        def _():
            bo_x.wait_recv()
            o_io[0, 0:H, :] = m.gother[:, :C]
            o_io[0, H:R, :] = m.n2[here, :C]

        for j, peer in enumerate((core, ydev, xdev)):
            copy = send(m.sm.at[j], m.smr.at[j], peer)
            serve_next(1)
            copy.wait_recv()
            m.sm[j + 1] = m.sm[j] + m.smr[j]
        z_copies = []
        for j in range(1, N):
            z_copies.append(send(m.sm.at[3], m.smz.at[j], (x, lax.rem(d + j, N), t)))
        settled = max(0, min(tail[0] - 5 * LAG - 1, GROUPS))
        settle(0, settled)
        serve_range(tail[0], GROUPS + 5 * LAG)
        everything = m.sm[3]
        for j in range(1, N):
            z_copies[j - 1].wait_recv()
            everything = everything + m.smz[j]
        o_sm[...] = jnp.zeros_like(o_sm)

        @pl.when(x == 0)
        def _():
            o_sm[0:1, :] = everything[0:1]

        @pl.when(x == 1)
        def _():
            o_sm[0:1, :] = everything[1:2]

        o_sm[1:2, :] = jnp.broadcast_to(
            jnp.sqrt(total(everything[2:3]) * (1.0 / (4 * R * N * D))), (1, D)
        )

        settle(settled, GROUPS)
        lax.fori_loop(0, GROUPS, lambda g, _: (leave(g).wait(), 0)[1], 0)
        waited = {id(copy) for copy in [n2_core, y_proj, *passed]}
        for k in range(2):
            n2f_copy(k).wait_send()
            gp3_copy(k).wait_send()
            gpy_copy(k).wait_send()
        for copy in pending:
            if id(copy) not in waited:
                copy.wait_send()
        for j in range(2):
            gn_copy(j).wait_send()
        for k in range(4):
            yf_copy(k).wait_send()

        @pl.when(x == 1)
        def _():
            gm_x.wait_send()
            for k in range(4):
                xf_copy(k).wait_send()

        @pl.when(x == 0)
        def _():
            bo_x.wait_send()

        assert counter[0] <= N_SEM

    return body, scratch_shapes, GRADS, (DOWN, UP, OUT, QKV)


def per_device(mesh):
    N = mesh.shape["dp"]
    assert mesh.shape["blk"] == 2 and mesh.shape["tensor"] == 4 and N % 2 == 0

    def run(stream_in, lengths, norm_gains, w_qkv, w_attn_out, w_up, w_down, cotangent):
        R, C = stream_in.shape
        D = norm_gains.shape[1]
        FF = w_up.shape[1]
        NH = w_qkv.shape[1] // (3 * HS)
        body, scratch, grad_rows, (DOWN, UP, OUT, QKV) = kernel_for(
            dict(R=R, H=R // 2, D=D, C=C, FF=FF, NH=NH, N=N)
        )
        vmem = pl.BlockSpec(memory_space=pltpu.VMEM)
        smem = pl.BlockSpec(memory_space=pltpu.SMEM)
        anywhere = pl.BlockSpec(memory_space=pl.ANY)
        block_io, grads, small = pl.pallas_call(
            body,
            out_shape=(
                jax.ShapeDtypeStruct((1, R, C), BF),
                jax.ShapeDtypeStruct((grad_rows, D), BF),
                jax.ShapeDtypeStruct((8, D), F32),
            ),
            in_specs=[smem, vmem] + [anywhere] * 6,
            out_specs=(vmem, anywhere, vmem),
            scratch_shapes=scratch,
            compiler_params=pltpu.CompilerParams(
                collective_id=0, has_side_effects=True, vmem_limit_bytes=63 << 20
            ),
        )(lengths, norm_gains, stream_in, cotangent, w_qkv.T, w_attn_out, w_up, w_down)

        QW, AW = grad_rows - QKV, QKV - OUT
        CUT = 192

        def spread(small_in, io_in, grads_in, gain, rms, io, qkv, out, up, down, *refs):
            held, io_held, wide, wide_up, wide_out, wide_down, isem, osem, csem = refs
            io_load = pltpu.make_async_copy(io_in, io_held, csem.at[0])
            io_copy = pltpu.make_async_copy(io_held, io, csem.at[1])

            def load(i):
                at = pl.ds(i * CUT, CUT)
                return pltpu.make_async_copy(grads_in.at[at], held.at[at], isem.at[i])

            for i in range(grad_rows // CUT):
                load(i).start()
            io_load.start()
            gain[...] = small_in[0:1, :]
            rms[0, 0] = jnp.max(small_in[1:2, :])
            stores = []
            for i in range(grad_rows // CUT):
                load(i).wait()
                at = i * CUT
                for first, ref, dst in (
                    (QKV, wide, qkv),
                    (OUT, wide_out, out),
                    (UP, wide_up, up),
                    (DOWN, wide_down, down),
                ):
                    if at >= first:
                        here = pl.ds(at - first, CUT)
                        ref[here, :] = held[at : at + CUT, : ref.shape[1]].astype(F32)
                        copy = pltpu.make_async_copy(ref.at[here], dst.at[here], osem.at[i])
                        break
                copy.start()
                stores.append(copy)
            io_load.wait()
            io_copy.start()
            for copy in stores:
                copy.wait()
            io_copy.wait()

        shapes = ((QW, D), (AW, C), (D, FF), (FF, C))
        cuts = grad_rows // CUT
        gain, rms, block_io, grad_qkv, grad_out, grad_up, grad_down = pl.pallas_call(
            spread,
            out_shape=(
                jax.ShapeDtypeStruct((1, D), F32),
                jax.ShapeDtypeStruct((1, 1), F32),
                jax.ShapeDtypeStruct((1, R, C), BF),
                *(jax.ShapeDtypeStruct(shape, F32) for shape in shapes),
            ),
            in_specs=[vmem, anywhere, anywhere],
            out_specs=(vmem, smem) + (anywhere,) * 5,
            scratch_shapes=[
                pltpu.VMEM((grad_rows, D), BF),
                pltpu.VMEM((1, R, C), BF),
                pltpu.VMEM((QW, D), F32),
                pltpu.VMEM((D, FF), F32),
                pltpu.VMEM((AW, C), F32),
                pltpu.VMEM((FF, C), F32),
                pltpu.SemaphoreType.DMA((cuts,)),
                pltpu.SemaphoreType.DMA((cuts,)),
                pltpu.SemaphoreType.DMA((2,)),
            ],
            compiler_params=pltpu.CompilerParams(vmem_limit_bytes=63 << 20),
        )(small, block_io, grads)
        return (block_io, gain, grad_qkv.T, grad_out, grad_up, grad_down, rms.reshape(()))

    return run


def solution(mesh):
    in_specs = (
        P(("dp", "tensor"), None),
        P("dp"),
        P("blk", None),
        P(None, "tensor"),
        P("tensor", None),
        P(None, "tensor"),
        P("tensor", None),
        P(("dp", "tensor"), None),
    )
    out_specs = (
        P("blk", ("dp", "tensor"), None),
        P("blk", None),
        P(None, "tensor"),
        P("tensor", None),
        P(None, "tensor"),
        P("tensor", None),
        P(),
    )
    return jax.shard_map(
        per_device(mesh), mesh=mesh, in_specs=in_specs, out_specs=out_specs, check_vma=False
    )
```
